32 devices in a mesh: dp: 8 (over z, y), mp: 4 (over x, core).
Axes of the slice: x: 2, y: 2, z: 4, core: 2. Of those that a mesh axis runs over, the one named last changes fastest.
Arguments:
- features: bfloat16 [32768, 512], P('dp', 'mp'), may hold values from -6 to 6
- lengths: int32 [8, 16], P('dp'), may hold values from 1 to 2048, 4096 in all within a row
- enc_conv3: bfloat16 [3, 512, 512], P(None, None, 'mp'), may hold values from -0.15625 to 0.15625
- enc_bias3: bfloat16 [512], P('mp'), may hold values from -3 to 3
- enc_conv1: bfloat16 [512, 512], P(None, 'mp'), may hold values from -0.5 to 0.5
- enc_bias1: bfloat16 [512], P('mp'), may hold values from -3 to 3
- codebooks: bfloat16 [2, 2, 1024, 256], replicated, may hold values from -3 to 3
- dec_conv3: bfloat16 [3, 512, 512], P(None, None, 'mp'), may hold values from -0.15625 to 0.15625
- dec_bias3: bfloat16 [512], P('mp'), may hold values from -3 to 3
- dec_conv1: bfloat16 [512, 512], P(None, 'mp'), may hold values from -0.5 to 0.5
- code_buffer: bfloat16 [1024, 512], replicated, may hold values from -6 to 6
- buffer_index: int32 [2, 2, 1024], replicated, may hold values from 0 to 1023
- out_cotangent: bfloat16 [32768, 512], P('dp', 'mp'), may hold values from -6 to 6
Outputs:
- grad_features: float32 [32768, 512], P('dp', 'mp')
- grad_enc_conv3: float32 [3, 512, 512], P(None, None, 'mp')
- grad_enc_bias3: float32 [512], P('mp')
- grad_enc_conv1: float32 [512, 512], P(None, 'mp')
- grad_enc_bias1: float32 [512], P('mp')
- grad_dec_conv3: float32 [3, 512, 512], P(None, None, 'mp')
- grad_dec_bias3: float32 [512], P('mp')
- grad_dec_conv1: float32 [512, 512], P(None, 'mp')
- grad_dec_bias1: float32 [512], P('mp')
- new_codebooks: float32 [2, 2, 1024, 256], replicated
The draws below stay inside these ranges and needn't reach their ends.
All inputs are finite; a program needn't handle non-finite values.
Results may differ from the reference program's by a relative error of at most 0.015.
The reference program's roundings to bfloat16 on the way count: a program that leaves them out, or rounds other values in their place, can miss the bound.
Values may be sent and summed in bfloat16 or wider, within the bound.
No kernel may reach another device: no remote copies, remote signals or barrier semaphores. Data moves between devices by JAX's collectives and lax.ppermute only.
A program may use at most 192 MiB of HBM per device.

```python
import math
import jax
import jax.numpy as jnp
import numpy as np
from jax import lax

D = 512
GROUPS = 2
LEVELS = 2
CODES = 1024
FRAMES_DEV = 4096
CLIPS_DEV = 16
BUF = 1024
GDIM = 256
MAXCLIP = 2048
FRAMES = 32768
N_DP = 8


def place_ends(array, rng, smallest, high):
    extent = array.shape
    index_at = [jax.random.randint(jax.random.fold_in(rng, axis), (), 0, extent[axis]) for axis in range(len(extent))]
    array = array.at[tuple(index_at)].set(smallest)
    longest = extent.index(max(extent))
    index_at[longest] = (index_at[longest] + 1) % extent[longest]
    return array.at[tuple(index_at)].set(high)


def steps_of(stream_key, dims, shards, least, high):
    def one(dim, blocks):
        heights = jax.random.uniform(jax.random.fold_in(jax.random.fold_in(stream_key, 6), dim), (blocks,), jnp.float32, least / len(shards), high / len(shards))
        return jnp.repeat(jnp.exp(heights), dims[dim] // blocks).reshape((-1,) + (1,) * (len(dims) - dim - 1))

    loudness = one(*shards[0])
    for cut in shards[1:]:
        loudness = loudness * one(*cut)
    return loudness


def profile(amount, total, most, skew):
    weights = [(1 << 20) // math.isqrt(rank ** skew) + 1 for rank in range(2, amount + 1)]
    spare, holding = total - most - (amount - 1), [1] * (amount - 1)
    while spare > 0:
        free = [i for i in range(amount - 1) if holding[i] < most]
        pool, remaining = sum([weights[i] for i in free]), spare
        for i in free:
            extra = min(most - holding[i], max(1, remaining * weights[i] // pool), spare)
            holding[i] = holding[i] + extra
            spare = spare - extra
    return np.array([most] + holding)


def ragged(rng, count, total, bound, lean):
    if count == 2:
        one = jax.random.randint(rng, (), max(1, total - bound), min(bound, total - 1) + 1)
        return jnp.stack([one, total - one])
    sizes = jnp.asarray(profile(count, total, bound, lean), jnp.int32)
    twos = (count - 1) // 2
    source_of, sink = sizes[1:1 + 2 * twos:2], sizes[2:2 + 2 * twos:2]
    room = jnp.minimum(source_of - 1, bound - sink)
    passed = jax.random.randint(jax.random.fold_in(rng, 1), (twos,), 0, 1 << 20) % (room + 1)
    sizes = sizes.at[1:1 + 2 * twos:2].set(source_of - passed).at[2:2 + 2 * twos:2].set(sink + passed)
    return sizes[jax.random.permutation(jax.random.fold_in(rng, 2), count)]


def normal_values(stream_key, dims, deviation, bound, cuts=(), held_as=jnp.bfloat16):
    drawn = jax.random.normal(stream_key, dims, jnp.float32) * deviation
    if len(cuts) > 0:
        drawn = steps_of(stream_key, dims, cuts, -0.22, 0.18) * drawn
    return jnp.clip(drawn, min=-bound, max=bound).astype(held_as)


def setup_inputs(seed: int = 0) -> dict:
    key_list = jax.random.split(jax.random.key(seed), 14)
    features = normal_values(key_list[0], (FRAMES, D), 1.0, 6.0, ((0, 8), (1, 4)))
    lengths = jax.vmap(lambda own: ragged(own, CLIPS_DEV, FRAMES_DEV, MAXCLIP, 2))(jax.random.split(key_list[1], N_DP)).reshape((N_DP, CLIPS_DEV)).astype(jnp.int32)
    enc_conv3 = normal_values(key_list[2], (3, D, D), (3 * D) ** -0.5, 0.15625, ((2, 4),))
    enc_bias3 = normal_values(key_list[3], (D,), 0.3, 3.0, ((0, 4),))
    enc_conv1 = normal_values(key_list[4], (D, D), (D // 4) ** -0.5, 0.5, ((1, 4),))
    enc_bias1 = normal_values(key_list[5], (D,), 0.3, 3.0, ((0, 4),))
    codebooks = normal_values(key_list[6], (GROUPS, LEVELS, CODES, GDIM), 0.5, 3.0)
    dec_conv3 = normal_values(key_list[7], (3, D, D), (3 * D) ** -0.5, 0.15625, ((2, 4),))
    dec_bias3 = normal_values(key_list[8], (D,), 0.3, 3.0, ((0, 4),))
    dec_conv1 = normal_values(key_list[9], (D, D), (D // 4) ** -0.5, 0.5, ((1, 4),))
    code_buffer = normal_values(key_list[10], (BUF, D), 1.0, 6.0)
    buffer_index = place_ends(jax.random.randint(key_list[11], (GROUPS, LEVELS, CODES), 0, BUF), jax.random.fold_in(key_list[11], 1), 0, BUF - 1).astype(jnp.int32)
    out_cotangent = normal_values(key_list[12], (FRAMES, D), 1.0, 6.0, ((0, 8), (1, 4)))
    return dict(features=features, lengths=lengths, enc_conv3=enc_conv3, enc_bias3=enc_bias3, enc_conv1=enc_conv1, enc_bias1=enc_bias1, codebooks=codebooks, dec_conv3=dec_conv3, dec_bias3=dec_bias3, dec_conv1=dec_conv1, code_buffer=code_buffer, buffer_index=buffer_index, out_cotangent=out_cotangent)


SOFTMAX_WARMTH = 8.0
THRESHOLD = 0.7
SHARPNESS = 4.0
STEP_SCALE = 0.5

@jax.custom_vjp
def low(v):
    return lax.optimization_barrier(v.astype(jnp.bfloat16)).astype(jnp.float32)

@jax.custom_vjp
def low_back(v):
    return v

def low_keep(v):
    return (low(v), None)

def low_pass(kept, grad):
    return (grad,)

def back_keep(v):
    return (v, None)

def back_low(kept, grad):
    return (low(grad),)
low.defvjp(low_keep, low_pass)
low_back.defvjp(back_keep, back_low)

def matrix_multiply(left_side, right_side):
    return jnp.dot(left_side, right_side, precision=lax.Precision.HIGHEST, preferred_element_type=jnp.float32)

def elu_fn(values):
    return jnp.where(values > 0, values, jnp.expm1(jnp.minimum(values, 0.0)))

def clip_masks(lengths):
    positions = jnp.arange(FRAMES_DEV, dtype=jnp.int32)
    clip_ends = jnp.cumsum(lengths, axis=1).astype(jnp.int32)
    starts = (clip_ends - lengths).astype(jnp.int32)
    is_start = jnp.any(positions[None, :, None] == starts[:, None, :], axis=2)
    prev_ok = jnp.where(is_start, 0.0, 1.0).astype(jnp.float32).reshape(-1)
    next_ok = jnp.concatenate([prev_ok[1:], jnp.zeros((1,), jnp.float32)])
    return (prev_ok, next_ok)

def conv_three(values, weight, bias_row, prev_ok, next_ok):
    zero_row = jnp.zeros((1, values.shape[1]), jnp.float32)
    before = jnp.concatenate([zero_row, values[:-1]], 0) * prev_ok[:, None]
    after_tap = jnp.concatenate([values[1:], zero_row], 0) * next_ok[:, None]
    return matrix_multiply(before, weight[0]) + matrix_multiply(values, weight[1]) + matrix_multiply(after_tap, weight[2]) + bias_row

def quantize_block(latent_rows, books):
    quant_parts = []
    usage_rows = []
    for group_idx in range(GROUPS):
        remain = latent_rows[:, group_idx * GDIM:(group_idx + 1) * GDIM]
        summed = jnp.zeros_like(remain)
        for level_idx in range(LEVELS):
            code_table_entries = books[group_idx, level_idx]
            current_residual = low(remain)
            distance_scores = low_back((2.0 * matrix_multiply(current_residual, code_table_entries.T) - lax.optimization_barrier(jnp.sum(code_table_entries * code_table_entries, axis=1))[None, :]) / SOFTMAX_WARMTH)
            probab = jax.nn.softmax(distance_scores, axis=1)
            picked = low_back(matrix_multiply(low(probab), code_table_entries))
            usage_rows.append(lax.optimization_barrier(jnp.sum(probab, axis=0)))
            remain = remain - picked
            summed = summed + picked
        quant_parts.append(summed)
    return (jnp.concatenate(quant_parts, axis=1), jnp.stack(usage_rows))

def forward(inputs, enc_w3, enc_b3, enc_w1, enc_b1, books, dec_w3, dec_b3, dec_w1, dec_b1, prev_ok, next_ok, cotangent):
    act_in = low(elu_fn(inputs))
    hidden_enc = low_back(conv_three(act_in, enc_w3, enc_b3, prev_ok, next_ok))
    act_mid = low(elu_fn(hidden_enc))
    latent = inputs + matrix_multiply(act_mid, enc_w1) + enc_b1
    latent = low(low_back(latent))
    block_rows = min(FRAMES, 4096)

    def one_block(latent_rows):
        return quantize_block(latent_rows, books)
    quant, usage = lax.map(jax.checkpoint(one_block), latent.reshape(FRAMES // block_rows, block_rows, D))
    quant = low(quant.reshape(FRAMES, D))
    act_dec = low(elu_fn(quant))
    hidden_dec = low_back(conv_three(act_dec, dec_w3, dec_b3, prev_ok, next_ok))
    act_dec_mid = low(elu_fn(hidden_dec))
    output = quant + matrix_multiply(act_dec_mid, dec_w1) + dec_b1
    return (jnp.sum(output * cotangent), lax.optimization_barrier(jnp.sum(usage, axis=0)))

def reference(features, lengths, enc_conv3, enc_bias3, enc_conv1, enc_bias1, codebooks, dec_conv3, dec_bias3, dec_conv1, code_buffer, buffer_index, out_cotangent):
    prev_ok, next_ok = clip_masks(lengths)
    cotangent = out_cotangent.astype(jnp.float32)
    out_bias = jnp.zeros((D,), jnp.float32)
    primals = tuple((item.astype(jnp.float32) for item in (features, enc_conv3, enc_bias3, enc_conv1, enc_bias1, codebooks, dec_conv3, dec_bias3, dec_conv1, out_bias)))

    def loss_fn(*params):
        return forward(*params, prev_ok, next_ok, cotangent)
    loss, pullback, usage = jax.vjp(loss_fn, *primals, has_aux=True)
    grads = pullback(jnp.ones_like(loss))
    ratio = usage.reshape(GROUPS, LEVELS, CODES) * (CODES / FRAMES)
    refresh = jax.nn.sigmoid(SHARPNESS * (THRESHOLD - ratio))[..., None]
    stepped = primals[5] - STEP_SCALE * (CODES / FRAMES) * grads[5]
    table = code_buffer.astype(jnp.float32)[buffer_index]
    chosen = jnp.stack([table[group_idx, :, :, group_idx * GDIM:(group_idx + 1) * GDIM] for group_idx in range(GROUPS)])
    new_codebooks = (1.0 - refresh) * stepped + refresh * chosen
    return (grads[0], grads[1], grads[2], grads[3], grads[4], grads[6], grads[7], grads[8], grads[9], new_codebooks)
```

```python
import jax
import jax.numpy as jnp
from jax import lax
from jax.sharding import PartitionSpec as P

SOFTMAX_WARMTH = 8.0
THRESHOLD = 0.7
SHARPNESS = 4.0
STEP_SCALE = 0.5
HALO = 16
BF16 = jnp.bfloat16
F32 = jnp.float32


def elu_fn(values):
    return jnp.where(values > 0, values, jnp.expm1(jnp.minimum(values, 0.0)))


def elu_slope(values):
    return jnp.where(values > 0, 1.0, jnp.exp(jnp.minimum(values, 0.0)))


def dot_nn(left, right):
    return jnp.dot(left, right, preferred_element_type=F32)


def dot_nt(left, right):
    return lax.dot_general(left, right, (((1,), (1,)), ((), ())), preferred_element_type=F32)


def dot_tn(left, right):
    return lax.dot_general(left, right, (((0,), (0,)), ((), ())), preferred_element_type=F32)


def swap(values, axis, bits):
    size = lax.axis_size(axis)
    return lax.ppermute(values, axis, [(i, i ^ bits) for i in range(size)])


def in_order(pieces, place, dim):
    stacked = jnp.stack(pieces)
    return jnp.concatenate(
        [
            lax.dynamic_index_in_dim(stacked, place ^ j, 0, keepdims=False)
            for j in range(len(pieces))
        ],
        dim,
    )


def to_frames(values, me, width, own):
    padded = jnp.pad(values, ((HALO, HALO), (0, 0)))
    pieces = []
    for k in range(width):
        piece = lax.dynamic_slice_in_dim(padded, (me ^ k) * own, own + 2 * HALO, 0)
        pieces.append(swap(piece, "mp", k) if k else piece)
    return in_order(pieces, me, 1)


def to_channels(values, me, width):
    cols = values.shape[1] // width
    pieces = []
    for k in range(width):
        piece = lax.dynamic_slice_in_dim(values, (me ^ k) * cols, cols, 1)
        pieces.append(swap(piece, "mp", k) if k else piece)
    return in_order(pieces, me, 0)


def gather_columns(block, me, width):
    held = [block]
    bit = width // 2
    offsets = [0]
    while bit:
        other = swap(jnp.stack(held), "mp", bit)
        held = held + [other[i] for i in range(len(held))]
        offsets = offsets + [o ^ bit for o in offsets]
        bit //= 2
    ordered = [None] * width
    for piece, offset in zip(held, offsets):
        ordered[offset] = piece
    return in_order(ordered, me, block.ndim - 1)


def exchange_steps(count):
    steps, stride, rest = [], 1, count
    while rest > 1:
        radix = 2 if (rest.bit_length() - 1) % 2 else 4
        steps.append((stride, radix))
        stride, rest = stride * radix, rest // radix
    return steps


def scatter_sum_dp(total, place):
    for stride, radix in exchange_steps(lax.axis_size("dp")):
        digit = (place // stride) % radix
        rows = total.shape[0] // radix
        summed = lax.dynamic_slice_in_dim(total, digit * rows, rows, 0)
        low = total.astype(BF16)
        for k in range(1, radix):
            piece = lax.dynamic_slice_in_dim(low, (digit ^ k) * rows, rows, 0)
            summed = summed + swap(piece, "dp", k * stride).astype(F32)
        total = summed
    return total


def gather_dp(block, place):
    for stride, radix in reversed(exchange_steps(lax.axis_size("dp"))):
        digit = (place // stride) % radix
        pieces = [block] + [swap(block, "dp", k * stride) for k in range(1, radix)]
        block = in_order(pieces, digit, 0)
    return block


def sum_columns(grads, me, width, place):
    cols = grads.shape[1] // width

    def block(offset):
        return lax.dynamic_slice_in_dim(grads, (me ^ offset) * cols, cols, 1)

    held = {k: block(k) for k in range(width)}
    bit = 1
    while bit < width:
        mine = [k for k in sorted(held) if not k & bit]
        other = swap(jnp.stack([held[k ^ bit] for k in mine]).astype(BF16), "mp", bit)
        held = {k: held[k] + other[i].astype(F32) for i, k in enumerate(mine)}
        bit *= 2
    return gather_dp(scatter_sum_dp(held[0], place).astype(BF16), place).astype(F32)


def sum_everywhere(values, width):
    bit = 1
    while bit < width:
        values = values + swap(values, "mp", bit)
        bit *= 2
    bit = 1
    while bit < lax.axis_size("dp"):
        values = values + swap(values, "dp", bit)
        bit *= 2
    return values


def shift_down(values):
    return jnp.concatenate([jnp.zeros_like(values[:1]), values[:-1]], 0)


def shift_up(values):
    return jnp.concatenate([values[1:], jnp.zeros_like(values[:1])], 0)


def taps(values, prev_ok, next_ok):
    zero = jnp.zeros((), values.dtype)
    return (
        jnp.where(prev_ok > 0, shift_down(values), zero),
        values,
        jnp.where(next_ok > 0, shift_up(values), zero),
    )


def conv_forward(values, weight, bias_row, prev_ok, next_ok):
    before, middle, after = taps(values, prev_ok, next_ok)
    return (
        dot_nn(before, weight[0])
        + dot_nn(middle, weight[1])
        + dot_nn(after, weight[2])
        + bias_row.astype(F32)
    )


def conv_input_grad(grad_out, weight, prev_ok, next_ok):
    return (
        dot_nt(grad_out, weight[1])
        + shift_up(dot_nt(grad_out, weight[0]) * prev_ok)
        + shift_down(dot_nt(grad_out, weight[2]) * next_ok)
    )


def body(
    features,
    lengths,
    enc_conv3,
    enc_bias3,
    enc_conv1,
    enc_bias1,
    codebooks,
    dec_conv3,
    dec_bias3,
    dec_conv1,
    code_buffer,
    buffer_index,
    out_cotangent,
):
    frames = features.shape[0]
    groups, levels, num_codes, group_dim = codebooks.shape
    width = lax.axis_size("mp")
    n_dp = lax.axis_size("dp")
    me = lax.axis_index("mp")
    place = lax.axis_index("dp")
    own = frames // width
    own_rows = slice(HALO, HALO + own)

    clip_ends = jnp.cumsum(lengths[0])
    starts = clip_ends - lengths[0]
    positions = me * own - HALO + jnp.arange(own + 2 * HALO + 1, dtype=jnp.int32)
    is_start = jnp.any(positions[:, None] == starts[None, :], axis=1) | (positions == frames)
    ok = jnp.where(is_start, 0.0, 1.0).astype(F32)[:, None]
    prev_ok, next_ok = ok[:-1], ok[1:]

    feat = to_frames(features, me, width, own)
    w_enc3 = gather_columns(enc_conv3, me, width)
    w_enc1 = gather_columns(enc_conv1, me, width)
    biases = gather_columns(jnp.stack([enc_bias3, enc_bias1, dec_bias3]), me, width)
    w_dec1 = gather_columns(dec_conv1, me, width)
    w_dec3 = gather_columns(dec_conv3, me, width)
    cot = to_frames(out_cotangent, me, width, own)

    feat_f = feat.astype(F32)
    act_in = elu_fn(feat_f).astype(BF16)
    hidden_enc = conv_forward(act_in, w_enc3, biases[0], prev_ok, next_ok)
    act_mid = elu_fn(hidden_enc).astype(BF16)
    latent = (feat_f + dot_nn(act_mid, w_enc1) + biases[1].astype(F32)).astype(BF16)

    saved, usage, quant_parts = [], [], []
    for g in range(groups):
        remain = latent[:, g * group_dim : (g + 1) * group_dim].astype(F32)
        summed = jnp.zeros_like(remain)
        for level in range(levels):
            book = codebooks[g, level]
            book_f = book.astype(F32)
            current = remain.astype(BF16)
            scores = (
                2.0 * dot_nt(current, book) - jnp.sum(book_f * book_f, axis=1)[None, :]
            ) / SOFTMAX_WARMTH
            terms = jnp.exp(scores - jnp.max(scores, axis=1, keepdims=True))
            probab = terms / jnp.sum(terms, axis=1, keepdims=True)
            probab_low = probab.astype(BF16)
            picked = dot_nn(probab_low, book)
            usage.append(jnp.sum(probab[own_rows], axis=0))
            saved.append((current, probab, probab_low))
            remain = remain - picked
            summed = summed + picked
        quant_parts.append(summed)
    quant = jnp.concatenate(quant_parts, axis=1).astype(BF16)
    usage_all = sum_everywhere(jnp.stack(usage), width)

    quant_f = quant.astype(F32)
    act_dec = elu_fn(quant_f).astype(BF16)
    hidden_dec = conv_forward(act_dec, w_dec3, biases[2], prev_ok, next_ok)
    act_dec_mid = elu_fn(hidden_dec).astype(BF16)
    cot_own = cot[own_rows]
    grad_dec_conv1 = sum_columns(dot_tn(act_dec_mid[own_rows], cot_own), me, width, place)
    grad_hidden_dec = (dot_nt(cot, w_dec1) * elu_slope(hidden_dec)).astype(BF16)
    grad_dec_conv3 = jnp.concatenate(
        [
            dot_tn(tap[own_rows], grad_hidden_dec[own_rows])
            for tap in taps(act_dec, prev_ok, next_ok)
        ],
        0,
    )
    grad_dec_conv3 = sum_columns(grad_dec_conv3, me, width, place)
    grad_quant = cot.astype(F32) + elu_slope(quant_f) * conv_input_grad(
        grad_hidden_dec, w_dec3, prev_ok, next_ok
    )

    grad_parts, book_grads = [], []
    for g in range(groups):
        grad_group = grad_quant[:, g * group_dim : (g + 1) * group_dim]
        grad_remain = jnp.zeros_like(grad_group)
        level_grads = []
        for level in reversed(range(levels)):
            current, probab, probab_low = saved[g * levels + level]
            book = codebooks[g, level]
            grad_picked = (grad_group - grad_remain).astype(BF16)
            grad_probab = dot_nt(grad_picked, book)
            grad_scores = (
                probab * (grad_probab - jnp.sum(probab * grad_probab, axis=1, keepdims=True))
            ).astype(BF16)
            grad_remain = grad_remain + dot_nn(grad_scores, book) * (2.0 / SOFTMAX_WARMTH)
            own_scores = grad_scores[own_rows]
            table = dot_tn(probab_low[own_rows], grad_picked[own_rows])
            table = table + (2.0 / SOFTMAX_WARMTH) * (
                dot_tn(own_scores, current[own_rows])
                - jnp.sum(own_scores.astype(F32), axis=0)[:, None] * book.astype(F32)
            )
            level_grads.append(table)
        grad_parts.append(grad_remain)
        book_grads.extend(level_grads[::-1])
    grad_latent = jnp.concatenate(grad_parts, axis=1).astype(BF16)

    total_rows = groups * levels * num_codes
    held = jnp.concatenate(book_grads, 0)
    first = jnp.int32(0)
    bit = 1
    while bit < width:
        rows = held.shape[0] // 2
        side = (me // bit) % 2
        sent = lax.dynamic_slice_in_dim(held, (1 - side) * rows, rows, 0).astype(BF16)
        held = lax.dynamic_slice_in_dim(held, side * rows, rows, 0) + swap(
            sent, "mp", bit
        ).astype(F32)
        first = first + side * rows
        bit *= 2
    rows = held.shape[0]
    held = scatter_sum_dp(held, place)
    for stride, radix in exchange_steps(n_dp):
        rows = rows // radix
        first = first + ((place // stride) % radix) * rows
    ratio = lax.dynamic_slice_in_dim(usage_all.reshape(total_rows), first, rows, 0) * (
        num_codes / (frames * n_dp)
    )
    refresh = jax.nn.sigmoid(SHARPNESS * (THRESHOLD - ratio))[:, None]
    own_books = lax.dynamic_slice_in_dim(
        codebooks.reshape(total_rows, group_dim), first, rows, 0
    ).astype(F32)
    stepped = own_books - STEP_SCALE * (num_codes / (frames * n_dp)) * held
    index = lax.dynamic_slice_in_dim(buffer_index.reshape(total_rows), first, rows, 0)
    row_group = (first + jnp.arange(rows, dtype=jnp.int32)) // (levels * num_codes)
    one_hot = (index[:, None] == jnp.arange(code_buffer.shape[0], dtype=jnp.int32)[None, :]).astype(
        BF16
    )
    both = dot_nn(one_hot, code_buffer)
    chosen = jnp.zeros((rows, group_dim), F32)
    for g in range(groups):
        chosen = jnp.where(
            (row_group == g)[:, None], both[:, g * group_dim : (g + 1) * group_dim], chosen
        )
    fresh = ((1.0 - refresh) * stepped + refresh * chosen).astype(BF16)
    fresh = gather_dp(fresh, place)
    bit = width // 2
    while bit:
        side = (me // bit) % 2
        fresh = in_order([fresh, swap(fresh, "mp", bit)], side, 0)
        bit //= 2
    new_codebooks = fresh.astype(F32).reshape(groups, levels, num_codes, group_dim)

    grad_enc_conv1 = sum_columns(
        dot_tn(act_mid[own_rows], grad_latent[own_rows]), me, width, place
    )
    grad_hidden_enc = (dot_nt(grad_latent, w_enc1) * elu_slope(hidden_enc)).astype(BF16)
    grad_enc_conv3 = jnp.concatenate(
        [
            dot_tn(tap[own_rows], grad_hidden_enc[own_rows])
            for tap in taps(act_in, prev_ok, next_ok)
        ],
        0,
    )
    grad_enc_conv3 = sum_columns(grad_enc_conv3, me, width, place)
    grad_features = (
        grad_latent.astype(F32)
        + elu_slope(feat_f) * conv_input_grad(grad_hidden_enc, w_enc3, prev_ok, next_ok)
    )[own_rows].astype(BF16)
    grad_features = to_channels(grad_features, me, width).astype(F32)

    bias_grads = jnp.stack(
        [
            jnp.sum(v[own_rows].astype(F32), axis=0)
            for v in (grad_hidden_enc, grad_latent, grad_hidden_dec, cot)
        ]
    )
    bias_grads = sum_everywhere(bias_grads, width)
    cols = features.shape[1]
    bias_grads = lax.dynamic_slice_in_dim(bias_grads, me * cols, cols, 1)

    return (
        grad_features,
        grad_enc_conv3.reshape(enc_conv3.shape),
        bias_grads[0],
        grad_enc_conv1,
        bias_grads[1],
        grad_dec_conv3.reshape(dec_conv3.shape),
        bias_grads[2],
        grad_dec_conv1,
        bias_grads[3],
        new_codebooks,
    )


def solution(mesh):
    return jax.shard_map(
        body,
        mesh=mesh,
        in_specs=(
            P("dp", "mp"),
            P("dp", None),
            P(None, None, "mp"),
            P("mp"),
            P(None, "mp"),
            P("mp"),
            P(),
            P(None, None, "mp"),
            P("mp"),
            P(None, "mp"),
            P(),
            P(),
            P("dp", "mp"),
        ),
        out_specs=(
            P("dp", "mp"),
            P(None, None, "mp"),
            P("mp"),
            P(None, "mp"),
            P("mp"),
            P(None, None, "mp"),
            P("mp"),
            P(None, "mp"),
            P("mp"),
            P(),
        ),
        check_vma=False,
    )
```

```python
import functools
import math

import jax
import jax.numpy as jnp
from jax import lax
from jax.experimental import pallas as pl
from jax.experimental.pallas import tpu as pltpu
from jax.sharding import PartitionSpec as P

SOFTMAX_WARMTH = 8.0
THRESHOLD = 0.7
SHARPNESS = 4.0
STEP_SCALE = 0.5
HALO = 16
LANES = 128
LOG2E = math.log2(math.e)
BF16 = jnp.bfloat16
F32 = jnp.float32
VMEM_LIMIT = 56 * 1024 * 1024


def dot_nn(left, right):
    return jnp.dot(left, right, preferred_element_type=F32)


def dot_nt(left, right):
    return lax.dot_general(left, right, (((1,), (1,)), ((), ())), preferred_element_type=F32)


def dot_tn(left, right):
    return lax.dot_general(left, right, (((0,), (0,)), ((), ())), preferred_element_type=F32)


def elu(values):
    return jnp.where(values > 0, values, jnp.exp(jnp.minimum(values, 0.0)) - 1.0)


def elu_slope(values):
    return jnp.exp(jnp.minimum(values, 0.0))


def swap(values, axis, bits):
    size = lax.axis_size(axis)
    return lax.ppermute(values, axis, [(i, i ^ bits) for i in range(size)])


def after(values, *others):
    return lax.optimization_barrier((values,) + others)[0]


def in_order(pieces, place, dim):
    stacked = jnp.stack(pieces)
    return jnp.concatenate(
        [
            lax.dynamic_index_in_dim(stacked, place ^ j, 0, keepdims=False)
            for j in range(len(pieces))
        ],
        dim,
    )


def frames_out(values, me, own):
    padded = jnp.pad(values, ((HALO, HALO), (0, 0)))

    def rows(k):
        return lax.dynamic_slice_in_dim(padded, (me ^ k) * own, own + 2 * HALO, 0)

    return rows(0), rows(1), jnp.stack([rows(2), rows(3)])


def exchange_steps(count):
    steps, stride, rest = [], 1, count
    while rest > 1:
        radix = 2 if (rest.bit_length() - 1) % 2 else 4
        steps.append((stride, radix))
        stride, rest = stride * radix, rest // radix
    return steps


def scatter_sum_dp(total, place, dim):
    for stride, radix in exchange_steps(lax.axis_size("dp")):
        digit = (place // stride) % radix
        size = total.shape[dim] // radix
        summed = lax.dynamic_slice_in_dim(total, digit * size, size, dim)
        for k in range(1, radix):
            piece = lax.dynamic_slice_in_dim(total, (digit ^ k) * size, size, dim).astype(BF16)
            summed = summed + swap(piece, "dp", k * stride).astype(F32)
        total = summed
    return total


def gather_dp(block, place):
    for stride, radix in reversed(exchange_steps(lax.axis_size("dp"))):
        digit = (place // stride) % radix
        pieces = [block] + [swap(block, "dp", k * stride) for k in range(1, radix)]
        block = in_order(pieces, digit, 0)
    return block


def sum_blocks(sent, kept, place):
    held = kept.astype(F32) + swap(sent, "mp", 1).astype(F32)
    held = held[0] + swap(held[1].astype(BF16), "mp", 2).astype(F32)
    return gather_dp(scatter_sum_dp(held, place, 0).astype(BF16), place)


def sum_everywhere(values, width):
    bit = 1
    while bit < width:
        values = values + swap(values, "mp", bit)
        bit *= 2
    bit = 1
    while bit < lax.axis_size("dp"):
        values = values + swap(values, "dp", bit)
        bit *= 2
    return values


def assemble(me, target, pieces):
    for k, piece in enumerate(pieces):
        columns = pl.ds(pl.multiple_of((me ^ k) * LANES, LANES), LANES)
        target[:, columns] = piece[...]


def taps_into(source, target, first_ok, last_ok, rows, depth):
    step = rows // 3
    for r in range(0, rows, step):
        here = slice(r, r + step)
        before = source[7 + r : 7 + r + step, :] * first_ok[here, :]
        later = source[9 + r : 9 + r + step, :] * last_ok[here, :]
        target[here, 0:depth] = before.astype(BF16)
        target[here, depth : 2 * depth] = source[8 + r : 8 + r + step, :].astype(BF16)
        target[here, 2 * depth : 3 * depth] = later.astype(BF16)


def encoder_kernel(
    me_ref, f0, f1, f2, f3, w0, w1, w2, w3, prev_ok, next_ok,
    hidden_ref, mid_ref, latent_ref, feat, weight, act, act3,
):
    me = me_ref[0]
    rows, depth = hidden_ref.shape
    assemble(me, feat, (f0, f1, f2, f3))
    assemble(me, weight, (w0, w1, w2, w3))
    step = rows // 3
    for r in range(0, rows, step):
        act[8 + r : 8 + r + step, :] = (
            elu(feat[r : r + step, :].astype(F32)).astype(BF16).astype(F32)
        )
    act[0:8, :] = jnp.zeros((8, depth), F32)
    act[8 + rows : 16 + rows, :] = jnp.zeros((8, depth), F32)
    taps_into(act, act3, prev_ok, next_ok, rows, depth)
    biases = weight[4 * depth : 4 * depth + 16, :].astype(F32)
    for r in range(0, rows, step):
        here = slice(r, r + step)
        hidden = dot_nn(act3[here, :], weight[0 : 3 * depth, :]) + biases[0:1, :]
        hidden_ref[here, :] = hidden
        mid = elu(hidden).astype(BF16)
        mid_ref[here, :] = mid
        latent = (
            feat[here, :].astype(F32)
            + dot_nn(mid, weight[3 * depth : 4 * depth, :])
            + biases[1:2, :]
        )
        latent_ref[here, :] = latent.astype(BF16)


def quantize_kernel(latent_ref, books, norms, quant_ref, usage_ref, prob_ref, second_ref, *, own):
    groups, levels, _, depth = books.shape
    rows = latent_ref.shape[0]
    place = pl.program_id(0) * rows + lax.broadcasted_iota(jnp.int32, (rows, 1), 0)
    mine = jnp.where((place >= HALO) & (place < HALO + own), 1.0, 0.0).astype(F32)

    @pl.when(pl.program_id(0) == 0)
    def _():
        usage_ref[...] = jnp.zeros_like(usage_ref)

    current = [latent_ref[:, g * depth : (g + 1) * depth] for g in range(groups)]
    remain = [c.astype(F32) for c in current]
    summed = [None] * groups
    for level in range(levels):
        for g in range(groups):
            book = books[g, level]
            scores = dot_nt(current[g], book) * (2.0 * LOG2E / SOFTMAX_WARMTH) - norms[g, level]
            terms = jnp.exp2(scores - jnp.max(scores, axis=1, keepdims=True))
            prob = terms * (1.0 / jnp.sum(terms, axis=1, keepdims=True))
            low = prob.astype(BF16)
            prob_ref[g, level] = low
            usage_ref[g, level] += jnp.sum(prob * mine, axis=0, keepdims=True)
            picked = dot_nn(low, book)
            summed[g] = picked if summed[g] is None else summed[g] + picked
            if level + 1 < levels:
                remain[g] = remain[g] - picked
                current[g] = remain[g].astype(BF16)
                second_ref[level, :, g * depth : (g + 1) * depth] = current[g]
    for g in range(groups):
        quant_ref[:, g * depth : (g + 1) * depth] = summed[g].astype(BF16)


def weight_grads(me, sent, kept, grad, deep, grad1, deep1, own, depth):
    here = slice(HALO, HALO + own)
    lane = lax.broadcasted_iota(jnp.int32, (own, LANES), 1)
    ones3 = jnp.where(lane == 0, 1.0, 0.0).astype(BF16)
    ones1 = jnp.where(lane == 1, 1.0, 0.0).astype(BF16)
    for k in range(4):
        columns = pl.ds(pl.multiple_of((me ^ k) * LANES, LANES), LANES)
        left = grad[here, columns]
        left1 = grad1[here, columns]
        target = (kept, sent)[k % 2].at[k // 2]
        target[:, 0 : 3 * depth] = dot_tn(left, deep[here, :]).astype(target.dtype)
        target[:, 3 * depth : 4 * depth] = dot_tn(left1, deep1[here, :]).astype(target.dtype)
        target[:, 4 * depth : 4 * depth + LANES] = (
            dot_tn(left, ones3) + dot_tn(left1, ones1)
        ).astype(target.dtype)


def input_grad(taps, weight, here, depth):
    return (
        dot_nt(taps[here, 2 * depth : 3 * depth], weight[0:depth, :])
        + dot_nt(taps[here, depth : 2 * depth], weight[depth : 2 * depth, :])
        + dot_nt(taps[here, 0:depth], weight[2 * depth : 3 * depth, :])
    )


def decoder_kernel(
    me_ref, quant, c0, c1, c2, c3, w0, w1, w2, w3, prev_ok, next_ok,
    grad_ref, sent, kept, cot, weight, act, act3, low, mid,
):
    me = me_ref[0]
    rows, depth = quant.shape
    own = rows - 2 * HALO
    assemble(me, cot, (c0, c1, c2, c3))
    assemble(me, weight, (w0, w1, w2, w3))
    step = rows // 3
    for r in range(0, rows, step):
        act[8 + r : 8 + r + step, :] = (
            elu(quant[r : r + step, :].astype(F32)).astype(BF16).astype(F32)
        )
    act[0:8, :] = jnp.zeros((8, depth), F32)
    act[8 + rows : 16 + rows, :] = jnp.zeros((8, depth), F32)
    taps_into(act, act3, prev_ok, next_ok, rows, depth)
    bias = weight[4 * depth : 4 * depth + 16, :].astype(F32)[0:1, :]
    for r in range(0, rows, step):
        here = slice(r, r + step)
        hidden = dot_nn(act3[here, :], weight[0 : 3 * depth, :]) + bias
        mid[here, :] = elu(hidden).astype(BF16)
        grad = dot_nt(cot[here, :], weight[3 * depth : 4 * depth, :]) * elu_slope(hidden)
        grad = grad.astype(BF16)
        low[here, :] = grad
        act[8 + r : 8 + r + step, :] = grad.astype(F32)
    weight_grads(me, sent, kept, low, act3, cot, mid, own, depth)
    taps_into(act, act3, prev_ok, next_ok, rows, depth)
    for r in range(0, rows, step):
        here = slice(r, r + step)
        grad_ref[here, :] = cot[here, :].astype(F32) + elu_slope(
            quant[here, :].astype(F32)
        ) * input_grad(act3, weight, here, depth)


def quantize_back_kernel(
    group_ref, grad_ref, prob_ref, first_ref, second_ref, books, turned,
    out_ref, table_ref, total, columns, *, own, levels,
):
    step = pl.program_id(0)
    rows = grad_ref.shape[0]
    place = step * rows + lax.broadcasted_iota(jnp.int32, (rows, 1), 0)
    mine = jnp.where((place >= HALO) & (place < HALO + own), 1.0, 0.0).astype(F32)
    mine_low = mine.astype(BF16)
    scale = 2.0 / SOFTMAX_WARMTH

    @pl.when(step == 0)
    def _():
        total[...] = jnp.zeros_like(total)
        columns[...] = jnp.zeros_like(columns)

    grad_remain = None
    for level in reversed(range(levels)):
        book = books[0, level]
        low = prob_ref[0, level]
        current = first_ref[...] if level == 0 else second_ref[level - 1]
        picked = grad_ref[...] if grad_remain is None else grad_ref[...] - grad_remain
        picked = picked.astype(BF16)
        grad_prob = dot_nt(picked, book)
        prob = low.astype(F32)
        inner = jnp.sum(prob * grad_prob, axis=1, keepdims=True)
        grad_scores = (prob * (grad_prob - inner)).astype(BF16)
        through = dot_nn(grad_scores, book) * scale
        grad_remain = through if grad_remain is None else grad_remain + through
        total[level] += dot_tn(picked * mine_low, low) + dot_tn(
            current * (mine_low * scale), grad_scores
        )
        columns[level] += jnp.sum(grad_scores.astype(F32) * mine, axis=0, keepdims=True)
    out_ref[...] = grad_remain.astype(BF16)

    @pl.when(step == pl.num_programs(0) - 1)
    def _():
        for level in range(levels):
            table_ref[level] = (
                total[level] - scale * columns[level] * turned[0, level].astype(F32)
            ).astype(BF16)


def encoder_grad_kernel(
    me_ref, grad_latent, hidden, mid, f0, f1, f2, f3, w0, w1, w2, w3, prev_ok, next_ok,
    sent, kept, out_sent, out_kept, feat, weight, act, act3, low,
):
    me = me_ref[0]
    rows, depth = grad_latent.shape
    own = rows - 2 * HALO
    assemble(me, feat, (f0, f1, f2, f3))
    assemble(me, weight, (w0, w1, w2, w3))
    step = rows // 3
    for r in range(0, rows, step):
        act[8 + r : 8 + r + step, :] = (
            elu(feat[r : r + step, :].astype(F32)).astype(BF16).astype(F32)
        )
    act[0:8, :] = jnp.zeros((8, depth), F32)
    act[8 + rows : 16 + rows, :] = jnp.zeros((8, depth), F32)
    taps_into(act, act3, prev_ok, next_ok, rows, depth)
    for r in range(0, rows, step):
        here = slice(r, r + step)
        grad = dot_nt(grad_latent[here, :], weight[3 * depth : 4 * depth, :])
        grad = (grad * elu_slope(hidden[here, :])).astype(BF16)
        low[here, :] = grad
        act[8 + r : 8 + r + step, :] = grad.astype(F32)
    weight_grads(me, sent, kept, low, act3, grad_latent, mid, own, depth)
    taps_into(act, act3, prev_ok, next_ok, rows, depth)
    for r in range(HALO, HALO + own, own // 4):
        here = slice(r, r + own // 4)
        feat[here, :] = (
            grad_latent[here, :].astype(F32)
            + elu_slope(feat[here, :].astype(F32)) * input_grad(act3, weight, here, depth)
        ).astype(BF16)
    for k in range(4):
        columns = pl.ds(pl.multiple_of((me ^ k) * LANES, LANES), LANES)
        (out_kept, out_sent)[k // 2][k % 2] = feat[HALO : HALO + own, columns]


def whole(count, smem_first=False):
    specs = [pl.BlockSpec(memory_space=pltpu.VMEM)] * count
    if smem_first:
        specs[0] = pl.BlockSpec(memory_space=pltpu.SMEM)
    return specs


def cost(flops, moved):
    return pl.CostEstimate(flops=int(flops), bytes_accessed=int(moved), transcendentals=0)


def shaped(shape, dtype):
    return jax.ShapeDtypeStruct(shape, dtype)


PARAMS = pltpu.CompilerParams(vmem_limit_bytes=VMEM_LIMIT)


def body(
    features,
    lengths,
    enc_conv3,
    enc_bias3,
    enc_conv1,
    enc_bias1,
    codebooks,
    dec_conv3,
    dec_bias3,
    dec_conv1,
    code_buffer,
    buffer_index,
    out_cotangent,
):
    frames, cols = features.shape
    groups, levels, num_codes, group_dim = codebooks.shape
    width = lax.axis_size("mp")
    n_dp = lax.axis_size("dp")
    me = lax.axis_index("mp")
    place = lax.axis_index("dp")
    own = frames // width
    rows = own + 2 * HALO
    depth = cols * width
    me_row = me.reshape(1)

    clip_ends = jnp.cumsum(lengths[0])
    starts = clip_ends - lengths[0]
    positions = me * own - HALO + jnp.arange(rows + 1, dtype=jnp.int32)
    is_start = jnp.any(positions[:, None] == starts[None, :], axis=1) | (positions == frames)
    ok = jnp.where(is_start, 0.0, 1.0).astype(F32)[:, None]
    prev_ok, next_ok = ok[:-1], ok[1:]

    def pack(conv3, conv1, biases):
        rows16 = jnp.pad(jnp.stack(biases), ((0, 16 - len(biases)), (0, 0)))
        return jnp.concatenate([conv3.reshape(3 * depth, cols), conv1, rows16], 0)

    f0, f1, f23 = frames_out(features, me, own)
    enc_own = pack(enc_conv3, enc_conv1, [enc_bias3, enc_bias1])
    got = swap(f23, "mp", 2)
    enc_other = swap(enc_own, "mp", 2)
    feat = (f0, got[0])
    other = swap(jnp.stack([f1, got[1]]), "mp", 1)
    feat = (f0, other[0], got[0], other[1])
    enc = swap(jnp.stack([enc_own, enc_other]), "mp", 1)
    enc = (enc_own, enc[0], enc_other, enc[1])

    c0, c1, c23 = frames_out(out_cotangent, me, own)
    dec_own = pack(dec_conv3, dec_conv1, [dec_bias3])
    dec_start, cot_start = after((dec_own, c23), enc_other, got)
    dec_other = swap(dec_start, "mp", 2)
    got = swap(cot_start, "mp", 2)
    other = swap(jnp.stack([c1, got[1]]), "mp", 1)
    cot = (c0, other[0], got[0], other[1])
    dec = swap(jnp.stack([dec_own, dec_other]), "mp", 1)
    dec = (dec_own, dec[0], dec_other, dec[1])

    books_f = codebooks.astype(F32)
    norms = jnp.sum(books_f * books_f, axis=3) * (LOG2E / SOFTMAX_WARMTH)
    norms = norms[:, :, None, :]
    turned = codebooks.transpose(0, 1, 3, 2)

    hidden_enc, act_mid, latent = pl.pallas_call(
        encoder_kernel,
        out_shape=(
            shaped((rows, depth), F32),
            shaped((rows, depth), BF16),
            shaped((rows, depth), BF16),
        ),
        in_specs=whole(11, True),
        out_specs=tuple(whole(3)),
        scratch_shapes=[
            pltpu.VMEM((rows, depth), BF16),
            pltpu.VMEM((4 * depth + 16, depth), BF16),
            pltpu.VMEM((rows + 16, depth), F32),
            pltpu.VMEM((rows, 3 * depth), BF16),
        ],
        compiler_params=PARAMS,
        cost_estimate=cost(8 * rows * depth * depth, 12e6),
    )(me_row, *feat, *enc, prev_ok, next_ok)

    step = rows // 3
    quant, usage, prob, second = pl.pallas_call(
        functools.partial(quantize_kernel, own=own),
        grid=(3,),
        out_shape=(
            shaped((rows, depth), BF16),
            shaped((groups, levels, 1, num_codes), F32),
            shaped((groups, levels, rows, num_codes), BF16),
            shaped((levels - 1, rows, depth), BF16),
        ),
        in_specs=[
            pl.BlockSpec((step, depth), lambda i: (i, 0)),
            pl.BlockSpec(codebooks.shape, lambda i: (0, 0, 0, 0)),
            pl.BlockSpec(norms.shape, lambda i: (0, 0, 0, 0)),
        ],
        out_specs=(
            pl.BlockSpec((step, depth), lambda i: (i, 0)),
            pl.BlockSpec((groups, levels, 1, num_codes), lambda i: (0, 0, 0, 0)),
            pl.BlockSpec((groups, levels, step, num_codes), lambda i: (0, 0, i, 0)),
            pl.BlockSpec((levels - 1, step, depth), lambda i: (0, i, 0)),
        ),
        compiler_params=PARAMS,
        cost_estimate=cost(16 * rows * num_codes * group_dim, 30e6),
    )(latent, codebooks, norms)
    usage_all = sum_everywhere(usage.reshape(groups * levels, num_codes), width)

    packed = 4 * depth + LANES
    grad_quant, dec_sent, dec_kept = pl.pallas_call(
        decoder_kernel,
        out_shape=(
            shaped((rows, depth), F32),
            shaped((2, cols, packed), BF16),
            shaped((2, cols, packed), F32),
        ),
        in_specs=whole(12, True),
        out_specs=tuple(whole(3)),
        scratch_shapes=[
            pltpu.VMEM((rows, depth), BF16),
            pltpu.VMEM((4 * depth + 16, depth), BF16),
            pltpu.VMEM((rows + 16, depth), F32),
            pltpu.VMEM((rows, 3 * depth), BF16),
            pltpu.VMEM((rows, depth), BF16),
            pltpu.VMEM((rows, depth), BF16),
        ],
        compiler_params=PARAMS,
        cost_estimate=cost(24 * rows * depth * depth, 20e6),
    )(me_row, quant, *cot, *dec, prev_ok, next_ok)

    def quantize_back(group):
        return pl.pallas_call(
            functools.partial(quantize_back_kernel, own=own, levels=levels),
            grid_spec=pltpu.PrefetchScalarGridSpec(
                num_scalar_prefetch=1,
                grid=(3,),
                in_specs=[
                    pl.BlockSpec((step, group_dim), lambda i, g: (i, g[0])),
                    pl.BlockSpec((1, levels, step, num_codes), lambda i, g: (g[0], 0, i, 0)),
                    pl.BlockSpec((step, group_dim), lambda i, g: (i, g[0])),
                    pl.BlockSpec((levels - 1, step, group_dim), lambda i, g: (0, i, g[0])),
                    pl.BlockSpec((1, levels, num_codes, group_dim), lambda i, g: (g[0], 0, 0, 0)),
                    pl.BlockSpec((1, levels, group_dim, num_codes), lambda i, g: (g[0], 0, 0, 0)),
                ],
                out_specs=(
                    pl.BlockSpec((step, group_dim), lambda i, g: (i, 0)),
                    pl.BlockSpec((levels, group_dim, num_codes), lambda i, g: (0, 0, 0)),
                ),
                scratch_shapes=[
                    pltpu.VMEM((levels, group_dim, num_codes), F32),
                    pltpu.VMEM((levels, 1, num_codes), F32),
                ],
            ),
            out_shape=(
                shaped((rows, group_dim), BF16),
                shaped((levels, group_dim, num_codes), BF16),
            ),
            compiler_params=PARAMS,
            cost_estimate=cost(16 * rows * num_codes * group_dim, 15e6),
        )(group.reshape(1), grad_quant, prob, latent, second, codebooks, turned)

    side, level_side = me % 2, me // 2
    grad_other, table_other = quantize_back(1 - side)
    grad_mine, table_mine = quantize_back(side)
    grad_latent = jnp.where(
        side == 0,
        jnp.concatenate([grad_mine, grad_other], 1),
        jnp.concatenate([grad_other, grad_mine], 1),
    )

    enc_sent, enc_kept, out_sent, out_kept = pl.pallas_call(
        encoder_grad_kernel,
        out_shape=(
            shaped((2, cols, packed), BF16),
            shaped((2, cols, packed), F32),
            shaped((2, own, cols), BF16),
            shaped((2, own, cols), BF16),
        ),
        in_specs=whole(14, True),
        out_specs=tuple(whole(4)),
        scratch_shapes=[
            pltpu.VMEM((rows, depth), BF16),
            pltpu.VMEM((4 * depth + 16, depth), BF16),
            pltpu.VMEM((rows + 16, depth), F32),
            pltpu.VMEM((rows, 3 * depth), BF16),
            pltpu.VMEM((rows, depth), BF16),
        ],
        compiler_params=PARAMS,
        cost_estimate=cost(16 * rows * depth * depth, 20e6),
    )(me_row, grad_latent, hidden_enc, act_mid, *feat, *enc, prev_ok, next_ok)

    tables = table_mine.astype(F32) + swap(table_other, "mp", 1).astype(F32)
    kept = lax.dynamic_index_in_dim(tables, level_side, 0, keepdims=False)
    sent = lax.dynamic_index_in_dim(tables, 1 - level_side, 0, keepdims=False)
    held = kept + swap(sent.astype(BF16), "mp", 2).astype(F32)
    held = scatter_sum_dp(held, place, 1)
    codes = held.shape[1]
    first = jnp.int32(0)
    size = num_codes
    for stride, radix in exchange_steps(n_dp):
        size = size // radix
        first = first + ((place // stride) % radix) * size

    def own_codes(array):
        start = (side, level_side, first) + (jnp.int32(0),) * (array.ndim - 3)
        return lax.dynamic_slice(array, start, (1, 1, codes) + array.shape[3:])[0, 0]

    index = own_codes(buffer_index)
    one_hot = index[:, None] == jnp.arange(code_buffer.shape[0], dtype=jnp.int32)[None, :]
    halves = lax.dynamic_slice_in_dim(code_buffer, side * group_dim, group_dim, 1)
    chosen = dot_nn(one_hot.astype(BF16), halves)
    share = num_codes / (frames * n_dp)
    ratio = own_codes(usage_all.reshape(groups, levels, num_codes)) * share
    refresh = jax.nn.sigmoid(SHARPNESS * (THRESHOLD - ratio))[:, None]
    stepped = own_codes(codebooks).astype(F32) - (STEP_SCALE * share) * held.T
    fresh = ((1.0 - refresh) * stepped + refresh * chosen).astype(BF16)
    fresh = gather_dp(fresh, place)
    fresh = in_order([fresh[None], swap(fresh[None], "mp", 2)], level_side, 0)
    fresh = in_order([fresh[None], swap(fresh[None], "mp", 1)], side, 0)
    new_codebooks = fresh.astype(F32)

    def unpack(total):
        total = total.T.astype(F32)
        return (
            total[: 3 * depth].reshape(3, depth, cols),
            total[4 * depth],
            total[3 * depth : 4 * depth],
            total[4 * depth + 1],
        )

    got = swap(out_sent, "mp", 2)
    kept = jnp.stack([out_kept[0], got[0]])
    other = swap(jnp.stack([out_kept[1], got[1]]), "mp", 1)
    grad_features = in_order([kept[0], other[0], kept[1], other[1]], me, 0).astype(F32)

    return (
        grad_features,
        *unpack(sum_blocks(enc_sent, enc_kept, place)),
        *unpack(sum_blocks(dec_sent, dec_kept, place)),
        new_codebooks,
    )


def solution(mesh):
    return jax.shard_map(
        body,
        mesh=mesh,
        in_specs=(
            P("dp", "mp"),
            P("dp", None),
            P(None, None, "mp"),
            P("mp"),
            P(None, "mp"),
            P("mp"),
            P(),
            P(None, None, "mp"),
            P("mp"),
            P(None, "mp"),
            P(),
            P(),
            P("dp", "mp"),
        ),
        out_specs=(
            P("dp", "mp"),
            P(None, None, "mp"),
            P("mp"),
            P(None, "mp"),
            P("mp"),
            P(None, None, "mp"),
            P("mp"),
            P(None, "mp"),
            P("mp"),
            P(),
        ),
        check_vma=False,
    )
```

```python
import functools
import math

import jax
import jax.numpy as jnp
from jax import lax
from jax.experimental import pallas as pl
from jax.experimental.pallas import tpu as pltpu
from jax.sharding import PartitionSpec as P

SOFTMAX_WARMTH = 8.0
THRESHOLD = 0.7
SHARPNESS = 4.0
STEP_SCALE = 0.5
HALO = 16
LANES = 128
LOG2E = math.log2(math.e)
BF16 = jnp.bfloat16
F32 = jnp.float32
VMEM_LIMIT = 56 * 1024 * 1024


def dot_nn(left, right):
    return jnp.dot(left, right, preferred_element_type=F32)


def dot_nt(left, right):
    return lax.dot_general(left, right, (((1,), (1,)), ((), ())), preferred_element_type=F32)


def dot_tn(left, right):
    return lax.dot_general(left, right, (((0,), (0,)), ((), ())), preferred_element_type=F32)


def elu(values):
    return jnp.where(values > 0, values, jnp.exp(jnp.minimum(values, 0.0)) - 1.0)


def elu_slope(values):
    return jnp.exp(jnp.minimum(values, 0.0))


def swap(values, axis, bits):
    size = lax.axis_size(axis)
    return lax.ppermute(values, axis, [(i, i ^ bits) for i in range(size)])


def after(values, *others):
    return lax.optimization_barrier((values,) + others)[0]


def frames_out(values, me, own):
    padded = jnp.pad(values, ((HALO, HALO), (0, 0)))
    return [
        lax.dynamic_slice_in_dim(padded, (me ^ k) * own, own + 2 * HALO, 0) for k in range(4)
    ]


def bits_of(count):
    return [1 << i for i in range(count.bit_length() - 1)]


def halves(total, place, bit, dim):
    size = total.shape[dim] // 2
    side = (place // bit) % 2
    mine = lax.dynamic_slice_in_dim(total, side * size, size, dim)
    other = lax.dynamic_slice_in_dim(total, (1 - side) * size, size, dim)
    return mine, other.astype(BF16)


def scatter_step(total, place, bit, dim):
    mine, other = halves(total, place, bit, dim)
    return mine + swap(other, "dp", bit).astype(F32)


def gather_step(block, axis, bit):
    return jnp.concatenate([block, swap(block, axis, bit)], 0)


def first_of(place, size, bits):
    first = jnp.int32(0)
    for bit in bits:
        size = size // 2
        first = first + ((place // bit) % 2) * size
    return first


def columns_of(me, k):
    return pl.ds(pl.multiple_of((me ^ k) * LANES, LANES), LANES)


def assemble(me, target, pieces):
    for k, piece in enumerate(pieces):
        target[:, columns_of(me, k)] = piece[...]


def assemble_halves(me, side, target, own, across, halves):
    target[:, columns_of(me, 0)] = own[...]
    target[:, columns_of(me, 1)] = across[...]
    for k in (2, 3):
        for j in range(2):
            piece = halves[2 * (k - 2) + j]
            rows = piece.shape[0]
            start = pl.multiple_of((side ^ j) * rows, 16)
            target[pl.ds(start, rows), columns_of(me, k)] = piece[...]


def taps_into(source, target, first_ok, last_ok, rows, depth):
    step = rows // 3
    for r in range(0, rows, step):
        here = slice(r, r + step)
        before = source[7 + r : 7 + r + step, :] * first_ok[here, :]
        later = source[9 + r : 9 + r + step, :] * last_ok[here, :]
        target[here, 0:depth] = before.astype(BF16)
        target[here, depth : 2 * depth] = source[8 + r : 8 + r + step, :].astype(BF16)
        target[here, 2 * depth : 3 * depth] = later.astype(BF16)


def encoder_kernel(
    me_ref, f0, f1, f2, f3, w0, w1, w2a, w2b, w3a, w3b, prev_ok, next_ok,
    hidden_ref, mid_ref, latent_ref, feat, weight, act, act3,
):
    me = me_ref[0]
    rows, depth = hidden_ref.shape
    assemble(me, feat, (f0, f1, f2, f3))
    assemble_halves(me, me_ref[1], weight, w0, w1, (w2a, w2b, w3a, w3b))
    step = rows // 3
    for r in range(0, rows, step):
        act[8 + r : 8 + r + step, :] = (
            elu(feat[r : r + step, :].astype(F32)).astype(BF16).astype(F32)
        )
    act[0:8, :] = jnp.zeros((8, depth), F32)
    act[8 + rows : 16 + rows, :] = jnp.zeros((8, depth), F32)
    taps_into(act, act3, prev_ok, next_ok, rows, depth)
    biases = weight[4 * depth : 4 * depth + 16, :].astype(F32)
    for r in range(0, rows, step):
        here = slice(r, r + step)
        hidden = dot_nn(act3[here, :], weight[0 : 3 * depth, :]) + biases[0:1, :]
        hidden_ref[here, :] = hidden
        mid = elu(hidden).astype(BF16)
        mid_ref[here, :] = mid
        latent = (
            feat[here, :].astype(F32)
            + dot_nn(mid, weight[3 * depth : 4 * depth, :])
            + biases[1:2, :]
        )
        latent_ref[here, :] = latent.astype(BF16)


def quantize_kernel(latent_ref, books, norms, quant_ref, usage_ref, prob_ref, second_ref, *, own):
    groups, levels, _, depth = books.shape
    rows = latent_ref.shape[0]
    place = pl.program_id(0) * rows + lax.broadcasted_iota(jnp.int32, (rows, 1), 0)
    mine = jnp.where((place >= HALO) & (place < HALO + own), 1.0, 0.0).astype(F32)

    @pl.when(pl.program_id(0) == 0)
    def _():
        usage_ref[...] = jnp.zeros_like(usage_ref)

    current = [latent_ref[:, g * depth : (g + 1) * depth] for g in range(groups)]
    remain = [c.astype(F32) for c in current]
    summed = [None] * groups
    for level in range(levels):
        for g in range(groups):
            book = books[g, level]
            scores = dot_nt(current[g], book) * (2.0 * LOG2E / SOFTMAX_WARMTH) - norms[g, level]
            terms = jnp.exp2(scores - jnp.max(scores, axis=1, keepdims=True))
            prob = terms * (1.0 / jnp.sum(terms, axis=1, keepdims=True))
            low = prob.astype(BF16)
            prob_ref[g, level] = low
            usage_ref[g, level] += jnp.sum(prob * mine, axis=0, keepdims=True)
            picked = dot_nn(low, book)
            summed[g] = picked if summed[g] is None else summed[g] + picked
            if level + 1 < levels:
                remain[g] = remain[g] - picked
                current[g] = remain[g].astype(BF16)
                second_ref[level, :, g * depth : (g + 1) * depth] = current[g]
    for g in range(groups):
        quant_ref[:, g * depth : (g + 1) * depth] = summed[g].astype(BF16)


def weight_grads(me, sent, kept, grad, deep, grad1, deep1, own, depth):
    here = slice(HALO, HALO + own)
    lane = lax.broadcasted_iota(jnp.int32, (own, LANES), 1)
    ones3 = jnp.where(lane == 0, 1.0, 0.0).astype(BF16)
    ones1 = jnp.where(lane == 1, 1.0, 0.0).astype(BF16)
    for k in range(4):
        columns = columns_of(me, k)
        left = grad[here, columns]
        left1 = grad1[here, columns]
        target = (kept, sent)[k % 2].at[k // 2]
        target[:, 0 : 3 * depth] = dot_tn(left, deep[here, :]).astype(target.dtype)
        target[:, 3 * depth : 4 * depth] = dot_tn(left1, deep1[here, :]).astype(target.dtype)
        target[:, 4 * depth : 4 * depth + LANES] = (
            dot_tn(left, ones3) + dot_tn(left1, ones1)
        ).astype(target.dtype)


def input_grad(taps, weight, here, depth):
    return (
        dot_nt(taps[here, 2 * depth : 3 * depth], weight[0:depth, :])
        + dot_nt(taps[here, depth : 2 * depth], weight[depth : 2 * depth, :])
        + dot_nt(taps[here, 0:depth], weight[2 * depth : 3 * depth, :])
    )


def decoder_kernel(
    me_ref, quant, c0, c1, c2, c3, w0, w1, w2, w3, prev_ok, next_ok,
    grad_ref, sent, kept, cot, weight, act, act3, low, mid,
):
    me = me_ref[0]
    rows, depth = quant.shape
    own = rows - 2 * HALO
    assemble(me, cot, (c0, c1, c2, c3))
    assemble(me, weight, (w0, w1, w2, w3))
    step = rows // 3
    for r in range(0, rows, step):
        act[8 + r : 8 + r + step, :] = (
            elu(quant[r : r + step, :].astype(F32)).astype(BF16).astype(F32)
        )
    act[0:8, :] = jnp.zeros((8, depth), F32)
    act[8 + rows : 16 + rows, :] = jnp.zeros((8, depth), F32)
    taps_into(act, act3, prev_ok, next_ok, rows, depth)
    bias = weight[4 * depth : 4 * depth + 16, :].astype(F32)[0:1, :]
    for r in range(0, rows, step):
        here = slice(r, r + step)
        hidden = dot_nn(act3[here, :], weight[0 : 3 * depth, :]) + bias
        mid[here, :] = elu(hidden).astype(BF16)
        grad = dot_nt(cot[here, :], weight[3 * depth : 4 * depth, :]) * elu_slope(hidden)
        grad = grad.astype(BF16)
        low[here, :] = grad
        act[8 + r : 8 + r + step, :] = grad.astype(F32)
    weight_grads(me, sent, kept, low, act3, cot, mid, own, depth)
    taps_into(act, act3, prev_ok, next_ok, rows, depth)
    for r in range(0, rows, step):
        here = slice(r, r + step)
        grad_ref[here, :] = cot[here, :].astype(F32) + elu_slope(
            quant[here, :].astype(F32)
        ) * input_grad(act3, weight, here, depth)


def quantize_back_kernel(
    group_ref, grad_ref, prob_ref, first_ref, second_ref, books, turned, usage,
    out_ref, table_ref, total, columns, *, own, levels,
):
    step = pl.program_id(0)
    rows = grad_ref.shape[0]
    place = step * rows + lax.broadcasted_iota(jnp.int32, (rows, 1), 0)
    mine = jnp.where((place >= HALO) & (place < HALO + own), 1.0, 0.0).astype(F32)
    mine_low = mine.astype(BF16)
    scale = 2.0 / SOFTMAX_WARMTH

    @pl.when(step == 0)
    def _():
        total[...] = jnp.zeros_like(total)
        columns[...] = jnp.zeros_like(columns)

    grad_remain = None
    for level in reversed(range(levels)):
        book = books[0, level]
        low = prob_ref[0, level]
        current = first_ref[...] if level == 0 else second_ref[level - 1]
        picked = grad_ref[...] if grad_remain is None else grad_ref[...] - grad_remain
        picked = picked.astype(BF16)
        grad_prob = dot_nt(picked, book)
        prob = low.astype(F32)
        inner = jnp.sum(prob * grad_prob, axis=1, keepdims=True)
        grad_scores = (prob * (grad_prob - inner)).astype(BF16)
        through = dot_nn(grad_scores, book) * scale
        grad_remain = through if grad_remain is None else grad_remain + through
        total[level] += dot_tn(picked * mine_low, low) + dot_tn(
            current * (mine_low * scale), grad_scores
        )
        columns[level] += jnp.sum(grad_scores.astype(F32) * mine, axis=0, keepdims=True)
    out_ref[...] = grad_remain.astype(BF16)

    @pl.when(step == pl.num_programs(0) - 1)
    def _():
        depth = turned.shape[2]
        for level in range(levels):
            table_ref[level, 0:depth, :] = (
                total[level] - scale * columns[level] * turned[0, level].astype(F32)
            ).astype(BF16)
            row = lax.broadcasted_iota(jnp.int32, (16, total.shape[2]), 0)
            table_ref[level, depth : depth + 16, :] = jnp.where(
                row == 0, usage[0, level], 0.0
            ).astype(BF16)


def encoder_grad_kernel(
    me_ref, grad_mine, grad_other, hidden, mid, f0, f1, f2, f3,
    w0, w1, w2a, w2b, w3a, w3b, prev_ok, next_ok,
    sent, kept, o0, o1, o2, o3, feat, weight, act, act3, low, grad_latent,
):
    me = me_ref[0]
    rows, depth = hidden.shape
    own = rows - 2 * HALO
    half = grad_mine.shape[1]
    side = me_ref[2]
    grad_latent[:, pl.ds(pl.multiple_of(side * half, half), half)] = grad_mine[...]
    grad_latent[:, pl.ds(pl.multiple_of((1 - side) * half, half), half)] = grad_other[...]
    assemble(me, feat, (f0, f1, f2, f3))
    assemble_halves(me, me_ref[1], weight, w0, w1, (w2a, w2b, w3a, w3b))
    step = rows // 3
    for r in range(0, rows, step):
        act[8 + r : 8 + r + step, :] = (
            elu(feat[r : r + step, :].astype(F32)).astype(BF16).astype(F32)
        )
    act[0:8, :] = jnp.zeros((8, depth), F32)
    act[8 + rows : 16 + rows, :] = jnp.zeros((8, depth), F32)
    taps_into(act, act3, prev_ok, next_ok, rows, depth)
    for r in range(0, rows, step):
        here = slice(r, r + step)
        grad = dot_nt(grad_latent[here, :], weight[3 * depth : 4 * depth, :])
        grad = (grad * elu_slope(hidden[here, :])).astype(BF16)
        low[here, :] = grad
        act[8 + r : 8 + r + step, :] = grad.astype(F32)
    weight_grads(me, sent, kept, low, act3, grad_latent, mid, own, depth)
    taps_into(act, act3, prev_ok, next_ok, rows, depth)
    for r in range(HALO, HALO + own, own // 4):
        here = slice(r, r + own // 4)
        feat[here, :] = (
            grad_latent[here, :].astype(F32)
            + elu_slope(feat[here, :].astype(F32)) * input_grad(act3, weight, here, depth)
        ).astype(BF16)
    for k, out in enumerate((o0, o1, o2, o3)):
        out[...] = feat[HALO : HALO + own, columns_of(me, k)]


def place_kernel(mask_ref, *refs, block):
    out, first = refs[-1], 0
    for ref in refs[:-1]:
        for r in range(0, ref.shape[0], block):
            start = pl.multiple_of((first + r) ^ mask_ref[0], block)
            out[pl.ds(start, block), :] = ref[r : r + block, :].astype(F32)
        first += ref.shape[0]


def whole(count, smem_first=False):
    specs = [pl.BlockSpec(memory_space=pltpu.VMEM)] * count
    if smem_first:
        specs[0] = pl.BlockSpec(memory_space=pltpu.SMEM)
    return specs


def cost(flops, moved):
    return pl.CostEstimate(flops=int(flops), bytes_accessed=int(moved), transcendentals=0)


def shaped(shape, dtype):
    return jax.ShapeDtypeStruct(shape, dtype)


PARAMS = pltpu.CompilerParams(vmem_limit_bytes=VMEM_LIMIT)


def body(
    features,
    lengths,
    enc_conv3,
    enc_bias3,
    enc_conv1,
    enc_bias1,
    codebooks,
    dec_conv3,
    dec_bias3,
    dec_conv1,
    code_buffer,
    buffer_index,
    out_cotangent,
):
    frames, cols = features.shape
    groups, levels, num_codes, group_dim = codebooks.shape
    width = lax.axis_size("mp")
    n_dp = lax.axis_size("dp")
    me = lax.axis_index("mp")
    place = lax.axis_index("dp")
    own = frames // width
    rows = own + 2 * HALO
    depth = cols * width
    side, level_side = me % 2, me // 2
    dp_bits = bits_of(n_dp)
    where_row = jnp.stack([me, place % 2, side])

    def pack(conv3, conv1, biases):
        rows32 = jnp.pad(jnp.stack(biases), ((0, 32 - len(biases)), (0, 0)))
        return jnp.concatenate([conv3.reshape(3 * depth, cols), conv1, rows32], 0)

    enc_own = pack(enc_conv3, enc_conv1, [enc_bias3, enc_bias1])
    half_rows = enc_own.shape[0] // 2
    enc_half = lax.dynamic_slice_in_dim(enc_own, (place % 2) * half_rows, half_rows, 0)
    enc_2a = swap(enc_half, "mp", 2)
    frames_of = frames_out(after(features, enc_half), me, own)
    feat = [frames_of[0]] + [swap(frames_of[k], "mp", k) for k in (1, 2, 3)]
    enc_1 = swap(enc_own, "mp", 1)
    enc_2b = swap(enc_2a, "dp", 1)
    enc_3a = swap(enc_2a, "mp", 1)
    enc_3b = swap(enc_2b, "mp", 1)
    enc = (enc_own, enc_1, enc_2a, enc_2b, enc_3a, enc_3b)

    dec_own = pack(dec_conv3, dec_conv1, [dec_bias3])
    dec_1 = swap(after(dec_own, enc_2a), "mp", 1)
    dec_2 = swap(after(dec_own, feat[2], feat[3]), "mp", 2)

    clip_ends = jnp.cumsum(lengths[0])
    starts = clip_ends - lengths[0]
    positions = me * own - HALO + jnp.arange(rows + 1, dtype=jnp.int32)
    is_start = jnp.any(positions[:, None] == starts[None, :], axis=1) | (positions == frames)
    ok = jnp.where(is_start, 0.0, 1.0).astype(F32)[:, None]
    prev_ok, next_ok = ok[:-1], ok[1:]

    books_f = codebooks.astype(F32)
    norms = jnp.sum(books_f * books_f, axis=3) * (LOG2E / SOFTMAX_WARMTH)
    norms = norms[:, :, None, :]
    turned = codebooks.transpose(0, 1, 3, 2)

    hidden_enc, act_mid, latent = pl.pallas_call(
        encoder_kernel,
        out_shape=(
            shaped((rows, depth), F32),
            shaped((rows, depth), BF16),
            shaped((rows, depth), BF16),
        ),
        in_specs=whole(13, True),
        out_specs=tuple(whole(3)),
        scratch_shapes=[
            pltpu.VMEM((rows, depth), BF16),
            pltpu.VMEM((4 * depth + 32, depth), BF16),
            pltpu.VMEM((rows + 16, depth), F32),
            pltpu.VMEM((rows, 3 * depth), BF16),
        ],
        compiler_params=PARAMS,
        cost_estimate=cost(8 * rows * depth * depth, 12e6),
    )(where_row, *feat, *enc, prev_ok, next_ok)

    dec_3 = swap(after(dec_2, latent), "mp", 1)
    dec = (dec_own, dec_1, dec_2, dec_3)
    frames_of = frames_out(after(out_cotangent, dec_2), me, own)
    cot = [frames_of[0]] + [swap(frames_of[k], "mp", k) for k in (1, 2, 3)]

    step = rows // 3
    quant, usage, prob, second = pl.pallas_call(
        functools.partial(quantize_kernel, own=own),
        grid=(3,),
        out_shape=(
            shaped((rows, depth), BF16),
            shaped((groups, levels, 1, num_codes), F32),
            shaped((groups, levels, rows, num_codes), BF16),
            shaped((levels - 1, rows, depth), BF16),
        ),
        in_specs=[
            pl.BlockSpec((step, depth), lambda i: (i, 0)),
            pl.BlockSpec(codebooks.shape, lambda i: (0, 0, 0, 0)),
            pl.BlockSpec(norms.shape, lambda i: (0, 0, 0, 0)),
        ],
        out_specs=(
            pl.BlockSpec((step, depth), lambda i: (i, 0)),
            pl.BlockSpec((groups, levels, 1, num_codes), lambda i: (0, 0, 0, 0)),
            pl.BlockSpec((groups, levels, step, num_codes), lambda i: (0, 0, i, 0)),
            pl.BlockSpec((levels - 1, step, depth), lambda i: (0, i, 0)),
        ),
        compiler_params=PARAMS,
        cost_estimate=cost(16 * rows * num_codes * group_dim, 30e6),
    )(latent, codebooks, norms)

    packed = 4 * depth + LANES
    grad_quant, dec_sent, dec_kept = pl.pallas_call(
        decoder_kernel,
        out_shape=(
            shaped((rows, depth), F32),
            shaped((2, cols, packed), BF16),
            shaped((2, cols, packed), F32),
        ),
        in_specs=whole(12, True),
        out_specs=tuple(whole(3)),
        scratch_shapes=[
            pltpu.VMEM((rows, depth), BF16),
            pltpu.VMEM((4 * depth + 32, depth), BF16),
            pltpu.VMEM((rows + 16, depth), F32),
            pltpu.VMEM((rows, 3 * depth), BF16),
            pltpu.VMEM((rows, depth), BF16),
            pltpu.VMEM((rows, depth), BF16),
        ],
        compiler_params=PARAMS,
        cost_estimate=cost(24 * rows * depth * depth, 20e6),
    )(where_row, quant, *cot, *dec, prev_ok, next_ok)

    def quantize_back(group, grads):
        return pl.pallas_call(
            functools.partial(quantize_back_kernel, own=own, levels=levels),
            grid_spec=pltpu.PrefetchScalarGridSpec(
                num_scalar_prefetch=1,
                grid=(3,),
                in_specs=[
                    pl.BlockSpec((step, group_dim), lambda i, g: (i, g[0])),
                    pl.BlockSpec((1, levels, step, num_codes), lambda i, g: (g[0], 0, i, 0)),
                    pl.BlockSpec((step, group_dim), lambda i, g: (i, g[0])),
                    pl.BlockSpec((levels - 1, step, group_dim), lambda i, g: (0, i, g[0])),
                    pl.BlockSpec((1, levels, num_codes, group_dim), lambda i, g: (g[0], 0, 0, 0)),
                    pl.BlockSpec((1, levels, group_dim, num_codes), lambda i, g: (g[0], 0, 0, 0)),
                    pl.BlockSpec((1, levels, 1, num_codes), lambda i, g: (g[0], 0, 0, 0)),
                ],
                out_specs=(
                    pl.BlockSpec((step, group_dim), lambda i, g: (i, 0)),
                    pl.BlockSpec((levels, group_dim + 16, num_codes), lambda i, g: (0, 0, 0)),
                ),
                scratch_shapes=[
                    pltpu.VMEM((levels, group_dim, num_codes), F32),
                    pltpu.VMEM((levels, 1, num_codes), F32),
                ],
            ),
            out_shape=(
                shaped((rows, group_dim), BF16),
                shaped((levels, group_dim + 16, num_codes), BF16),
            ),
            compiler_params=PARAMS,
            cost_estimate=cost(16 * rows * num_codes * group_dim, 15e6),
        )(group.reshape(1), grads, prob, latent, second, codebooks, turned, usage)

    grad_other, table_other = quantize_back(1 - side, grad_quant)
    dec_got = swap(dec_sent, "mp", 1)
    dec_held = dec_kept + after(dec_got, table_other).astype(F32)
    dec_x = swap(dec_held[1].astype(BF16), "mp", 2)
    table_got = swap(table_other, "mp", 1)
    grad_mine, table_mine = quantize_back(side, after(grad_quant, dec_held))
    dec_x, table_got, grad_mine, table_mine = lax.optimization_barrier(
        (dec_x, table_got, grad_mine, table_mine)
    )
    dec_held = dec_held[0] + dec_x.astype(F32)
    tables = table_mine.astype(F32) + table_got.astype(F32)
    book_held = lax.dynamic_index_in_dim(tables, level_side, 0, keepdims=False)
    sent = lax.dynamic_index_in_dim(tables, 1 - level_side, 0, keepdims=False)
    sent = sent.astype(BF16)
    dec_mine, dec_y = halves(dec_held, place, dp_bits[0], 0)
    grad_mine = after(grad_mine, sent, dec_y)
    book_x = swap(sent, "mp", 2)
    dec_y = swap(dec_y, "dp", dp_bits[0])

    enc_sent, enc_kept, *outs = pl.pallas_call(
        encoder_grad_kernel,
        out_shape=(
            shaped((2, cols, packed), BF16),
            shaped((2, cols, packed), F32),
        )
        + (shaped((own, cols), BF16),) * 4,
        in_specs=whole(17, True),
        out_specs=tuple(whole(6)),
        scratch_shapes=[
            pltpu.VMEM((rows, depth), BF16),
            pltpu.VMEM((4 * depth + 32, depth), BF16),
            pltpu.VMEM((rows + 16, depth), F32),
            pltpu.VMEM((rows, 3 * depth), BF16),
            pltpu.VMEM((rows, depth), BF16),
            pltpu.VMEM((rows, depth), BF16),
        ],
        compiler_params=PARAMS,
        cost_estimate=cost(16 * rows * depth * depth, 20e6),
    )(where_row, grad_mine, grad_other, hidden_enc, act_mid, *feat, *enc, prev_ok, next_ok)

    enc_sent, book_x, dec_y = lax.optimization_barrier((enc_sent, book_x, dec_y))
    enc_got = swap(enc_sent, "mp", 1)
    book_held = book_held + book_x.astype(F32)
    dec_held = dec_mine + dec_y.astype(F32)
    enc_held = enc_kept + enc_got.astype(F32)
    enc_held = enc_held[0] + swap(enc_held[1].astype(BF16), "mp", 2).astype(F32)
    for bit in dp_bits:
        book_held = scatter_step(book_held, place, bit, 1)
    for bit in dp_bits[1:]:
        dec_held = scatter_step(dec_held, place, bit, 0)
    for bit in dp_bits:
        enc_held = scatter_step(enc_held, place, bit, 0)

    codes = book_held.shape[1]
    first = first_of(place, num_codes, dp_bits)

    def own_codes(array):
        start = (side, level_side, first) + (jnp.int32(0),) * (array.ndim - 3)
        return lax.dynamic_slice(array, start, (1, 1, codes) + array.shape[3:])[0, 0]

    index = own_codes(buffer_index)
    one_hot = index[:, None] == jnp.arange(code_buffer.shape[0], dtype=jnp.int32)[None, :]
    buffer_half = lax.dynamic_slice_in_dim(code_buffer, side * group_dim, group_dim, 1)
    chosen = dot_nn(one_hot.astype(BF16), buffer_half)
    share = num_codes / (frames * n_dp)
    book_held = book_held.T
    ratio = book_held[:, group_dim : group_dim + 1] * share
    refresh = jax.nn.sigmoid(SHARPNESS * (THRESHOLD - ratio))
    stepped = own_codes(codebooks).astype(F32) - (STEP_SCALE * share) * book_held[:, :group_dim]
    fresh = ((1.0 - refresh) * stepped + refresh * chosen).astype(BF16)
    for bit in reversed(dp_bits):
        fresh = gather_step(fresh, "dp", bit)
    fresh = gather_step(fresh, "mp", 2)
    fresh_other = swap(fresh, "mp", 1)

    def put(mask, block, total, *pieces):
        return pl.pallas_call(
            functools.partial(place_kernel, block=block),
            out_shape=shaped((total, pieces[0].shape[1]), F32),
            in_specs=whole(1 + len(pieces), True),
            out_specs=whole(1)[0],
            compiler_params=PARAMS,
            cost_estimate=cost(0, 8 * total * pieces[0].shape[1]),
        )(mask.reshape(1), *pieces)

    mask = (side * levels + level_side) * num_codes + first
    new_codebooks = put(mask, codes, groups * levels * num_codes, fresh, fresh_other)

    turn = jnp.arange(cols, dtype=jnp.int32)
    turn = (turn[:, None] ^ first_of(place, cols, dp_bits)) == turn[None, :]
    turn = turn.astype(BF16)

    def unpack(held):
        held = held.astype(BF16)
        for bit in reversed(dp_bits):
            held = gather_step(held, "dp", bit)
        biases = dot_tn(held[:, 4 * depth :], turn)
        return (
            dot_tn(held[:, : 3 * depth], turn).reshape(3, depth, cols),
            biases[0],
            dot_tn(held[:, 3 * depth : 4 * depth], turn),
            biases[1],
        )

    outs = [outs[0]] + [swap(outs[k], "mp", k) for k in (1, 2, 3)]
    grad_features = put(me * own, own, frames, *outs)

    return (
        grad_features,
        *unpack(enc_held),
        *unpack(dec_held),
        new_codebooks.reshape(codebooks.shape),
    )


def solution(mesh):
    return jax.shard_map(
        body,
        mesh=mesh,
        in_specs=(
            P("dp", "mp"),
            P("dp", None),
            P(None, None, "mp"),
            P("mp"),
            P(None, "mp"),
            P("mp"),
            P(),
            P(None, None, "mp"),
            P("mp"),
            P(None, "mp"),
            P(),
            P(),
            P("dp", "mp"),
        ),
        out_specs=(
            P("dp", "mp"),
            P(None, None, "mp"),
            P("mp"),
            P(None, "mp"),
            P("mp"),
            P(None, None, "mp"),
            P("mp"),
            P(None, "mp"),
            P("mp"),
            P(),
        ),
        check_vma=False,
    )
```

```python
import functools
import math

import jax
import jax.numpy as jnp
from jax import lax
from jax.experimental import pallas as pl
from jax.experimental.pallas import tpu as pltpu
from jax.sharding import PartitionSpec as P

SOFTMAX_WARMTH = 8.0
THRESHOLD = 0.7
SHARPNESS = 4.0
STEP_SCALE = 0.5
HALO = 16
LANES = 128
LOG2E = math.log2(math.e)
BF16 = jnp.bfloat16
F32 = jnp.float32
VMEM_LIMIT = 56 * 1024 * 1024


def dot_nn(left, right):
    return jnp.dot(left, right, preferred_element_type=F32)


def dot_nt(left, right):
    return lax.dot_general(left, right, (((1,), (1,)), ((), ())), preferred_element_type=F32)


def dot_tn(left, right):
    return lax.dot_general(left, right, (((0,), (0,)), ((), ())), preferred_element_type=F32)


def elu(values):
    return jnp.where(values > 0, values, jnp.exp(jnp.minimum(values, 0.0)) - 1.0)


def elu_slope(values):
    return jnp.exp(jnp.minimum(values, 0.0))


def swap(values, axis, bits):
    size = lax.axis_size(axis)
    return lax.ppermute(values, axis, [(i, i ^ bits) for i in range(size)])


def after(values, *others):
    return lax.optimization_barrier((values,) + others)[0]


def parts_of(total, count):
    size = total.shape[0] // count
    return [total[k * size : k * size + size] for k in range(count)]


def swap_both(values, dp_bits, mp_bits):
    mp = lax.axis_size("mp")
    count = lax.axis_size("dp") * mp
    pairs = [(i, i ^ (dp_bits * mp + mp_bits)) for i in range(count)]
    return lax.ppermute(values, ("dp", "mp"), pairs)


def low_sum(*terms):
    return functools.reduce(lambda x, y: x + y, [t.astype(F32) for t in terms])


def columns_of(me, k):
    return pl.ds(pl.multiple_of((me ^ k) * LANES, LANES), LANES)


def assemble(me, target, pieces):
    for k, piece in enumerate(pieces):
        target[:, columns_of(me, k)] = piece[...]


def assemble_halves(me, side, target, own, across, halves):
    target[:, columns_of(me, 0)] = own[...]
    target[:, columns_of(me, 1)] = across[...]
    for k in (2, 3):
        for j in range(2):
            piece = halves[2 * (k - 2) + j]
            rows = piece.shape[0]
            start = pl.multiple_of((side ^ j) * rows, 16)
            target[pl.ds(start, rows), columns_of(me, k)] = piece[...]


def frames_kernel(where_ref, values, *outs):
    own = outs[0].shape[0] - 2 * HALO
    for k, out in enumerate(outs):
        start = pl.multiple_of((where_ref[0] ^ k) * own, own)
        above = pl.multiple_of(jnp.maximum(start - HALO, 0), HALO)
        below = pl.multiple_of(jnp.minimum(start + own, values.shape[0] - HALO), HALO)
        out[0:HALO, :] = values[pl.ds(above, HALO), :]
        out[HALO : HALO + own, :] = values[pl.ds(start, own), :]
        out[HALO + own : 2 * HALO + own, :] = values[pl.ds(below, HALO), :]


def pack_kernel(where_ref, conv3, conv1, *refs, count):
    biases, weight = refs[:count], refs[count]
    first, second = conv3.shape[0], conv3.shape[0] + conv1.shape[0]
    weight[0:first, :] = conv3[...]
    weight[first:second, :] = conv1[...]
    row = lax.broadcasted_iota(jnp.int32, (32, LANES), 0)
    rows = jnp.zeros((32, LANES), F32)
    for i, bias in enumerate(biases):
        rows = jnp.where(row == i, bias[...].astype(F32), rows)
    weight[second : second + 32, :] = rows.astype(BF16)
    for half in refs[count + 1 :]:
        size = half.shape[0]
        half[...] = weight[pl.ds(pl.multiple_of(where_ref[1] * size, 16), size), :]


def taps_into(source, target, first_ok, last_ok, rows, depth):
    step = rows // 3
    for r in range(0, rows, step):
        here = slice(r, r + step)
        before = source[7 + r : 7 + r + step, :] * first_ok[here, :]
        later = source[9 + r : 9 + r + step, :] * last_ok[here, :]
        target[here, 0:depth] = before.astype(BF16)
        target[here, depth : 2 * depth] = source[8 + r : 8 + r + step, :].astype(BF16)
        target[here, 2 * depth : 3 * depth] = later.astype(BF16)


def encoder_kernel(
    me_ref, f0, f1, f2, f3, w0, w1, w2a, w2b, w3a, w3b, prev_ok, next_ok,
    hidden_ref, mid_ref, latent_ref, feat, weight, act, act3,
):
    me = me_ref[0]
    rows, depth = hidden_ref.shape
    assemble(me, feat, (f0, f1, f2, f3))
    assemble_halves(me, me_ref[1], weight, w0, w1, (w2a, w2b, w3a, w3b))
    step = rows // 3
    for r in range(0, rows, step):
        act[8 + r : 8 + r + step, :] = (
            elu(feat[r : r + step, :].astype(F32)).astype(BF16).astype(F32)
        )
    act[0:8, :] = jnp.zeros((8, depth), F32)
    act[8 + rows : 16 + rows, :] = jnp.zeros((8, depth), F32)
    taps_into(act, act3, prev_ok, next_ok, rows, depth)
    biases = weight[4 * depth : 4 * depth + 16, :].astype(F32)
    for r in range(0, rows, step):
        here = slice(r, r + step)
        hidden = dot_nn(act3[here, :], weight[0 : 3 * depth, :]) + biases[0:1, :]
        hidden_ref[here, :] = hidden
        mid = elu(hidden).astype(BF16)
        mid_ref[here, :] = mid
        latent = (
            feat[here, :].astype(F32)
            + dot_nn(mid, weight[3 * depth : 4 * depth, :])
            + biases[1:2, :]
        )
        latent_ref[here, :] = latent.astype(BF16)


def quantize_kernel(latent_ref, books, norms, quant_ref, usage_ref, prob_ref, second_ref, *, own):
    groups, levels, _, depth = books.shape
    rows = latent_ref.shape[0]
    place = pl.program_id(0) * rows + lax.broadcasted_iota(jnp.int32, (rows, 1), 0)
    mine = jnp.where((place >= HALO) & (place < HALO + own), 1.0, 0.0).astype(F32)

    @pl.when(pl.program_id(0) == 0)
    def _():
        usage_ref[...] = jnp.zeros_like(usage_ref)

    current = [latent_ref[:, g * depth : (g + 1) * depth] for g in range(groups)]
    remain = [c.astype(F32) for c in current]
    summed = [None] * groups
    for level in range(levels):
        for g in range(groups):
            book = books[g, level]
            scores = dot_nt(current[g], book) * (2.0 * LOG2E / SOFTMAX_WARMTH) - norms[g, level]
            terms = jnp.exp2(scores - jnp.max(scores, axis=1, keepdims=True))
            prob = terms * (1.0 / jnp.sum(terms, axis=1, keepdims=True))
            low = prob.astype(BF16)
            prob_ref[g, level] = low
            usage_ref[g, level] += jnp.sum(prob * mine, axis=0, keepdims=True)
            picked = dot_nn(low, book)
            summed[g] = picked if summed[g] is None else summed[g] + picked
            if level + 1 < levels:
                remain[g] = remain[g] - picked
                current[g] = remain[g].astype(BF16)
                second_ref[level, :, g * depth : (g + 1) * depth] = current[g]
    for g in range(groups):
        quant_ref[:, g * depth : (g + 1) * depth] = summed[g].astype(BF16)


def weight_grads(where_ref, near, targets, grad, deep, grad1, deep1, own, depth):
    here = slice(HALO, HALO + own)
    lane = lax.broadcasted_iota(jnp.int32, (own, LANES), 1)
    ones3 = jnp.where(lane == 0, 1.0, 0.0).astype(BF16)
    ones1 = jnp.where(lane == 1, 1.0, 0.0).astype(BF16)
    size = LANES // near
    for k, target in enumerate(targets):
        left = grad[here, columns_of(where_ref[0], k)]
        left1 = grad1[here, columns_of(where_ref[0], k)]

        def put(first, count, values, target=target):
            for j in range(near):
                start = pl.multiple_of((where_ref[1] ^ j) * size, size)
                target[pl.ds(start, size), first : first + count] = values[
                    j * size : j * size + size, :
                ].astype(target.dtype)

        put(0, 3 * depth, dot_tn(left, deep[here, :]))
        put(3 * depth, depth, dot_tn(left1, deep1[here, :]))
        put(4 * depth, LANES, dot_tn(left, ones3) + dot_tn(left1, ones1))


def input_grad(taps, weight, here, depth):
    return (
        dot_nt(taps[here, 2 * depth : 3 * depth], weight[0:depth, :])
        + dot_nt(taps[here, depth : 2 * depth], weight[depth : 2 * depth, :])
        + dot_nt(taps[here, 0:depth], weight[2 * depth : 3 * depth, :])
    )


def decoder_kernel(
    me_ref, quant, c0, c1, c2, c3, w0, w1, w2, w3, prev_ok, next_ok,
    grad_ref, g0, g1, g2, g3, cot, weight, act, act3, low, mid, *, near,
):
    me = me_ref[0]
    rows, depth = quant.shape
    own = rows - 2 * HALO
    assemble(me, cot, (c0, c1, c2, c3))
    assemble(me, weight, (w0, w1, w2, w3))
    step = rows // 3
    for r in range(0, rows, step):
        act[8 + r : 8 + r + step, :] = (
            elu(quant[r : r + step, :].astype(F32)).astype(BF16).astype(F32)
        )
    act[0:8, :] = jnp.zeros((8, depth), F32)
    act[8 + rows : 16 + rows, :] = jnp.zeros((8, depth), F32)
    taps_into(act, act3, prev_ok, next_ok, rows, depth)
    bias = weight[4 * depth : 4 * depth + 16, :].astype(F32)[0:1, :]
    for r in range(0, rows, step):
        here = slice(r, r + step)
        hidden = dot_nn(act3[here, :], weight[0 : 3 * depth, :]) + bias
        mid[here, :] = elu(hidden).astype(BF16)
        grad = dot_nt(cot[here, :], weight[3 * depth : 4 * depth, :]) * elu_slope(hidden)
        grad = grad.astype(BF16)
        low[here, :] = grad
        act[8 + r : 8 + r + step, :] = grad.astype(F32)
    weight_grads(me_ref, near, (g0, g1, g2, g3), low, act3, cot, mid, own, depth)
    taps_into(act, act3, prev_ok, next_ok, rows, depth)
    for r in range(0, rows, step):
        here = slice(r, r + step)
        grad_ref[here, :] = cot[here, :].astype(F32) + elu_slope(
            quant[here, :].astype(F32)
        ) * input_grad(act3, weight, here, depth)


def quantize_back_kernel(
    group_ref, grad_ref, prob_ref, first_ref, second_ref, books, usage,
    out_ref, kept_ref, sent_ref, mark_ref, total, columns, *, own, levels,
):
    step = pl.program_id(0)
    rows = grad_ref.shape[0]
    place = step * rows + lax.broadcasted_iota(jnp.int32, (rows, 1), 0)
    mine = jnp.where((place >= HALO) & (place < HALO + own), 1.0, 0.0).astype(F32)
    mine_low = mine.astype(BF16)
    scale = 2.0 / SOFTMAX_WARMTH

    @pl.when(step == 0)
    def _():
        total[...] = jnp.zeros_like(total)
        columns[...] = jnp.zeros_like(columns)

    grad_remain = None
    for level in reversed(range(levels)):
        book = books[0, level]
        low = prob_ref[0, level]
        current = first_ref[...] if level == 0 else second_ref[level - 1]
        picked = grad_ref[...] if grad_remain is None else grad_ref[...] - grad_remain
        picked = picked.astype(BF16)
        grad_prob = dot_nt(picked, book)
        prob = low.astype(F32)
        inner = jnp.sum(prob * grad_prob, axis=1, keepdims=True)
        grad_scores = (prob * (grad_prob - inner)).astype(BF16)
        through = dot_nn(grad_scores, book) * scale
        grad_remain = through if grad_remain is None else grad_remain + through
        total[level] += dot_tn(picked * mine_low, low) + dot_tn(
            current * (mine_low * scale), grad_scores
        )
        columns[level] += jnp.sum(grad_scores.astype(F32) * mine, axis=0, keepdims=True)
    out_ref[...] = grad_remain.astype(BF16)

    @pl.when(step == pl.num_programs(0) - 1)
    def _():
        depth = books.shape[3]
        row = lax.broadcasted_iota(jnp.int32, (16, kept_ref.shape[2]), 0)
        for j, table in enumerate((kept_ref, sent_ref)):
            level = group_ref[1] ^ j
            codes = table.shape[2]
            turned = books[0, level].astype(F32).T
            for k in range(table.shape[0]):
                here = slice(k * codes, k * codes + codes)
                part = group_ref[2] ^ k
                table[part, 0:depth, :] = (
                    total[level, :, here] - scale * columns[level, :, here] * turned[:, here]
                ).astype(BF16)
                table[part, depth : depth + 16, :] = jnp.where(
                    row == 0, usage[0, level, :, here], 0.0
                ).astype(BF16)
        mark_ref[...] = jnp.zeros_like(mark_ref)


def encoder_weight_grad_kernel(
    me_ref, grad_mine, grad_other, hidden, mid, f0, f1, f2, f3,
    w0, w1, w2a, w2b, w3a, w3b, prev_ok, next_ok,
    g0, g1, g2, g3, low, grad_latent, mark, feat, weight, act, act3, *, near,
):
    mark[...] = jnp.zeros_like(mark)
    me = me_ref[0]
    rows, depth = hidden.shape
    own = rows - 2 * HALO
    half = grad_mine.shape[1]
    side = me_ref[2]
    grad_latent[:, pl.ds(pl.multiple_of(side * half, half), half)] = grad_mine[...]
    grad_latent[:, pl.ds(pl.multiple_of((1 - side) * half, half), half)] = grad_other[...]
    assemble(me, feat, (f0, f1, f2, f3))
    assemble_halves(me, me_ref[1], weight, w0, w1, (w2a, w2b, w3a, w3b))
    step = rows // 3
    for r in range(0, rows, step):
        act[8 + r : 8 + r + step, :] = (
            elu(feat[r : r + step, :].astype(F32)).astype(BF16).astype(F32)
        )
    act[0:8, :] = jnp.zeros((8, depth), F32)
    act[8 + rows : 16 + rows, :] = jnp.zeros((8, depth), F32)
    taps_into(act, act3, prev_ok, next_ok, rows, depth)
    for r in range(0, rows, step):
        here = slice(r, r + step)
        grad = dot_nt(grad_latent[here, :], weight[3 * depth : 4 * depth, :])
        low[here, :] = (grad * elu_slope(hidden[here, :])).astype(BF16)
    weight_grads(me_ref, near, (g0, g1, g2, g3), low, act3, grad_latent, mid, own, depth)


def encoder_input_grad_kernel(
    me_ref, low, grad_latent, f0, f1, f2, f3, w0, w1, w2a, w2b, w3a, w3b, prev_ok, next_ok,
    o0, o1, o2, o3, feat, weight, act, act3,
):
    me = me_ref[0]
    rows, depth = low.shape
    own = rows - 2 * HALO
    assemble(me, feat, (f0, f1, f2, f3))
    assemble_halves(me, me_ref[1], weight, w0, w1, (w2a, w2b, w3a, w3b))
    act[8 : 8 + rows, :] = low[...].astype(F32)
    act[0:8, :] = jnp.zeros((8, depth), F32)
    act[8 + rows : 16 + rows, :] = jnp.zeros((8, depth), F32)
    taps_into(act, act3, prev_ok, next_ok, rows, depth)
    for r in range(HALO, HALO + own, own // 4):
        here = slice(r, r + own // 4)
        feat[here, :] = (
            grad_latent[here, :].astype(F32)
            + elu_slope(feat[here, :].astype(F32)) * input_grad(act3, weight, here, depth)
        ).astype(BF16)
    for k, out in enumerate((o0, o1, o2, o3)):
        out[...] = feat[HALO : HALO + own, columns_of(me, k)]


def place_kernel(mask_ref, *refs, block):
    out, first = refs[-1], 0
    for ref in refs[:-1]:
        for r in range(0, ref.shape[0], block):
            start = pl.multiple_of((first + r) ^ mask_ref[0], block)
            out[pl.ds(start, block), :] = ref[r : r + block, :].astype(F32)
        first += ref.shape[0]


def whole(count, smem_first=False):
    specs = [pl.BlockSpec(memory_space=pltpu.VMEM)] * count
    if smem_first:
        specs[0] = pl.BlockSpec(memory_space=pltpu.SMEM)
    return specs


def cost(flops, moved):
    return pl.CostEstimate(flops=int(flops), bytes_accessed=int(moved), transcendentals=0)


def shaped(shape, dtype):
    return jax.ShapeDtypeStruct(shape, dtype)


PARAMS = pltpu.CompilerParams(vmem_limit_bytes=VMEM_LIMIT)


def body(
    features,
    lengths,
    enc_conv3,
    enc_bias3,
    enc_conv1,
    enc_bias1,
    codebooks,
    dec_conv3,
    dec_bias3,
    dec_conv1,
    code_buffer,
    buffer_index,
    out_cotangent,
):
    frames, cols = features.shape
    groups, levels, num_codes, group_dim = codebooks.shape
    width = lax.axis_size("mp")
    n_dp = lax.axis_size("dp")
    me = lax.axis_index("mp")
    place = lax.axis_index("dp")
    own = frames // width
    rows = own + 2 * HALO
    depth = cols * width
    side, level_side = me % 2, me // 2
    near = 2 if n_dp % 2 == 0 else n_dp
    near_at = place % near
    far_bits = [near << i for i in range((n_dp // near).bit_length() - 1)]
    where_row = jnp.stack([me, place % near, side])

    def pack(row, conv3, conv1, biases, half):
        total = conv3.shape[0] * conv3.shape[1] + conv1.shape[0] + 32
        shapes = [shaped((total, cols), BF16)] + [shaped((total // 2, cols), BF16)] * half
        return pl.pallas_call(
            functools.partial(pack_kernel, count=len(biases)),
            out_shape=shapes,
            in_specs=whole(3 + len(biases), True),
            out_specs=whole(len(shapes)),
            compiler_params=PARAMS,
            cost_estimate=cost(0, 1e6),
        )(
            row,
            conv3.reshape(3 * depth, cols),
            conv1,
            *[bias.reshape(1, cols) for bias in biases],
        )

    def frames_out(row, values):
        return pl.pallas_call(
            frames_kernel,
            out_shape=[shaped((rows, cols), BF16)] * 4,
            in_specs=whole(2, True),
            out_specs=whole(4),
            compiler_params=PARAMS,
            cost_estimate=cost(0, 2e6),
        )(row, values)

    enc_own, enc_half = pack(where_row, enc_conv3, enc_conv1, [enc_bias3, enc_bias1], 1)
    enc_2a = swap(enc_half, "mp", 2)
    feat = list(frames_out(after(where_row, enc_half), features))
    feat[2], feat[3] = swap(feat[2], "mp", 2), swap(feat[3], "mp", 3)
    feat[1] = swap(feat[1], "mp", 1)
    enc_1 = swap(enc_own, "mp", 1)
    enc_2b = swap(enc_2a, "dp", 1)
    enc_3a = swap(enc_2a, "mp", 1)
    enc_3b = swap(enc_2b, "mp", 1)
    enc = (enc_own, enc_1, enc_2a, enc_2b, enc_3a, enc_3b)

    clip_ends = jnp.cumsum(lengths[0])
    starts = clip_ends - lengths[0]

    def ok_at(shift):
        at = me * own - HALO + shift + jnp.arange(rows, dtype=jnp.int32)
        is_start = jnp.any(at[:, None] == starts[None, :], axis=1) | (at == frames)
        return jnp.where(is_start, 0.0, 1.0).astype(F32)[:, None]

    prev_ok, next_ok = ok_at(0), ok_at(1)
    books_f = codebooks.astype(F32)
    norms = jnp.sum(books_f * books_f, axis=3) * (LOG2E / SOFTMAX_WARMTH)
    norms = norms[:, :, None, :]

    codes = num_codes // near
    first = near_at * codes

    def own_codes(array):
        start = (side, level_side, first) + (jnp.int32(0),) * (array.ndim - 3)
        return lax.dynamic_slice(array, start, (1, 1, codes) + array.shape[3:])[0, 0]

    index = own_codes(buffer_index)
    one_hot = index[:, None] == jnp.arange(code_buffer.shape[0], dtype=jnp.int32)[None, :]
    buffer_half = lax.dynamic_slice_in_dim(code_buffer, side * group_dim, group_dim, 1)
    chosen = dot_nn(one_hot.astype(BF16), buffer_half)
    books_own = own_codes(codebooks).astype(F32)

    at = jnp.arange(cols, dtype=jnp.int32)
    turn = ((at[:, None] ^ (near_at * (cols // near))) == at[None, :]).astype(BF16)
    early_row = after(where_row, chosen, books_own, turn, norms, prev_ok, next_ok)

    (dec_own,) = pack(early_row, dec_conv3, dec_conv1, [dec_bias3], 0)
    cot = list(frames_out(early_row, out_cotangent))
    dec_1 = swap(dec_own, "mp", 1)
    dec_2 = swap(after(dec_own, feat[2], feat[3]), "mp", 2)

    hidden_enc, act_mid, latent = pl.pallas_call(
        encoder_kernel,
        out_shape=(
            shaped((rows, depth), F32),
            shaped((rows, depth), BF16),
            shaped((rows, depth), BF16),
        ),
        in_specs=whole(13, True),
        out_specs=tuple(whole(3)),
        scratch_shapes=[
            pltpu.VMEM((rows, depth), BF16),
            pltpu.VMEM((4 * depth + 32, depth), BF16),
            pltpu.VMEM((rows + 16, depth), F32),
            pltpu.VMEM((rows, 3 * depth), BF16),
        ],
        compiler_params=PARAMS,
        cost_estimate=cost(8 * rows * depth * depth, 12e6),
    )(after(where_row, cot[0], dec_own), *feat, *enc, prev_ok, next_ok)

    dec_3 = swap(after(dec_2, latent), "mp", 1)
    dec = (dec_own, dec_1, dec_2, dec_3)
    cot[2], cot[3], _ = lax.optimization_barrier((cot[2], cot[3], dec_2))
    cot = [cot[0]] + [swap(cot[k], "mp", k) for k in (1, 2, 3)]

    step = rows // 3
    quant, usage, prob, second = pl.pallas_call(
        functools.partial(quantize_kernel, own=own),
        grid=(3,),
        out_shape=(
            shaped((rows, depth), BF16),
            shaped((groups, levels, 1, num_codes), F32),
            shaped((groups, levels, rows, num_codes), BF16),
            shaped((levels - 1, rows, depth), BF16),
        ),
        in_specs=[
            pl.BlockSpec((step, depth), lambda i: (i, 0)),
            pl.BlockSpec(codebooks.shape, lambda i: (0, 0, 0, 0)),
            pl.BlockSpec(norms.shape, lambda i: (0, 0, 0, 0)),
        ],
        out_specs=(
            pl.BlockSpec((step, depth), lambda i: (i, 0)),
            pl.BlockSpec((groups, levels, 1, num_codes), lambda i: (0, 0, 0, 0)),
            pl.BlockSpec((groups, levels, step, num_codes), lambda i: (0, 0, i, 0)),
            pl.BlockSpec((levels - 1, step, depth), lambda i: (0, i, 0)),
        ),
        compiler_params=PARAMS,
        cost_estimate=cost(16 * rows * num_codes * group_dim, 30e6),
    )(latent, codebooks, norms)

    packed = 4 * depth + LANES
    grads_shape = tuple(
        shaped((cols, packed), dtype) for dtype in (F32, BF16, F32, BF16)
    )
    grad_quant, *dec_grads = pl.pallas_call(
        functools.partial(decoder_kernel, near=near),
        out_shape=(shaped((rows, depth), F32),) + grads_shape,
        in_specs=whole(12, True),
        out_specs=tuple(whole(5)),
        scratch_shapes=[
            pltpu.VMEM((rows, depth), BF16),
            pltpu.VMEM((4 * depth + 32, depth), BF16),
            pltpu.VMEM((rows + 16, depth), F32),
            pltpu.VMEM((rows, 3 * depth), BF16),
            pltpu.VMEM((rows, depth), BF16),
            pltpu.VMEM((rows, depth), BF16),
        ],
        compiler_params=PARAMS,
        cost_estimate=cost(24 * rows * depth * depth, 20e6),
    )(where_row, quant, *cot, *dec, prev_ok, next_ok)

    table_shape = (near, group_dim + 16, num_codes // near)

    def quantize_back(group):
        return pl.pallas_call(
            functools.partial(quantize_back_kernel, own=own, levels=levels),
            grid_spec=pltpu.PrefetchScalarGridSpec(
                num_scalar_prefetch=1,
                grid=(3,),
                in_specs=[
                    pl.BlockSpec((step, group_dim), lambda i, g: (i, g[0])),
                    pl.BlockSpec((1, levels, step, num_codes), lambda i, g: (g[0], 0, i, 0)),
                    pl.BlockSpec((step, group_dim), lambda i, g: (i, g[0])),
                    pl.BlockSpec((levels - 1, step, group_dim), lambda i, g: (0, i, g[0])),
                    pl.BlockSpec((1, levels, num_codes, group_dim), lambda i, g: (g[0], 0, 0, 0)),
                    pl.BlockSpec((1, levels, 1, num_codes), lambda i, g: (g[0], 0, 0, 0)),
                ],
                out_specs=(
                    pl.BlockSpec((step, group_dim), lambda i, g: (i, 0)),
                    pl.BlockSpec(table_shape, lambda i, g: (0, 0, 0)),
                    pl.BlockSpec(table_shape, lambda i, g: (0, 0, 0)),
                    pl.BlockSpec((8, LANES), lambda i, g: (0, 0)),
                ),
                scratch_shapes=[
                    pltpu.VMEM((levels, group_dim, num_codes), F32),
                    pltpu.VMEM((levels, 1, num_codes), F32),
                ],
            ),
            out_shape=(
                shaped((rows, group_dim), BF16),
                shaped(table_shape, BF16),
                shaped(table_shape, BF16),
                shaped((8, LANES), F32),
            ),
            compiler_params=PARAMS,
            cost_estimate=cost(16 * rows * num_codes * group_dim, 15e6),
        )(jnp.stack([group, level_side, near_at]), grad_quant, prob, latent, second, codebooks, usage)

    def gather_near(block):
        return jnp.concatenate([block] + [swap(block, "dp", k) for k in range(1, near)], 0)

    def stage(*groups):
        flat = lax.optimization_barrier(tuple(x for group in groups for x in group))
        out = []
        for group in groups:
            out.append(list(flat[: len(group)]))
            flat = flat[len(group) :]
        return out

    grad_other, kept_other, sent_other, mark = quantize_back(1 - side)
    dec_1g, dec_3g = swap(dec_grads[1], "mp", 1), swap(dec_grads[3], "mp", 1)
    dec_send = low_sum(dec_grads[2], dec_3g).astype(BF16)

    (mine, _), (dec_send,) = stage([side, mark], [dec_send])
    dec_x = swap(dec_send, "mp", 2)
    kept_got, sent_got = swap(kept_other, "mp", 1), swap(sent_other, "mp", 1)
    grad_mine, kept_mine, sent_mine, mark = quantize_back(mine)
    book_send = low_sum(sent_mine, sent_got).astype(BF16)
    dec_mine, *dec_send = parts_of(low_sum(dec_grads[0], dec_1g, dec_x), near)
    dec_send = [piece.astype(BF16) for piece in dec_send]

    (row, _), (book_send,), dec_send = stage([where_row, mark], [book_send], dec_send)
    book_x = swap(book_send, "mp", 2)
    dec_got = [swap(piece, "dp", k + 1) for k, piece in enumerate(dec_send)]
    *enc_grads, low, grad_latent, mark = pl.pallas_call(
        functools.partial(encoder_weight_grad_kernel, near=near),
        out_shape=grads_shape + (shaped((rows, depth), BF16),) * 2 + (shaped((8, LANES), F32),),
        in_specs=whole(17, True),
        out_specs=tuple(whole(7)),
        scratch_shapes=[
            pltpu.VMEM((rows, depth), BF16),
            pltpu.VMEM((4 * depth + 32, depth), BF16),
            pltpu.VMEM((rows + 16, depth), F32),
            pltpu.VMEM((rows, 3 * depth), BF16),
        ],
        compiler_params=PARAMS,
        cost_estimate=cost(12 * rows * depth * depth, 20e6),
    )(row, grad_mine, grad_other, hidden_enc, act_mid, *feat, *enc, prev_ok, next_ok)

    def book_sum(k):
        return low_sum(kept_mine[k], kept_got[k], book_x[k])

    def pair_sum(held, sent, bit):
        return held + swap(sent, "dp", bit).astype(F32)

    dec_held = low_sum(dec_mine, *dec_got)
    enc_1g, enc_3g = swap(enc_grads[1], "mp", 1), swap(enc_grads[3], "mp", 1)
    book_send, (dec_send, _) = stage(
        [book_sum(k).astype(BF16) for k in range(1, near)], [dec_held.astype(BF16), mark]
    )
    book_got = [swap(piece, "dp", k + 1) for k, piece in enumerate(book_send)]
    dec_held = pair_sum(dec_held, dec_send, far_bits[0])
    enc_mine, *enc_near = parts_of(low_sum(enc_grads[0], enc_1g), near)
    enc_near = [piece.astype(BF16) for piece in enc_near]
    enc_far = parts_of(low_sum(enc_grads[2], enc_3g).astype(BF16), near)
    book_held = low_sum(book_sum(0), *book_got)

    (row,), enc_near, enc_far, (book_send, dec_send) = stage(
        [where_row], enc_near, enc_far, [book_held.astype(BF16), dec_held.astype(BF16)]
    )
    enc_got = [swap(piece, "dp", k + 1) for k, piece in enumerate(enc_near)] + [
        swap_both(piece, k, 2) for k, piece in enumerate(enc_far)
    ]
    book_held = pair_sum(book_held, book_send, far_bits[0])
    dec_held = pair_sum(dec_held, dec_send, far_bits[1])
    for bit in far_bits[2:]:
        dec_held = pair_sum(dec_held, dec_held.astype(BF16), bit)
    outs = pl.pallas_call(
        encoder_input_grad_kernel,
        out_shape=(shaped((own, cols), BF16),) * 4,
        in_specs=whole(15, True),
        out_specs=tuple(whole(4)),
        scratch_shapes=[
            pltpu.VMEM((rows, depth), BF16),
            pltpu.VMEM((4 * depth + 32, depth), BF16),
            pltpu.VMEM((rows + 16, depth), F32),
            pltpu.VMEM((rows, 3 * depth), BF16),
        ],
        compiler_params=PARAMS,
        cost_estimate=cost(6 * rows * depth * depth, 10e6),
    )(row, low, grad_latent, *feat, *enc, prev_ok, next_ok)

    enc_held = low_sum(enc_mine, *enc_got)
    (book_send, dec_send, enc_send), outs_send = stage(
        [book_held.astype(BF16), dec_held.astype(BF16), enc_held.astype(BF16)], outs[1:]
    )
    book_held = pair_sum(book_held, book_send, far_bits[1])
    enc_held = pair_sum(enc_held, enc_send, far_bits[0])
    outs = [outs[0]] + [swap(piece, "mp", k + 1) for k, piece in enumerate(outs_send)]
    dec_held = gather_near(dec_send)
    for bit in far_bits[2:]:
        book_held = pair_sum(book_held, book_held.astype(BF16), bit)

    share = num_codes / (frames * n_dp)
    book_held = book_held.T
    ratio = book_held[:, group_dim : group_dim + 1] * share
    refresh = jax.nn.sigmoid(SHARPNESS * (THRESHOLD - ratio))
    stepped = books_own - (STEP_SCALE * share) * book_held[:, :group_dim]
    fresh = ((1.0 - refresh) * stepped + refresh * chosen).astype(BF16)

    (fresh, enc_send), _ = stage([fresh, enc_held.astype(BF16)], [])
    enc_held = pair_sum(enc_held, enc_send, far_bits[1])
    for bit in far_bits[2:]:
        enc_held = pair_sum(enc_held, enc_held.astype(BF16), bit)
    fresh = [
        swap_both(fresh, k, bits) if k or bits else fresh for bits in (0, 2) for k in range(near)
    ]
    enc_turn = enc_held.astype(BF16)
    enc_held = gather_near(enc_turn)
    fresh = fresh + [swap(part, "mp", 1) for part in fresh]

    def put(mask, block, total, *pieces):
        return pl.pallas_call(
            functools.partial(place_kernel, block=block),
            out_shape=shaped((total, pieces[0].shape[1]), F32),
            in_specs=whole(1 + len(pieces), True),
            out_specs=whole(1)[0],
            compiler_params=PARAMS,
            cost_estimate=cost(0, 8 * total * pieces[0].shape[1]),
        )(mask.reshape(1), *pieces)

    mask = (side * levels + level_side) * num_codes + first
    new_codebooks = put(mask, codes, groups * levels * num_codes, *fresh)

    def unpack(held):
        biases = dot_tn(held[:, 4 * depth :], turn)
        return (
            dot_tn(held[:, : 3 * depth], turn).reshape(3, depth, cols),
            biases[0],
            dot_tn(held[:, 3 * depth : 4 * depth], turn),
            biases[1],
        )

    grad_features = put(after(me * own, enc_turn), own, frames, *outs)

    return (
        grad_features,
        *unpack(enc_held),
        *unpack(dec_held),
        new_codebooks.reshape(codebooks.shape),
    )


def solution(mesh):
    return jax.shard_map(
        body,
        mesh=mesh,
        in_specs=(
            P("dp", "mp"),
            P("dp", None),
            P(None, None, "mp"),
            P("mp"),
            P(None, "mp"),
            P("mp"),
            P(),
            P(None, None, "mp"),
            P("mp"),
            P(None, "mp"),
            P(),
            P(),
            P("dp", "mp"),
        ),
        out_specs=(
            P("dp", "mp"),
            P(None, None, "mp"),
            P("mp"),
            P(None, "mp"),
            P("mp"),
            P(None, None, "mp"),
            P("mp"),
            P(None, "mp"),
            P("mp"),
            P(),
        ),
        check_vma=False,
    )
```

```python
import functools
import math

import jax
import jax.numpy as jnp
from jax import lax
from jax.experimental import pallas as pl
from jax.experimental.pallas import tpu as pltpu
from jax.sharding import PartitionSpec as P

SOFTMAX_WARMTH = 8.0
THRESHOLD = 0.7
SHARPNESS = 4.0
STEP_SCALE = 0.5
HALO = 16
LANES = 128
LOG2E = math.log2(math.e)
BF16 = jnp.bfloat16
F32 = jnp.float32
VMEM_LIMIT = 56 * 1024 * 1024


def dot_nn(left, right):
    return jnp.dot(left, right, preferred_element_type=F32)


def dot_nt(left, right):
    return lax.dot_general(left, right, (((1,), (1,)), ((), ())), preferred_element_type=F32)


def dot_tn(left, right):
    return lax.dot_general(left, right, (((0,), (0,)), ((), ())), preferred_element_type=F32)


def elu(values):
    return jnp.where(values > 0, values, jnp.exp(jnp.minimum(values, 0.0)) - 1.0)


def elu_slope(values):
    return jnp.exp(jnp.minimum(values, 0.0))


def swap(values, axis, bits):
    size = lax.axis_size(axis)
    return lax.ppermute(values, axis, [(i, i ^ bits) for i in range(size)])


def after(values, *others):
    return lax.optimization_barrier((values,) + others)[0]


def parts_of(total, count):
    size = total.shape[0] // count
    return [total[k * size : k * size + size] for k in range(count)]


def swap_both(values, dp_bits, mp_bits):
    mp = lax.axis_size("mp")
    count = lax.axis_size("dp") * mp
    pairs = [(i, i ^ (dp_bits * mp + mp_bits)) for i in range(count)]
    return lax.ppermute(values, ("dp", "mp"), pairs)


def low_sum(*terms):
    return functools.reduce(lambda x, y: x + y, [t.astype(F32) for t in terms])


def columns_of(me, k):
    return pl.ds(pl.multiple_of((me ^ k) * LANES, LANES), LANES)


def assemble(me, target, pieces):
    for k, piece in enumerate(pieces):
        target[:, columns_of(me, k)] = piece[...]


def assemble_halves(me, side, target, own, across, halves):
    target[:, columns_of(me, 0)] = own[...]
    target[:, columns_of(me, 1)] = across[...]
    for k in (2, 3):
        for j in range(2):
            piece = halves[2 * (k - 2) + j]
            rows = piece.shape[0]
            start = pl.multiple_of((side ^ j) * rows, 16)
            target[pl.ds(start, rows), columns_of(me, k)] = piece[...]


def frames_kernel(where_ref, values, *outs):
    own = outs[0].shape[0] - 2 * HALO
    for k, out in enumerate(outs):
        start = pl.multiple_of((where_ref[0] ^ k) * own, own)
        above = pl.multiple_of(jnp.maximum(start - HALO, 0), HALO)
        below = pl.multiple_of(jnp.minimum(start + own, values.shape[0] - HALO), HALO)
        out[0:HALO, :] = values[pl.ds(above, HALO), :]
        out[HALO : HALO + own, :] = values[pl.ds(start, own), :]
        out[HALO + own : 2 * HALO + own, :] = values[pl.ds(below, HALO), :]


def pack_kernel(where_ref, conv3, conv1, *refs, count):
    biases, weight = refs[:count], refs[count]
    first, second = conv3.shape[0], conv3.shape[0] + conv1.shape[0]
    weight[0:first, :] = conv3[...]
    weight[first:second, :] = conv1[...]
    row = lax.broadcasted_iota(jnp.int32, (32, LANES), 0)
    rows = jnp.zeros((32, LANES), F32)
    for i, bias in enumerate(biases):
        rows = jnp.where(row == i, bias[...].astype(F32), rows)
    weight[second : second + 32, :] = rows.astype(BF16)
    for half in refs[count + 1 :]:
        size = half.shape[0]
        half[...] = weight[pl.ds(pl.multiple_of(where_ref[1] * size, 16), size), :]


def taps_into(source, target, first_ok, last_ok, rows, depth):
    step = rows // 3
    for r in range(0, rows, step):
        here = slice(r, r + step)
        before = source[7 + r : 7 + r + step, :] * first_ok[here, :]
        later = source[9 + r : 9 + r + step, :] * last_ok[here, :]
        target[here, 0:depth] = before.astype(BF16)
        target[here, depth : 2 * depth] = source[8 + r : 8 + r + step, :].astype(BF16)
        target[here, 2 * depth : 3 * depth] = later.astype(BF16)


def encoder_kernel(
    me_ref, f0, f1, f2, f3, w0, w1, w2a, w2b, w3a, w3b, prev_ok, next_ok,
    hidden_ref, mid_ref, latent_ref, feat, weight, act, act3,
):
    me = me_ref[0]
    rows, depth = hidden_ref.shape
    assemble(me, feat, (f0, f1, f2, f3))
    assemble_halves(me, me_ref[1], weight, w0, w1, (w2a, w2b, w3a, w3b))
    step = rows // 3
    for r in range(0, rows, step):
        act[8 + r : 8 + r + step, :] = (
            elu(feat[r : r + step, :].astype(F32)).astype(BF16).astype(F32)
        )
    act[0:8, :] = jnp.zeros((8, depth), F32)
    act[8 + rows : 16 + rows, :] = jnp.zeros((8, depth), F32)
    taps_into(act, act3, prev_ok, next_ok, rows, depth)
    biases = weight[4 * depth : 4 * depth + 16, :].astype(F32)
    for r in range(0, rows, step):
        here = slice(r, r + step)
        hidden = dot_nn(act3[here, :], weight[0 : 3 * depth, :]) + biases[0:1, :]
        hidden_ref[here, :] = hidden
        mid = elu(hidden).astype(BF16)
        mid_ref[here, :] = mid
        latent = (
            feat[here, :].astype(F32)
            + dot_nn(mid, weight[3 * depth : 4 * depth, :])
            + biases[1:2, :]
        )
        latent_ref[here, :] = latent.astype(BF16)


def quantize_kernel(latent_ref, books, norms, quant_ref, usage_ref, prob_ref, second_ref, *, own):
    groups, levels, _, depth = books.shape
    rows = latent_ref.shape[0]
    place = pl.program_id(0) * rows + lax.broadcasted_iota(jnp.int32, (rows, 1), 0)
    mine = jnp.where((place >= HALO) & (place < HALO + own), 1.0, 0.0).astype(F32)

    @pl.when(pl.program_id(0) == 0)
    def _():
        usage_ref[...] = jnp.zeros_like(usage_ref)

    current = [latent_ref[:, g * depth : (g + 1) * depth] for g in range(groups)]
    remain = [c.astype(F32) for c in current]
    summed = [None] * groups
    for level in range(levels):
        for g in range(groups):
            book = books[g, level]
            scores = dot_nt(current[g], book) * (2.0 * LOG2E / SOFTMAX_WARMTH) - norms[g, level]
            terms = jnp.exp2(scores - jnp.max(scores, axis=1, keepdims=True))
            prob = terms * (1.0 / jnp.sum(terms, axis=1, keepdims=True))
            low = prob.astype(BF16)
            prob_ref[g, level] = low
            usage_ref[g, level] += jnp.sum(prob * mine, axis=0, keepdims=True)
            picked = dot_nn(low, book)
            summed[g] = picked if summed[g] is None else summed[g] + picked
            if level + 1 < levels:
                remain[g] = remain[g] - picked
                current[g] = remain[g].astype(BF16)
                second_ref[level, :, g * depth : (g + 1) * depth] = current[g]
    for g in range(groups):
        quant_ref[:, g * depth : (g + 1) * depth] = summed[g].astype(BF16)


def weight_grads(where_ref, near, targets, grad, deep, grad1, deep1, own, depth):
    here = slice(HALO, HALO + own)
    lane = lax.broadcasted_iota(jnp.int32, (own, LANES), 1)
    ones3 = jnp.where(lane == 0, 1.0, 0.0).astype(BF16)
    ones1 = jnp.where(lane == 1, 1.0, 0.0).astype(BF16)
    size = LANES // near

    def ordered(values):
        return jnp.concatenate(
            [values[here, columns_of(where_ref[0], k)] for k in range(len(targets))], 1
        )

    def put(first, values):
        count = values.shape[1]
        for k, target in enumerate(targets):
            for j in range(near):
                start = pl.multiple_of((where_ref[1] ^ j) * size, size)
                row = k * LANES + j * size
                target[pl.ds(start, size), first : first + count] = values[
                    row : row + size, :
                ].astype(target.dtype)

    left, left1 = ordered(grad), ordered(grad1)
    for first in range(0, 3 * depth, depth):
        put(first, dot_tn(left, deep[here, first : first + depth]))
    put(3 * depth, dot_tn(left1, deep1[here, :]))
    put(4 * depth, dot_tn(left, ones3) + dot_tn(left1, ones1))


def input_grad(taps, weight, here, depth):
    return (
        dot_nt(taps[here, 2 * depth : 3 * depth], weight[0:depth, :])
        + dot_nt(taps[here, depth : 2 * depth], weight[depth : 2 * depth, :])
        + dot_nt(taps[here, 0:depth], weight[2 * depth : 3 * depth, :])
    )


def decoder_kernel(
    me_ref, quant, c0, c1, c2, c3, w0, w1, w2, w3, prev_ok, next_ok,
    grad_ref, g0, g2, sent, cot, weight, act, act3, low, mid, *, near,
):
    me = me_ref[0]
    rows, depth = quant.shape
    own = rows - 2 * HALO
    assemble(me, cot, (c0, c1, c2, c3))
    assemble(me, weight, (w0, w1, w2, w3))
    step = rows // 3
    for r in range(0, rows, step):
        act[8 + r : 8 + r + step, :] = (
            elu(quant[r : r + step, :].astype(F32)).astype(BF16).astype(F32)
        )
    act[0:8, :] = jnp.zeros((8, depth), F32)
    act[8 + rows : 16 + rows, :] = jnp.zeros((8, depth), F32)
    taps_into(act, act3, prev_ok, next_ok, rows, depth)
    bias = weight[4 * depth : 4 * depth + 16, :].astype(F32)[0:1, :]
    for r in range(0, rows, step):
        here = slice(r, r + step)
        hidden = dot_nn(act3[here, :], weight[0 : 3 * depth, :]) + bias
        mid[here, :] = elu(hidden).astype(BF16)
        grad = dot_nt(cot[here, :], weight[3 * depth : 4 * depth, :]) * elu_slope(hidden)
        grad = grad.astype(BF16)
        low[here, :] = grad
        act[8 + r : 8 + r + step, :] = grad.astype(F32)
    targets = (g0, sent.at[0], g2, sent.at[1])
    weight_grads(me_ref, near, targets, low, act3, cot, mid, own, depth)
    taps_into(act, act3, prev_ok, next_ok, rows, depth)
    for r in range(0, rows, step):
        here = slice(r, r + step)
        grad_ref[here, :] = cot[here, :].astype(F32) + elu_slope(
            quant[here, :].astype(F32)
        ) * input_grad(act3, weight, here, depth)


def quantize_back_kernel(
    group_ref, grad_ref, prob_ref, first_ref, second_ref, books, usage,
    out_ref, table_ref, mark_ref, total, columns, *, own, levels,
):
    step = pl.program_id(0)
    rows = grad_ref.shape[0]
    place = step * rows + lax.broadcasted_iota(jnp.int32, (rows, 1), 0)
    mine = jnp.where((place >= HALO) & (place < HALO + own), 1.0, 0.0).astype(F32)
    mine_low = mine.astype(BF16)
    scale = 2.0 / SOFTMAX_WARMTH

    @pl.when(step == 0)
    def _():
        total[...] = jnp.zeros_like(total)
        columns[...] = jnp.zeros_like(columns)

    grad_remain = None
    for level in reversed(range(levels)):
        book = books[0, level]
        low = prob_ref[0, level]
        current = first_ref[...] if level == 0 else second_ref[level - 1]
        picked = grad_ref[...] if grad_remain is None else grad_ref[...] - grad_remain
        picked = picked.astype(BF16)
        grad_prob = dot_nt(picked, book)
        prob = low.astype(F32)
        inner = jnp.sum(prob * grad_prob, axis=1, keepdims=True)
        grad_scores = (prob * (grad_prob - inner)).astype(BF16)
        through = dot_nn(grad_scores, book) * scale
        grad_remain = through if grad_remain is None else grad_remain + through
        left = jnp.concatenate([picked * mine_low, current * (mine_low * scale)], 0)
        total[level] += dot_tn(left, jnp.concatenate([low, grad_scores], 0))
        columns[level] += jnp.sum(grad_scores.astype(F32) * mine, axis=0, keepdims=True)
    out_ref[...] = grad_remain.astype(BF16)

    @pl.when(step == pl.num_programs(0) - 1)
    def _():
        depth = books.shape[3]
        row = lax.broadcasted_iota(jnp.int32, (16, table_ref.shape[3]), 0)
        for j in range(levels):
            table = table_ref.at[j]
            level = group_ref[1] ^ j
            codes = table.shape[2]
            turned = books[0, level].astype(F32).T
            for k in range(table.shape[0]):
                here = slice(k * codes, k * codes + codes)
                part = group_ref[2] ^ k
                table[part, 0:depth, :] = (
                    total[level, :, here] - scale * columns[level, :, here] * turned[:, here]
                ).astype(BF16)
                table[part, depth : depth + 16, :] = jnp.where(
                    row == 0, usage[0, level, :, here], 0.0
                ).astype(BF16)
        mark_ref[...] = jnp.zeros_like(mark_ref)


def encoder_weight_grad_kernel(
    me_ref, grad_mine, grad_other, hidden, mid, f0, f1, f2, f3,
    w0, w1, w2a, w2b, w3a, w3b, prev_ok, next_ok,
    g0, g2, sent, low, grad_latent, mark, feat, weight, act, act3, *, near,
):
    mark[...] = jnp.zeros_like(mark)
    me = me_ref[0]
    rows, depth = hidden.shape
    own = rows - 2 * HALO
    half = grad_mine.shape[1]
    side = me_ref[2]
    grad_latent[:, pl.ds(pl.multiple_of(side * half, half), half)] = grad_mine[...]
    grad_latent[:, pl.ds(pl.multiple_of((1 - side) * half, half), half)] = grad_other[...]
    assemble(me, feat, (f0, f1, f2, f3))
    assemble_halves(me, me_ref[1], weight, w0, w1, (w2a, w2b, w3a, w3b))
    step = rows // 3
    for r in range(0, rows, step):
        act[8 + r : 8 + r + step, :] = (
            elu(feat[r : r + step, :].astype(F32)).astype(BF16).astype(F32)
        )
    act[0:8, :] = jnp.zeros((8, depth), F32)
    act[8 + rows : 16 + rows, :] = jnp.zeros((8, depth), F32)
    taps_into(act, act3, prev_ok, next_ok, rows, depth)
    for r in range(0, rows, step):
        here = slice(r, r + step)
        grad = dot_nt(grad_latent[here, :], weight[3 * depth : 4 * depth, :])
        low[here, :] = (grad * elu_slope(hidden[here, :])).astype(BF16)
    targets = (g0, sent.at[0], g2, sent.at[1])
    weight_grads(me_ref, near, targets, low, act3, grad_latent, mid, own, depth)


def encoder_input_grad_kernel(
    me_ref, low, grad_latent, f0, f1, f2, f3, w0, w1, w2a, w2b, w3a, w3b, prev_ok, next_ok,
    o0, o1, o2, o3, mark, feat, weight, act, act3,
):
    mark[...] = jnp.zeros_like(mark)
    me = me_ref[0]
    rows, depth = low.shape
    own = rows - 2 * HALO
    assemble(me, feat, (f0, f1, f2, f3))
    assemble_halves(me, me_ref[1], weight, w0, w1, (w2a, w2b, w3a, w3b))
    act[8 : 8 + rows, :] = low[...].astype(F32)
    act[0:8, :] = jnp.zeros((8, depth), F32)
    act[8 + rows : 16 + rows, :] = jnp.zeros((8, depth), F32)
    taps_into(act, act3, prev_ok, next_ok, rows, depth)
    for r in range(HALO, HALO + own, own // 4):
        here = slice(r, r + own // 4)
        feat[here, :] = (
            grad_latent[here, :].astype(F32)
            + elu_slope(feat[here, :].astype(F32)) * input_grad(act3, weight, here, depth)
        ).astype(BF16)
    for k, out in enumerate((o0, o1, o2, o3)):
        out[...] = feat[HALO : HALO + own, columns_of(me, k)]


def place_kernel(mask_ref, *refs, block):
    out, first = refs[-1], 0
    for ref in refs[:-1]:
        for r in range(0, ref.shape[0], block):
            start = pl.multiple_of((first + r) ^ mask_ref[0], block)
            out[pl.ds(start, block), :] = ref[r : r + block, :].astype(F32)
        first += ref.shape[0]


def sum_of(*refs):
    return functools.reduce(lambda x, y: x + y, [ref[...].astype(F32) for ref in refs])


def halve_kernel(where_ref, d0, d1, dx, t0, t1, mine, sent, book_sent, mark):
    half = mine.shape[0]
    total = sum_of(d0, d1.at[0], dx)
    mine[...] = total[:half]
    sent[...] = total[half:].astype(BF16)
    book_sent[...] = sum_of(t0.at[1], t1.at[1]).astype(BF16)
    mark[...] = jnp.zeros_like(mark)


def near_kernel(
    where_ref, t0, t1, bx, d0, d1, core, book_mine, book_sent, dec_mine, dec_sent, passed
):
    passed[...] = core[...]
    for k, out in enumerate((book_mine, book_sent)):
        out[...] = sum_of(t0.at[0, k], t1.at[0, k], bx.at[k]).astype(out.dtype)
    total = sum_of(d0, d1)
    dec_mine[...] = total
    dec_sent[...] = total.astype(BF16)


def spread_kernel(
    where_ref, b0, b1, e0, e2, core, d0, d1,
    book_mine, book_sent, enc_mine, enc_near, enc_x, enc_both, dec_mine, dec_sent, mark,
):
    half = enc_mine.shape[0]
    total = sum_of(e0, core.at[0])
    enc_mine[...] = total[:half]
    enc_near[...] = total[half:].astype(BF16)
    total = sum_of(e2, core.at[1])
    enc_x[...] = total[:half].astype(BF16)
    enc_both[...] = total[half:].astype(BF16)
    for mine, sent, total in (
        (book_mine, book_sent, sum_of(b0, b1)),
        (dec_mine, dec_sent, sum_of(d0, d1)),
    ):
        mine[...] = total
        sent[...] = total.astype(BF16)
    mark[...] = jnp.zeros_like(mark)


def sum_kernel(
    where_ref, b0, b1, e0, e1, e2, e3, d0, d1, book_mine, book_sent, enc_mine, enc_sent, dec_sent
):
    for mine, sent, total in (
        (book_mine, book_sent, sum_of(b0, b1)),
        (enc_mine, enc_sent, sum_of(e0, e1, e2, e3)),
    ):
        mine[...] = total
        sent[...] = total.astype(BF16)
    dec_sent[...] = sum_of(d0, d1).astype(BF16)


def refresh_kernel(where_ref, b0, b1, books, chosen, e0, e1, fresh, enc_mine, enc_sent, *, share):
    held = sum_of(b0, b1)
    depth = books.shape[0]
    ratio = held[depth : depth + 1, :] * share
    refresh = jax.nn.sigmoid(SHARPNESS * (THRESHOLD - ratio))
    stepped = books[...] - (STEP_SCALE * share) * held[:depth, :]
    fresh[...] = ((1.0 - refresh) * stepped + refresh * chosen[...]).T.astype(BF16)
    total = sum_of(e0, e1)
    enc_mine[...] = total
    enc_sent[...] = total.astype(BF16)


def join_kernel(where_ref, e0, e1, enc):
    enc[...] = sum_of(e0, e1).astype(BF16)


def unpack_kernel(mask_ref, *refs, block):
    *parts, conv3, conv1, bias3, bias1, held = refs
    first = 0
    for part in parts:
        for r in range(0, part.shape[0], block):
            start = pl.multiple_of((first + r) ^ mask_ref[0], block)
            held[pl.ds(start, block), :] = part[r : r + block, :].astype(F32)
        first += part.shape[0]
    count3, count1 = conv3.shape[0], conv1.shape[0]
    conv3[...] = held[:, 0:count3].T
    conv1[...] = held[:, count3 : count3 + count1].T
    biases = held[:, count3 + count1 :].T
    bias3[...] = biases[0:1, :]
    bias1[...] = biases[1:2, :]


def whole(count, smem_first=False):
    specs = [pl.BlockSpec(memory_space=pltpu.VMEM)] * count
    if smem_first:
        specs[0] = pl.BlockSpec(memory_space=pltpu.SMEM)
    return specs


def cost(flops, moved):
    return pl.CostEstimate(flops=int(flops), bytes_accessed=int(moved), transcendentals=0)


def shaped(shape, dtype):
    return jax.ShapeDtypeStruct(shape, dtype)


PARAMS = pltpu.CompilerParams(vmem_limit_bytes=VMEM_LIMIT)
LIGHT = pltpu.CompilerParams(vmem_limit_bytes=14 * 1024 * 1024)


def tied(kernel, first, count):
    def without(*refs):
        kernel(*refs[:first], *refs[first + count :])

    return without


def call(kernel, row, inputs, outs, scratch=(), ties=(), price=None, params=None):
    return pl.pallas_call(
        tied(kernel, 1 + len(inputs), len(ties)),
        out_shape=[shaped(*out) for out in outs],
        in_specs=whole(1 + len(inputs), True) + [pl.BlockSpec(memory_space=pl.ANY)] * len(ties),
        out_specs=whole(len(outs)),
        scratch_shapes=[pltpu.VMEM(*buffer) for buffer in scratch],
        compiler_params=params or LIGHT,
        cost_estimate=price or cost(0, 2e6),
    )(row, *inputs, *ties)


def body(
    features,
    lengths,
    enc_conv3,
    enc_bias3,
    enc_conv1,
    enc_bias1,
    codebooks,
    dec_conv3,
    dec_bias3,
    dec_conv1,
    code_buffer,
    buffer_index,
    out_cotangent,
):
    frames, cols = features.shape
    groups, levels, num_codes, group_dim = codebooks.shape
    width = lax.axis_size("mp")
    n_dp = lax.axis_size("dp")
    me = lax.axis_index("mp")
    place = lax.axis_index("dp")
    own = frames // width
    rows = own + 2 * HALO
    depth = cols * width
    side, level_side = me % 2, me // 2
    near = 2 if n_dp % 2 == 0 else n_dp
    near_at = place % near
    far_bits = [near << i for i in range((n_dp // near).bit_length() - 1)]
    where_row = jnp.stack([me, near_at, side, place // near])
    quad = near == 2 and n_dp == 8

    def pack(row, conv3, conv1, biases, half):
        total = conv3.shape[0] * conv3.shape[1] + conv1.shape[0] + 32
        shapes = [shaped((total, cols), BF16)] + [shaped((total // 2, cols), BF16)] * half
        return pl.pallas_call(
            functools.partial(pack_kernel, count=len(biases)),
            out_shape=shapes,
            in_specs=whole(3 + len(biases), True),
            out_specs=whole(len(shapes)),
            compiler_params=LIGHT,
            cost_estimate=cost(0, 1e6),
        )(
            row,
            conv3.reshape(3 * depth, cols),
            conv1,
            *[bias.reshape(1, cols) for bias in biases],
        )

    def frames_out(row, values):
        return pl.pallas_call(
            frames_kernel,
            out_shape=[shaped((rows, cols), BF16)] * 4,
            in_specs=whole(2, True),
            out_specs=whole(4),
            compiler_params=LIGHT,
            cost_estimate=cost(0, 2e6),
        )(row, values)

    enc_own, enc_half = pack(where_row, enc_conv3, enc_conv1, [enc_bias3, enc_bias1], 1)
    enc_2a = swap(enc_half, "mp", 2)
    feat = list(frames_out(after(where_row, enc_half), features))
    feat[2], feat[3] = swap(feat[2], "mp", 2), swap(feat[3], "mp", 3)
    feat[1] = swap(feat[1], "mp", 1)
    enc_1 = swap(enc_own, "mp", 1)
    enc_2b = swap(enc_2a, "dp", 1)
    enc_3a = swap(enc_2a, "mp", 1)
    enc_3b = swap(enc_2b, "mp", 1)
    enc = (enc_own, enc_1, enc_2a, enc_2b, enc_3a, enc_3b)

    clip_ends = jnp.cumsum(lengths[0])
    starts = clip_ends - lengths[0]

    def ok_at(shift):
        at = me * own - HALO + shift + jnp.arange(rows, dtype=jnp.int32)
        is_start = jnp.any(at[:, None] == starts[None, :], axis=1) | (at == frames)
        return jnp.where(is_start, 0.0, 1.0).astype(F32)[:, None]

    prev_ok, next_ok = ok_at(0), ok_at(1)
    books_f = codebooks.astype(F32)
    norms = jnp.sum(books_f * books_f, axis=3) * (LOG2E / SOFTMAX_WARMTH)
    norms = norms[:, :, None, :]

    codes = num_codes // near
    first = near_at * codes

    def own_codes(array):
        start = (side, level_side, first) + (jnp.int32(0),) * (array.ndim - 3)
        return lax.dynamic_slice(array, start, (1, 1, codes) + array.shape[3:])[0, 0]

    index = own_codes(buffer_index)
    one_hot = index[:, None] == jnp.arange(code_buffer.shape[0], dtype=jnp.int32)[None, :]
    buffer_half = lax.dynamic_slice_in_dim(code_buffer, side * group_dim, group_dim, 1)
    chosen = dot_nn(one_hot.astype(BF16), buffer_half)
    books_own = own_codes(codebooks).astype(F32)
    if quad:
        chosen, books_own = chosen.T, books_own.T

    at = jnp.arange(cols, dtype=jnp.int32)
    turn = ((at[:, None] ^ (near_at * (cols // near))) == at[None, :]).astype(BF16)
    early_row = after(where_row, chosen, books_own, turn, norms, prev_ok, next_ok)

    (dec_own,) = pack(early_row, dec_conv3, dec_conv1, [dec_bias3], 0)
    cot = list(frames_out(early_row, out_cotangent))
    dec_1 = swap(dec_own, "mp", 1)
    dec_2 = swap(after(dec_own, feat[2], feat[3]), "mp", 2)

    hidden_enc, act_mid, latent = pl.pallas_call(
        encoder_kernel,
        out_shape=(
            shaped((rows, depth), F32),
            shaped((rows, depth), BF16),
            shaped((rows, depth), BF16),
        ),
        in_specs=whole(13, True),
        out_specs=tuple(whole(3)),
        scratch_shapes=[
            pltpu.VMEM((rows, depth), BF16),
            pltpu.VMEM((4 * depth + 32, depth), BF16),
            pltpu.VMEM((rows + 16, depth), F32),
            pltpu.VMEM((rows, 3 * depth), BF16),
        ],
        compiler_params=PARAMS,
        cost_estimate=cost(8 * rows * depth * depth, 12e6),
    )(after(where_row, cot[0], dec_own), *feat, *enc, prev_ok, next_ok)

    dec_3 = swap(after(dec_2, latent), "mp", 1)
    dec = (dec_own, dec_1, dec_2, dec_3)
    cot[2], cot[3], _ = lax.optimization_barrier((cot[2], cot[3], dec_2))
    cot = [cot[0]] + [swap(cot[k], "mp", k) for k in (1, 2, 3)]

    step = rows // 3
    quant, usage, prob, second = pl.pallas_call(
        functools.partial(quantize_kernel, own=own),
        grid=(3,),
        out_shape=(
            shaped((rows, depth), BF16),
            shaped((groups, levels, 1, num_codes), F32),
            shaped((groups, levels, rows, num_codes), BF16),
            shaped((levels - 1, rows, depth), BF16),
        ),
        in_specs=[
            pl.BlockSpec((step, depth), lambda i: (i, 0)),
            pl.BlockSpec(codebooks.shape, lambda i: (0, 0, 0, 0)),
            pl.BlockSpec(norms.shape, lambda i: (0, 0, 0, 0)),
        ],
        out_specs=(
            pl.BlockSpec((step, depth), lambda i: (i, 0)),
            pl.BlockSpec((groups, levels, 1, num_codes), lambda i: (0, 0, 0, 0)),
            pl.BlockSpec((groups, levels, step, num_codes), lambda i: (0, 0, i, 0)),
            pl.BlockSpec((levels - 1, step, depth), lambda i: (0, i, 0)),
        ),
        compiler_params=PARAMS,
        cost_estimate=cost(16 * rows * num_codes * group_dim, 30e6),
    )(latent, codebooks, norms)

    packed = 4 * depth + LANES
    grads_shape = (
        shaped((cols, packed), F32),
        shaped((cols, packed), F32),
        shaped((2, cols, packed), BF16),
    )
    grad_quant, *dec_grads = pl.pallas_call(
        functools.partial(decoder_kernel, near=near),
        out_shape=(shaped((rows, depth), F32),) + grads_shape,
        in_specs=whole(12, True),
        out_specs=tuple(whole(4)),
        scratch_shapes=[
            pltpu.VMEM((rows, depth), BF16),
            pltpu.VMEM((4 * depth + 32, depth), BF16),
            pltpu.VMEM((rows + 16, depth), F32),
            pltpu.VMEM((rows, 3 * depth), BF16),
            pltpu.VMEM((rows, depth), BF16),
            pltpu.VMEM((rows, depth), BF16),
        ],
        compiler_params=PARAMS,
        cost_estimate=cost(24 * rows * depth * depth, 20e6),
    )(where_row, quant, *cot, *dec, prev_ok, next_ok)

    table_shape = (levels, near, group_dim + 16, num_codes // near)

    def quantize_back(group, *ties):
        return pl.pallas_call(
            tied(functools.partial(quantize_back_kernel, own=own, levels=levels), 7, len(ties)),
            grid_spec=pltpu.PrefetchScalarGridSpec(
                num_scalar_prefetch=1,
                grid=(3,),
                in_specs=[
                    pl.BlockSpec((step, group_dim), lambda i, g: (i, g[0])),
                    pl.BlockSpec((1, levels, step, num_codes), lambda i, g: (g[0], 0, i, 0)),
                    pl.BlockSpec((step, group_dim), lambda i, g: (i, g[0])),
                    pl.BlockSpec((levels - 1, step, group_dim), lambda i, g: (0, i, g[0])),
                    pl.BlockSpec((1, levels, num_codes, group_dim), lambda i, g: (g[0], 0, 0, 0)),
                    pl.BlockSpec((1, levels, 1, num_codes), lambda i, g: (g[0], 0, 0, 0)),
                ]
                + [pl.BlockSpec(memory_space=pl.ANY)] * len(ties),
                out_specs=(
                    pl.BlockSpec((step, group_dim), lambda i, g: (i, 0)),
                    pl.BlockSpec(table_shape, lambda i, g: (0, 0, 0, 0)),
                    pl.BlockSpec((8, LANES), lambda i, g: (0, 0)),
                ),
                scratch_shapes=[
                    pltpu.VMEM((levels, group_dim, num_codes), F32),
                    pltpu.VMEM((levels, 1, num_codes), F32),
                ],
            ),
            out_shape=(
                shaped((rows, group_dim), BF16),
                shaped(table_shape, BF16),
                shaped((8, LANES), F32),
            ),
            compiler_params=PARAMS,
            cost_estimate=cost(16 * rows * num_codes * group_dim, 15e6),
        )(
            jnp.stack([group, level_side, near_at]),
            grad_quant, prob, latent, second, codebooks, usage, *ties,
        )

    taken = [((rows, depth), BF16), ((4 * depth + 32, depth), BF16)]
    taken += [((rows + 16, depth), F32), ((rows, 3 * depth), BF16)]

    def encoder_weight_grads(*ties):
        return call(
            functools.partial(encoder_weight_grad_kernel, near=near),
            where_row,
            [grad_mine, grad_other, hidden_enc, act_mid, *feat, *enc, prev_ok, next_ok],
            [(out.shape, out.dtype) for out in grads_shape]
            + [((rows, depth), BF16)] * 2 + [((8, LANES), F32)],
            taken,
            ties,
            cost(12 * rows * depth * depth, 20e6),
            PARAMS,
        )

    def encoder_input_grads(low, grad_latent, *ties):
        return call(
            encoder_input_grad_kernel,
            where_row,
            [low, grad_latent, *feat, *enc, prev_ok, next_ok],
            [((own, cols), BF16)] * 4 + [((8, LANES), F32)],
            taken,
            ties,
            cost(6 * rows * depth * depth, 10e6),
            PARAMS,
        )

    def put(mask, block, total, pieces, ties=()):
        return call(
            functools.partial(place_kernel, block=block),
            mask.reshape(1),
            pieces,
            [((total, pieces[0].shape[1]), F32)],
            ties=ties,
            price=cost(0, 8 * total * pieces[0].shape[1]),
        )[0]

    def gather_near(block):
        return jnp.concatenate([block] + [swap(block, "dp", k) for k in range(1, near)], 0)

    def stage(*groups):
        flat = lax.optimization_barrier(tuple(x for group in groups for x in group))
        out = []
        for group in groups:
            out.append(list(flat[: len(group)]))
            flat = flat[len(group) :]
        return out

    grad_other, table_other, mark = quantize_back(1 - side)
    dec_0, dec_2, dec_send = dec_grads
    dec_core = swap(dec_send, "mp", 1)
    dec_send = low_sum(dec_2, dec_core[1]).astype(BF16)
    dec_x = swap(dec_send, "mp", 2)
    table_got = swap(table_other, "mp", 1)
    grad_mine, table_mine, mark = quantize_back(side, mark, dec_send)

    if quad:
        packed_half, table = (cols // 2, packed), table_shape[2:]
        mark_shape = ((8, LANES), F32)
        dec_mine, dec_send, book_send, mark = call(
            halve_kernel,
            where_row,
            [dec_0, dec_core, dec_x, table_mine, table_got],
            [(packed_half, F32), (packed_half, BF16), (table_shape[1:], BF16), mark_shape],
        )
        book_x, dec_got = swap(book_send, "mp", 2), swap(dec_send, "dp", 1)
        enc_0, enc_2, enc_send, low, grad_latent, mark = encoder_weight_grads(mark)
        book_mine, book_send, dec_mine, dec_send, enc_send = call(
            near_kernel,
            where_row,
            [table_mine, table_got, book_x, dec_mine, dec_got, enc_send],
            [(table, F32), (table, BF16), (packed_half, F32), (packed_half, BF16)]
            + [((2, cols, packed), BF16)],
            ties=[mark],
        )
        enc_core = swap(enc_send, "mp", 1)
        book_got, dec_got = swap(book_send, "dp", 1), swap(dec_send, "dp", 2)
        book_mine, book_send, enc_mine, enc_near, enc_x, enc_both, dec_mine, dec_send, mark = call(
            spread_kernel,
            where_row,
            [book_mine, book_got, enc_0, enc_2, enc_core, dec_mine, dec_got],
            [(table, F32), (table, BF16), (packed_half, F32)] + [(packed_half, BF16)] * 3
            + [(packed_half, F32), (packed_half, BF16), mark_shape],
        )
        enc_got = [swap(enc_near, "dp", 1), swap(enc_x, "mp", 2), swap_both(enc_both, 1, 2)]
        book_got, dec_got = swap(book_send, "dp", 2), swap(dec_send, "dp", 4)
        *outs, mark = encoder_input_grads(low, grad_latent, mark)
        book_mine, book_send, enc_mine, enc_send, dec_send = call(
            sum_kernel,
            where_row,
            [book_mine, book_got, enc_mine, *enc_got, dec_mine, dec_got],
            [(table, F32), (table, BF16), (packed_half, F32)] + [(packed_half, BF16)] * 2,
            ties=[mark],
        )
        book_got, enc_got = swap(book_send, "dp", 4), swap(enc_send, "dp", 2)
        dec_got = swap(dec_send, "dp", 1)
        outs = [outs[0]] + [swap(outs[k], "mp", k) for k in (1, 2, 3)]
        grad_features = put(me * own, own, frames, outs)
        fresh, enc_mine, enc_send = call(
            functools.partial(refresh_kernel, share=num_codes / (frames * n_dp)),
            where_row,
            [book_mine, book_got, books_own, chosen, enc_mine, enc_got],
            [((codes, group_dim), BF16), (packed_half, F32), (packed_half, BF16)],
            ties=[grad_features],
        )
        fresh = [fresh, swap(fresh, "dp", 1), swap(fresh, "mp", 2), swap_both(fresh, 1, 2)]
        enc_got = swap(enc_send, "dp", 4)
        (enc_send,) = call(join_kernel, where_row, [enc_mine, enc_got], [(packed_half, BF16)])
        enc_got = swap(enc_send, "dp", 1)
        fresh = fresh + [swap(piece, "mp", 1) for piece in fresh]
        mask = (side * levels + level_side) * num_codes + first
        new_codebooks = put(mask, codes, groups * levels * num_codes, fresh)

        def unpack(mask, *parts):
            conv3, conv1, bias3, bias1 = call(
                functools.partial(unpack_kernel, block=cols // 2),
                mask.reshape(1),
                parts,
                [((3 * depth, cols), F32), ((depth, cols), F32)] + [((1, cols), F32)] * 2,
                [((cols, packed), F32)],
            )
            return (conv3.reshape(3, depth, cols), bias3[0], conv1, bias1[0])

        half = near_at * (cols // 2)
        return (
            grad_features,
            *unpack(half, enc_send, enc_got),
            *unpack(half, dec_send, dec_got),
            new_codebooks.reshape(codebooks.shape),
        )

    book_send = low_sum(table_mine[1], table_got[1]).astype(BF16)
    dec_mine, *dec_send = parts_of(low_sum(dec_0, dec_core[0], dec_x), near)
    dec_send = [piece.astype(BF16) for piece in dec_send]

    (mark,), (book_send,), dec_send = stage([mark], [book_send], dec_send)
    book_x = swap(book_send, "mp", 2)
    dec_got = [swap(piece, "dp", k + 1) for k, piece in enumerate(dec_send)]
    enc_0, enc_2, enc_send, low, grad_latent, mark = encoder_weight_grads(mark)

    def book_sum(k):
        return low_sum(table_mine[0, k], table_got[0, k], book_x[k])

    def pair_sum(held, sent, bit):
        return held + swap(sent, "dp", bit).astype(F32)

    dec_held = low_sum(dec_mine, *dec_got)
    enc_core = swap(enc_send, "mp", 1)
    book_send, (dec_send, _) = stage(
        [book_sum(k).astype(BF16) for k in range(1, near)], [dec_held.astype(BF16), mark]
    )
    book_got = [swap(piece, "dp", k + 1) for k, piece in enumerate(book_send)]
    dec_held = pair_sum(dec_held, dec_send, far_bits[0])
    enc_mine, *enc_near = parts_of(low_sum(enc_0, enc_core[0]), near)
    enc_near = [piece.astype(BF16) for piece in enc_near]
    enc_far = parts_of(low_sum(enc_2, enc_core[1]).astype(BF16), near)
    book_held = low_sum(book_sum(0), *book_got)

    (mark,), enc_near, enc_far, (book_send, dec_send) = stage(
        [mark], enc_near, enc_far, [book_held.astype(BF16), dec_held.astype(BF16)]
    )
    enc_got = [swap(piece, "dp", k + 1) for k, piece in enumerate(enc_near)] + [
        swap_both(piece, k, 2) for k, piece in enumerate(enc_far)
    ]
    book_held = pair_sum(book_held, book_send, far_bits[0])
    dec_held = pair_sum(dec_held, dec_send, far_bits[1])
    for bit in far_bits[2:]:
        dec_held = pair_sum(dec_held, dec_held.astype(BF16), bit)
    *outs, _ = encoder_input_grads(low, grad_latent, mark)

    enc_held = low_sum(enc_mine, *enc_got)
    (book_send, dec_send, enc_send), outs_send = stage(
        [book_held.astype(BF16), dec_held.astype(BF16), enc_held.astype(BF16)], outs[1:]
    )
    book_held = pair_sum(book_held, book_send, far_bits[1])
    enc_held = pair_sum(enc_held, enc_send, far_bits[0])
    outs = [outs[0]] + [swap(piece, "mp", k + 1) for k, piece in enumerate(outs_send)]
    dec_held = gather_near(dec_send)
    for bit in far_bits[2:]:
        book_held = pair_sum(book_held, book_held.astype(BF16), bit)

    share = num_codes / (frames * n_dp)
    book_held = book_held.T
    ratio = book_held[:, group_dim : group_dim + 1] * share
    refresh = jax.nn.sigmoid(SHARPNESS * (THRESHOLD - ratio))
    stepped = books_own - (STEP_SCALE * share) * book_held[:, :group_dim]
    fresh = ((1.0 - refresh) * stepped + refresh * chosen).astype(BF16)

    ((fresh, enc_send),) = stage([fresh, enc_held.astype(BF16)])
    enc_held = pair_sum(enc_held, enc_send, far_bits[1])
    for bit in far_bits[2:]:
        enc_held = pair_sum(enc_held, enc_held.astype(BF16), bit)
    fresh = [
        swap_both(fresh, k, bits) if k or bits else fresh for bits in (0, 2) for k in range(near)
    ]
    enc_held = gather_near(enc_held.astype(BF16))
    fresh = fresh + [swap(part, "mp", 1) for part in fresh]

    mask = (side * levels + level_side) * num_codes + first
    new_codebooks = put(mask, codes, groups * levels * num_codes, fresh)

    def unpack(held):
        biases = dot_tn(held[:, 4 * depth :], turn)
        return (
            dot_tn(held[:, : 3 * depth], turn).reshape(3, depth, cols),
            biases[0],
            dot_tn(held[:, 3 * depth : 4 * depth], turn),
            biases[1],
        )

    grad_features = put(me * own, own, frames, outs)

    return (
        grad_features,
        *unpack(enc_held),
        *unpack(dec_held),
        new_codebooks.reshape(codebooks.shape),
    )


def solution(mesh):
    return jax.shard_map(
        body,
        mesh=mesh,
        in_specs=(
            P("dp", "mp"),
            P("dp", None),
            P(None, None, "mp"),
            P("mp"),
            P(None, "mp"),
            P("mp"),
            P(),
            P(None, None, "mp"),
            P("mp"),
            P(None, "mp"),
            P(),
            P(),
            P("dp", "mp"),
        ),
        out_specs=(
            P("dp", "mp"),
            P(None, None, "mp"),
            P("mp"),
            P(None, "mp"),
            P("mp"),
            P(None, None, "mp"),
            P("mp"),
            P(None, "mp"),
            P("mp"),
            P(),
        ),
        check_vma=False,
    )
```

```python
import functools
import math

import jax
import jax.numpy as jnp
from jax import lax
from jax.experimental import pallas as pl
from jax.experimental.pallas import tpu as pltpu
from jax.sharding import PartitionSpec as P

SOFTMAX_WARMTH = 8.0
THRESHOLD = 0.7
SHARPNESS = 4.0
STEP_SCALE = 0.5
HALO = 16
LANES = 128
LOG2E = math.log2(math.e)
BF16 = jnp.bfloat16
F32 = jnp.float32
VMEM_LIMIT = 56 * 1024 * 1024


def dot_nn(left, right):
    return jnp.dot(left, right, preferred_element_type=F32)


def dot_nt(left, right):
    return lax.dot_general(left, right, (((1,), (1,)), ((), ())), preferred_element_type=F32)


def dot_tn(left, right):
    return lax.dot_general(left, right, (((0,), (0,)), ((), ())), preferred_element_type=F32)


def elu(values):
    return jnp.where(values > 0, values, jnp.exp(jnp.minimum(values, 0.0)) - 1.0)


def elu_slope(values):
    return jnp.exp(jnp.minimum(values, 0.0))


def swap(values, axis, bits):
    size = lax.axis_size(axis)
    return lax.ppermute(values, axis, [(i, i ^ bits) for i in range(size)])


def after(values, *others):
    return lax.optimization_barrier((values,) + others)[0]


def parts_of(total, count):
    size = total.shape[0] // count
    return [total[k * size : k * size + size] for k in range(count)]


def swap_both(values, dp_bits, mp_bits):
    mp = lax.axis_size("mp")
    count = lax.axis_size("dp") * mp
    pairs = [(i, i ^ (dp_bits * mp + mp_bits)) for i in range(count)]
    return lax.ppermute(values, ("dp", "mp"), pairs)


def low_sum(*terms):
    return functools.reduce(lambda x, y: x + y, [t.astype(F32) for t in terms])


def columns_of(me, k):
    return pl.ds(pl.multiple_of((me ^ k) * LANES, LANES), LANES)


def assemble(me, target, pieces):
    for k, piece in enumerate(pieces):
        target[:, columns_of(me, k)] = piece[...]


def assemble_halves(me, side, target, own, across, halves):
    target[:, columns_of(me, 0)] = own[...]
    target[:, columns_of(me, 1)] = across[...]
    for k in (2, 3):
        for j in range(2):
            piece = halves[2 * (k - 2) + j]
            rows = piece.shape[0]
            start = pl.multiple_of((side ^ j) * rows, 16)
            target[pl.ds(start, rows), columns_of(me, k)] = piece[...]


def frames_kernel(where_ref, values, *outs):
    own = outs[0].shape[0] - 2 * HALO
    for k, out in enumerate(outs):
        start = pl.multiple_of((where_ref[0] ^ k) * own, own)
        above = pl.multiple_of(jnp.maximum(start - HALO, 0), HALO)
        below = pl.multiple_of(jnp.minimum(start + own, values.shape[0] - HALO), HALO)
        out[0:HALO, :] = values[pl.ds(above, HALO), :]
        out[HALO : HALO + own, :] = values[pl.ds(start, own), :]
        out[HALO + own : 2 * HALO + own, :] = values[pl.ds(below, HALO), :]


def pack_kernel(where_ref, conv3, conv1, *refs, count):
    biases, weight = refs[:count], refs[count]
    first, second = conv3.shape[0], conv3.shape[0] + conv1.shape[0]
    weight[0:first, :] = conv3[...]
    weight[first:second, :] = conv1[...]
    row = lax.broadcasted_iota(jnp.int32, (32, LANES), 0)
    rows = jnp.zeros((32, LANES), F32)
    for i, bias in enumerate(biases):
        rows = jnp.where(row == i, bias[...].astype(F32), rows)
    weight[second : second + 32, :] = rows.astype(BF16)
    for half in refs[count + 1 :]:
        size = half.shape[0]
        half[...] = weight[pl.ds(pl.multiple_of(where_ref[1] * size, 16), size), :]


def taps_into(source, target, first_ok, last_ok, rows, depth):
    step = rows // 3
    for r in range(0, rows, step):
        here = slice(r, r + step)
        before = source[7 + r : 7 + r + step, :] * first_ok[here, :]
        later = source[9 + r : 9 + r + step, :] * last_ok[here, :]
        target[here, 0:depth] = before.astype(BF16)
        target[here, depth : 2 * depth] = source[8 + r : 8 + r + step, :].astype(BF16)
        target[here, 2 * depth : 3 * depth] = later.astype(BF16)


def encoder_kernel(
    me_ref, f0, f1, f2, f3, w0, w1, w2a, w2b, w3a, w3b, prev_ok, next_ok,
    hidden_ref, mid_ref, latent_ref, feat, weight, act, act3,
):
    me = me_ref[0]
    rows, depth = hidden_ref.shape
    assemble(me, feat, (f0, f1, f2, f3))
    assemble_halves(me, me_ref[1], weight, w0, w1, (w2a, w2b, w3a, w3b))
    step = rows // 3
    for r in range(0, rows, step):
        act[8 + r : 8 + r + step, :] = (
            elu(feat[r : r + step, :].astype(F32)).astype(BF16).astype(F32)
        )
    act[0:8, :] = jnp.zeros((8, depth), F32)
    act[8 + rows : 16 + rows, :] = jnp.zeros((8, depth), F32)
    taps_into(act, act3, prev_ok, next_ok, rows, depth)
    biases = weight[4 * depth : 4 * depth + 16, :].astype(F32)
    for r in range(0, rows, step):
        here = slice(r, r + step)
        hidden = dot_nn(act3[here, :], weight[0 : 3 * depth, :]) + biases[0:1, :]
        hidden_ref[here, :] = hidden
        mid = elu(hidden).astype(BF16)
        mid_ref[here, :] = mid
        latent = (
            feat[here, :].astype(F32)
            + dot_nn(mid, weight[3 * depth : 4 * depth, :])
            + biases[1:2, :]
        )
        latent_ref[here, :] = latent.astype(BF16)


def quantize_kernel(latent_ref, books, norms, quant_ref, usage_ref, prob_ref, second_ref, *, own):
    groups, levels, _, depth = books.shape
    rows = latent_ref.shape[0]
    place = pl.program_id(0) * rows + lax.broadcasted_iota(jnp.int32, (rows, 1), 0)
    mine = jnp.where((place >= HALO) & (place < HALO + own), 1.0, 0.0).astype(F32)

    @pl.when(pl.program_id(0) == 0)
    def _():
        usage_ref[...] = jnp.zeros_like(usage_ref)

    current = [latent_ref[:, g * depth : (g + 1) * depth] for g in range(groups)]
    remain = [c.astype(F32) for c in current]
    summed = [None] * groups
    for level in range(levels):
        for g in range(groups):
            book = books[g, level]
            scores = dot_nt(current[g], book) * (2.0 * LOG2E / SOFTMAX_WARMTH) - norms[g, level]
            terms = jnp.exp2(scores - jnp.max(scores, axis=1, keepdims=True))
            prob = terms * (1.0 / jnp.sum(terms, axis=1, keepdims=True))
            low = prob.astype(BF16)
            prob_ref[g, level] = low
            usage_ref[g, level] += jnp.sum(prob * mine, axis=0, keepdims=True)
            picked = dot_nn(low, book)
            summed[g] = picked if summed[g] is None else summed[g] + picked
            if level + 1 < levels:
                remain[g] = remain[g] - picked
                current[g] = remain[g].astype(BF16)
                second_ref[level, :, g * depth : (g + 1) * depth] = current[g]
    for g in range(groups):
        quant_ref[:, g * depth : (g + 1) * depth] = summed[g].astype(BF16)


def weight_grads(where_ref, near, targets, grad, deep, grad1, deep1, own, depth):
    here = slice(HALO, HALO + own)
    lane = lax.broadcasted_iota(jnp.int32, (own, LANES), 1)
    ones3 = jnp.where(lane == 0, 1.0, 0.0).astype(BF16)
    ones1 = jnp.where(lane == 1, 1.0, 0.0).astype(BF16)
    size = LANES // near

    def ordered(values):
        return jnp.concatenate(
            [values[here, columns_of(where_ref[0], k)] for k in range(len(targets))], 1
        )

    def put(first, values):
        count = values.shape[1]
        for k, target in enumerate(targets):
            for j in range(near):
                start = pl.multiple_of((where_ref[1] ^ j) * size, size)
                row = k * LANES + j * size
                target[pl.ds(start, size), first : first + count] = values[
                    row : row + size, :
                ].astype(target.dtype)

    left, left1 = ordered(grad), ordered(grad1)
    for first in range(0, 3 * depth, depth):
        put(first, dot_tn(left, deep[here, first : first + depth]))
    put(3 * depth, dot_tn(left1, deep1[here, :]))
    put(4 * depth, dot_tn(left, ones3) + dot_tn(left1, ones1))


def input_grad(taps, weight, here, depth):
    return (
        dot_nt(taps[here, 2 * depth : 3 * depth], weight[0:depth, :])
        + dot_nt(taps[here, depth : 2 * depth], weight[depth : 2 * depth, :])
        + dot_nt(taps[here, 0:depth], weight[2 * depth : 3 * depth, :])
    )


def decoder_kernel(
    me_ref, quant, c0, c1, c2, c3, w0, w1, w2, w3, prev_ok, next_ok,
    grad_ref, g0, g2, sent, cot, weight, act, act3, low, mid, *, near,
):
    me = me_ref[0]
    rows, depth = quant.shape
    own = rows - 2 * HALO
    assemble(me, cot, (c0, c1, c2, c3))
    assemble(me, weight, (w0, w1, w2, w3))
    step = rows // 3
    for r in range(0, rows, step):
        act[8 + r : 8 + r + step, :] = (
            elu(quant[r : r + step, :].astype(F32)).astype(BF16).astype(F32)
        )
    act[0:8, :] = jnp.zeros((8, depth), F32)
    act[8 + rows : 16 + rows, :] = jnp.zeros((8, depth), F32)
    taps_into(act, act3, prev_ok, next_ok, rows, depth)
    bias = weight[4 * depth : 4 * depth + 16, :].astype(F32)[0:1, :]
    for r in range(0, rows, step):
        here = slice(r, r + step)
        hidden = dot_nn(act3[here, :], weight[0 : 3 * depth, :]) + bias
        mid[here, :] = elu(hidden).astype(BF16)
        grad = dot_nt(cot[here, :], weight[3 * depth : 4 * depth, :]) * elu_slope(hidden)
        grad = grad.astype(BF16)
        low[here, :] = grad
        act[8 + r : 8 + r + step, :] = grad.astype(F32)
    targets = (g0, sent.at[0], g2, sent.at[1])
    weight_grads(me_ref, near, targets, low, act3, cot, mid, own, depth)
    taps_into(act, act3, prev_ok, next_ok, rows, depth)
    for r in range(0, rows, step):
        here = slice(r, r + step)
        grad_ref[here, :] = cot[here, :].astype(F32) + elu_slope(
            quant[here, :].astype(F32)
        ) * input_grad(act3, weight, here, depth)


def quantize_back_kernel(
    group_ref, grad_ref, prob_ref, first_ref, second_ref, books, usage,
    out_ref, table_ref, mark_ref, total, columns, *, own, levels,
):
    step = pl.program_id(0)
    rows = grad_ref.shape[0]
    place = step * rows + lax.broadcasted_iota(jnp.int32, (rows, 1), 0)
    mine = jnp.where((place >= HALO) & (place < HALO + own), 1.0, 0.0).astype(F32)
    mine_low = mine.astype(BF16)
    scale = 2.0 / SOFTMAX_WARMTH

    @pl.when(step == 0)
    def _():
        total[...] = jnp.zeros_like(total)
        columns[...] = jnp.zeros_like(columns)

    grad_remain = None
    for level in reversed(range(levels)):
        book = books[0, level]
        low = prob_ref[0, level]
        current = first_ref[...] if level == 0 else second_ref[level - 1]
        picked = grad_ref[...] if grad_remain is None else grad_ref[...] - grad_remain
        picked = picked.astype(BF16)
        grad_prob = dot_nt(picked, book)
        prob = low.astype(F32)
        inner = jnp.sum(prob * grad_prob, axis=1, keepdims=True)
        grad_scores = (prob * (grad_prob - inner)).astype(BF16)
        through = dot_nn(grad_scores, book) * scale
        grad_remain = through if grad_remain is None else grad_remain + through
        left = jnp.concatenate([picked * mine_low, current * (mine_low * scale)], 0)
        total[level] += dot_tn(left, jnp.concatenate([low, grad_scores], 0))
        columns[level] += jnp.sum(grad_scores.astype(F32) * mine, axis=0, keepdims=True)
    out_ref[...] = grad_remain.astype(BF16)

    @pl.when(step == pl.num_programs(0) - 1)
    def _():
        depth = books.shape[3]
        row = lax.broadcasted_iota(jnp.int32, (16, table_ref.shape[3]), 0)
        for j in range(levels):
            table = table_ref.at[j]
            level = group_ref[1] ^ j
            codes = table.shape[2]
            turned = books[0, level].astype(F32).T
            for k in range(table.shape[0]):
                here = slice(k * codes, k * codes + codes)
                part = group_ref[2] ^ k
                table[part, 0:depth, :] = (
                    total[level, :, here] - scale * columns[level, :, here] * turned[:, here]
                ).astype(BF16)
                table[part, depth : depth + 16, :] = jnp.where(
                    row == 0, usage[0, level, :, here], 0.0
                ).astype(BF16)
        mark_ref[...] = jnp.zeros_like(mark_ref)


def encoder_weight_grad_kernel(
    me_ref, grad_mine, grad_other, hidden, mid, f0, f1, f2, f3,
    w0, w1, w2a, w2b, w3a, w3b, prev_ok, next_ok,
    g0, g2, sent, low, grad_latent, mark, feat, weight, act, act3, *, near,
):
    mark[...] = jnp.zeros_like(mark)
    me = me_ref[0]
    rows, depth = hidden.shape
    own = rows - 2 * HALO
    half = grad_mine.shape[1]
    side = me_ref[2]
    grad_latent[:, pl.ds(pl.multiple_of(side * half, half), half)] = grad_mine[...]
    grad_latent[:, pl.ds(pl.multiple_of((1 - side) * half, half), half)] = grad_other[...]
    assemble(me, feat, (f0, f1, f2, f3))
    assemble_halves(me, me_ref[1], weight, w0, w1, (w2a, w2b, w3a, w3b))
    step = rows // 3
    for r in range(0, rows, step):
        act[8 + r : 8 + r + step, :] = (
            elu(feat[r : r + step, :].astype(F32)).astype(BF16).astype(F32)
        )
    act[0:8, :] = jnp.zeros((8, depth), F32)
    act[8 + rows : 16 + rows, :] = jnp.zeros((8, depth), F32)
    taps_into(act, act3, prev_ok, next_ok, rows, depth)
    for r in range(0, rows, step):
        here = slice(r, r + step)
        grad = dot_nt(grad_latent[here, :], weight[3 * depth : 4 * depth, :])
        low[here, :] = (grad * elu_slope(hidden[here, :])).astype(BF16)
    targets = (g0, sent.at[0], g2, sent.at[1])
    weight_grads(me_ref, near, targets, low, act3, grad_latent, mid, own, depth)


def encoder_input_grad_kernel(
    me_ref, low, grad_latent, f0, f1, f2, f3, w0, w1, w2a, w2b, w3a, w3b, prev_ok, next_ok,
    o0, o1, o2, o3, mark, feat, weight, act, act3,
):
    mark[...] = jnp.zeros_like(mark)
    me = me_ref[0]
    rows, depth = low.shape
    own = rows - 2 * HALO
    assemble(me, feat, (f0, f1, f2, f3))
    assemble_halves(me, me_ref[1], weight, w0, w1, (w2a, w2b, w3a, w3b))
    act[8 : 8 + rows, :] = low[...].astype(F32)
    act[0:8, :] = jnp.zeros((8, depth), F32)
    act[8 + rows : 16 + rows, :] = jnp.zeros((8, depth), F32)
    taps_into(act, act3, prev_ok, next_ok, rows, depth)
    for r in range(HALO, HALO + own, own // 4):
        here = slice(r, r + own // 4)
        feat[here, :] = (
            grad_latent[here, :].astype(F32)
            + elu_slope(feat[here, :].astype(F32)) * input_grad(act3, weight, here, depth)
        ).astype(BF16)
    for k, out in enumerate((o0, o1, o2, o3)):
        out[...] = feat[HALO : HALO + own, columns_of(me, k)]


def place_kernel(mask_ref, *refs, block):
    out, first = refs[-1], 0
    for ref in refs[:-1]:
        for r in range(0, ref.shape[0], block):
            start = pl.multiple_of((first + r) ^ mask_ref[0], block)
            out[pl.ds(start, block), :] = ref[r : r + block, :].astype(F32)
        first += ref.shape[0]


def sum_of(*refs):
    return functools.reduce(lambda x, y: x + y, [ref[...].astype(F32) for ref in refs])


def halve_kernel(where_ref, d0, d1, dx, t0, t1, mine, sent, book_sent, mark):
    half = mine.shape[0]
    total = sum_of(d0, d1.at[0], dx)
    mine[...] = total[:half]
    sent[...] = total[half:].astype(BF16)
    book_sent[...] = sum_of(t0.at[1], t1.at[1]).astype(BF16)
    mark[...] = jnp.zeros_like(mark)


def near_kernel(
    where_ref, t0, t1, bx, d0, d1, core, book_mine, book_sent, dec_mine, dec_sent, passed
):
    passed[...] = core[...]
    for k, out in enumerate((book_mine, book_sent)):
        out[...] = sum_of(t0.at[0, k], t1.at[0, k], bx.at[k]).astype(out.dtype)
    total = sum_of(d0, d1)
    dec_mine[...] = total
    dec_sent[...] = total.astype(BF16)


def spread_kernel(
    where_ref, b0, b1, e0, e2, core, d0, d1,
    book_mine, book_sent, enc_mine, enc_near, enc_x, enc_both, dec_mine, dec_sent, mark,
):
    half = enc_mine.shape[0]
    total = sum_of(e0, core.at[0])
    enc_mine[...] = total[:half]
    enc_near[...] = total[half:].astype(BF16)
    total = sum_of(e2, core.at[1])
    enc_x[...] = total[:half].astype(BF16)
    enc_both[...] = total[half:].astype(BF16)
    for mine, sent, total in (
        (book_mine, book_sent, sum_of(b0, b1)),
        (dec_mine, dec_sent, sum_of(d0, d1)),
    ):
        mine[...] = total
        sent[...] = total.astype(BF16)
    mark[...] = jnp.zeros_like(mark)


def sum_kernel(
    where_ref, b0, b1, e0, e1, e2, e3, d0, d1, book_mine, book_sent, enc_mine, enc_sent, dec_sent
):
    for mine, sent, total in (
        (book_mine, book_sent, sum_of(b0, b1)),
        (enc_mine, enc_sent, sum_of(e0, e1, e2, e3)),
    ):
        mine[...] = total
        sent[...] = total.astype(BF16)
    dec_sent[...] = sum_of(d0, d1).astype(BF16)


def refresh_kernel(where_ref, b0, b1, books, chosen, e0, e1, fresh, enc_mine, enc_sent, *, share):
    held = sum_of(b0, b1)
    depth = books.shape[0]
    ratio = held[depth : depth + 1, :] * share
    refresh = jax.nn.sigmoid(SHARPNESS * (THRESHOLD - ratio))
    stepped = books[...] - (STEP_SCALE * share) * held[:depth, :]
    fresh[...] = ((1.0 - refresh) * stepped + refresh * chosen[...]).T.astype(BF16)
    total = sum_of(e0, e1)
    enc_mine[...] = total
    enc_sent[...] = total.astype(BF16)


def join_kernel(where_ref, e0, e1, enc):
    enc[...] = sum_of(e0, e1).astype(BF16)


def unpack_kernel(mask_ref, *refs, block):
    *parts, conv3, conv1, bias3, bias1, held = refs
    first = 0
    for part in parts:
        for r in range(0, part.shape[0], block):
            start = pl.multiple_of((first + r) ^ mask_ref[0], block)
            held[pl.ds(start, block), :] = part[r : r + block, :].astype(F32)
        first += part.shape[0]
    count3, count1 = conv3.shape[0], conv1.shape[0]
    conv3[...] = held[:, 0:count3].T
    conv1[...] = held[:, count3 : count3 + count1].T
    biases = held[:, count3 + count1 :].T
    bias3[...] = biases[0:1, :]
    bias1[...] = biases[1:2, :]


def whole(count, smem_first=False):
    specs = [pl.BlockSpec(memory_space=pltpu.VMEM)] * count
    if smem_first:
        specs[0] = pl.BlockSpec(memory_space=pltpu.SMEM)
    return specs


def cost(flops, moved):
    return pl.CostEstimate(flops=int(flops), bytes_accessed=int(moved), transcendentals=0)


def shaped(shape, dtype):
    return jax.ShapeDtypeStruct(shape, dtype)


PARAMS = pltpu.CompilerParams(vmem_limit_bytes=VMEM_LIMIT)
LIGHT = pltpu.CompilerParams(vmem_limit_bytes=14 * 1024 * 1024)


def tied(kernel, first, count):
    def without(*refs):
        kernel(*refs[:first], *refs[first + count :])

    return without


def call(kernel, row, inputs, outs, scratch=(), ties=(), price=None, params=None):
    return pl.pallas_call(
        tied(kernel, 1 + len(inputs), len(ties)),
        out_shape=[shaped(*out) for out in outs],
        in_specs=whole(1 + len(inputs), True) + [pl.BlockSpec(memory_space=pl.ANY)] * len(ties),
        out_specs=whole(len(outs)),
        scratch_shapes=[pltpu.VMEM(*buffer) for buffer in scratch],
        compiler_params=params or LIGHT,
        cost_estimate=price or cost(0, 2e6),
    )(row, *inputs, *ties)


def body(
    features,
    lengths,
    enc_conv3,
    enc_bias3,
    enc_conv1,
    enc_bias1,
    codebooks,
    dec_conv3,
    dec_bias3,
    dec_conv1,
    code_buffer,
    buffer_index,
    out_cotangent,
):
    frames, cols = features.shape
    groups, levels, num_codes, group_dim = codebooks.shape
    width = lax.axis_size("mp")
    n_dp = lax.axis_size("dp")
    me = lax.axis_index("mp")
    place = lax.axis_index("dp")
    own = frames // width
    rows = own + 2 * HALO
    depth = cols * width
    side, level_side = me % 2, me // 2
    near = 2 if n_dp % 2 == 0 else n_dp
    near_at = place % near
    far_bits = [near << i for i in range((n_dp // near).bit_length() - 1)]
    where_row = jnp.stack([me, near_at, side, place // near])
    quad = near == 2 and n_dp == 8

    def pack(row, conv3, conv1, biases, half):
        total = conv3.shape[0] * conv3.shape[1] + conv1.shape[0] + 32
        shapes = [shaped((total, cols), BF16)] + [shaped((total // 2, cols), BF16)] * half
        return pl.pallas_call(
            functools.partial(pack_kernel, count=len(biases)),
            out_shape=shapes,
            in_specs=whole(3 + len(biases), True),
            out_specs=whole(len(shapes)),
            compiler_params=PARAMS if half else LIGHT,
            cost_estimate=cost(0, 1e6),
        )(
            row,
            conv3.reshape(3 * depth, cols),
            conv1,
            *[bias.reshape(1, cols) for bias in biases],
        )

    def frames_out(row, values):
        return pl.pallas_call(
            frames_kernel,
            out_shape=[shaped((rows, cols), BF16)] * 4,
            in_specs=whole(2, True),
            out_specs=whole(4),
            compiler_params=LIGHT,
            cost_estimate=cost(0, 2e6),
        )(row, values)

    enc_own, enc_half = pack(where_row, enc_conv3, enc_conv1, [enc_bias3, enc_bias1], 1)
    enc_2a = swap(enc_half, "mp", 2)
    feat = list(frames_out(after(where_row, enc_half), features))
    feat[2], feat[3] = swap(feat[2], "mp", 2), swap(feat[3], "mp", 3)
    feat[1] = swap(feat[1], "mp", 1)
    enc_1 = swap(enc_own, "mp", 1)
    enc_2b = swap(enc_2a, "dp", 1)
    enc_3a = swap(enc_2a, "mp", 1)
    enc_3b = swap(enc_2b, "mp", 1)
    enc = (enc_own, enc_1, enc_2a, enc_2b, enc_3a, enc_3b)

    clip_ends = jnp.cumsum(lengths[0])
    starts = clip_ends - lengths[0]

    def ok_at(shift):
        at = me * own - HALO + shift + jnp.arange(rows, dtype=jnp.int32)
        is_start = jnp.any(at[:, None] == starts[None, :], axis=1) | (at == frames)
        return jnp.where(is_start, 0.0, 1.0).astype(F32)[:, None]

    prev_ok, next_ok = ok_at(0), ok_at(1)
    books_f = codebooks.astype(F32)
    norms = jnp.sum(books_f * books_f, axis=3) * (LOG2E / SOFTMAX_WARMTH)
    norms = norms[:, :, None, :]

    codes = num_codes // near
    first = near_at * codes

    def own_codes(array):
        start = (side, level_side, first) + (jnp.int32(0),) * (array.ndim - 3)
        return lax.dynamic_slice(array, start, (1, 1, codes) + array.shape[3:])[0, 0]

    index = own_codes(buffer_index)
    one_hot = index[:, None] == jnp.arange(code_buffer.shape[0], dtype=jnp.int32)[None, :]
    buffer_half = lax.dynamic_slice_in_dim(code_buffer, side * group_dim, group_dim, 1)
    chosen = dot_nn(one_hot.astype(BF16), buffer_half)
    books_own = own_codes(codebooks).astype(F32)
    if quad:
        chosen, books_own = chosen.T, books_own.T

    at = jnp.arange(cols, dtype=jnp.int32)
    turn = ((at[:, None] ^ (near_at * (cols // near))) == at[None, :]).astype(BF16)
    early_row = after(where_row, chosen, books_own, turn, norms, prev_ok, next_ok)

    (dec_own,) = pack(early_row, dec_conv3, dec_conv1, [dec_bias3], 0)
    cot = list(frames_out(early_row, out_cotangent))
    dec_1 = swap(dec_own, "mp", 1)
    dec_2 = swap(after(dec_own, feat[2], feat[3]), "mp", 2)

    hidden_enc, act_mid, latent = pl.pallas_call(
        encoder_kernel,
        out_shape=(
            shaped((rows, depth), F32),
            shaped((rows, depth), BF16),
            shaped((rows, depth), BF16),
        ),
        in_specs=whole(13, True),
        out_specs=tuple(whole(3)),
        scratch_shapes=[
            pltpu.VMEM((rows, depth), BF16),
            pltpu.VMEM((4 * depth + 32, depth), BF16),
            pltpu.VMEM((rows + 16, depth), F32),
            pltpu.VMEM((rows, 3 * depth), BF16),
        ],
        compiler_params=PARAMS,
        cost_estimate=cost(8 * rows * depth * depth, 12e6),
    )(after(where_row, cot[0], dec_own), *feat, *enc, prev_ok, next_ok)

    dec_3 = swap(after(dec_2, latent), "mp", 1)
    dec = (dec_own, dec_1, dec_2, dec_3)
    cot[2], cot[3], _ = lax.optimization_barrier((cot[2], cot[3], dec_2))
    cot = [cot[0]] + [swap(cot[k], "mp", k) for k in (1, 2, 3)]

    step = rows // 3
    quant, usage, prob, second = pl.pallas_call(
        functools.partial(quantize_kernel, own=own),
        grid=(3,),
        out_shape=(
            shaped((rows, depth), BF16),
            shaped((groups, levels, 1, num_codes), F32),
            shaped((groups, levels, rows, num_codes), BF16),
            shaped((levels - 1, rows, depth), BF16),
        ),
        in_specs=[
            pl.BlockSpec((step, depth), lambda i: (i, 0)),
            pl.BlockSpec(codebooks.shape, lambda i: (0, 0, 0, 0)),
            pl.BlockSpec(norms.shape, lambda i: (0, 0, 0, 0)),
        ],
        out_specs=(
            pl.BlockSpec((step, depth), lambda i: (i, 0)),
            pl.BlockSpec((groups, levels, 1, num_codes), lambda i: (0, 0, 0, 0)),
            pl.BlockSpec((groups, levels, step, num_codes), lambda i: (0, 0, i, 0)),
            pl.BlockSpec((levels - 1, step, depth), lambda i: (0, i, 0)),
        ),
        compiler_params=PARAMS,
        cost_estimate=cost(16 * rows * num_codes * group_dim, 30e6),
    )(latent, codebooks, norms)

    packed = 4 * depth + LANES
    grads_shape = (
        shaped((cols, packed), F32),
        shaped((cols, packed), F32),
        shaped((2, cols, packed), BF16),
    )
    grad_quant, *dec_grads = pl.pallas_call(
        functools.partial(decoder_kernel, near=near),
        out_shape=(shaped((rows, depth), F32),) + grads_shape,
        in_specs=whole(12, True),
        out_specs=tuple(whole(4)),
        scratch_shapes=[
            pltpu.VMEM((rows, depth), BF16),
            pltpu.VMEM((4 * depth + 32, depth), BF16),
            pltpu.VMEM((rows + 16, depth), F32),
            pltpu.VMEM((rows, 3 * depth), BF16),
            pltpu.VMEM((rows, depth), BF16),
            pltpu.VMEM((rows, depth), BF16),
        ],
        compiler_params=PARAMS,
        cost_estimate=cost(24 * rows * depth * depth, 20e6),
    )(where_row, quant, *cot, *dec, prev_ok, next_ok)

    table_shape = (levels, near, group_dim + 16, num_codes // near)

    def quantize_back(group, *ties):
        return pl.pallas_call(
            tied(functools.partial(quantize_back_kernel, own=own, levels=levels), 7, len(ties)),
            grid_spec=pltpu.PrefetchScalarGridSpec(
                num_scalar_prefetch=1,
                grid=(2,),
                in_specs=[
                    pl.BlockSpec((rows // 2, group_dim), lambda i, g: (i, g[0])),
                    pl.BlockSpec((1, levels, rows // 2, num_codes), lambda i, g: (g[0], 0, i, 0)),
                    pl.BlockSpec((rows // 2, group_dim), lambda i, g: (i, g[0])),
                    pl.BlockSpec((levels - 1, rows // 2, group_dim), lambda i, g: (0, i, g[0])),
                    pl.BlockSpec((1, levels, num_codes, group_dim), lambda i, g: (g[0], 0, 0, 0)),
                    pl.BlockSpec((1, levels, 1, num_codes), lambda i, g: (g[0], 0, 0, 0)),
                ]
                + [pl.BlockSpec(memory_space=pl.ANY)] * len(ties),
                out_specs=(
                    pl.BlockSpec((rows // 2, group_dim), lambda i, g: (i, 0)),
                    pl.BlockSpec(table_shape, lambda i, g: (0, 0, 0, 0)),
                    pl.BlockSpec((8, LANES), lambda i, g: (0, 0)),
                ),
                scratch_shapes=[
                    pltpu.VMEM((levels, group_dim, num_codes), F32),
                    pltpu.VMEM((levels, 1, num_codes), F32),
                ],
            ),
            out_shape=(
                shaped((rows, group_dim), BF16),
                shaped(table_shape, BF16),
                shaped((8, LANES), F32),
            ),
            compiler_params=PARAMS,
            cost_estimate=cost(16 * rows * num_codes * group_dim, 15e6),
        )(
            jnp.stack([group, level_side, near_at]),
            grad_quant, prob, latent, second, codebooks, usage, *ties,
        )

    taken = [((rows, depth), BF16), ((4 * depth + 32, depth), BF16)]
    taken += [((rows + 16, depth), F32), ((rows, 3 * depth), BF16)]

    def encoder_weight_grads(*ties):
        return call(
            functools.partial(encoder_weight_grad_kernel, near=near),
            where_row,
            [grad_mine, grad_other, hidden_enc, act_mid, *feat, *enc, prev_ok, next_ok],
            [(out.shape, out.dtype) for out in grads_shape]
            + [((rows, depth), BF16)] * 2 + [((8, LANES), F32)],
            taken,
            ties,
            cost(12 * rows * depth * depth, 20e6),
            PARAMS,
        )

    def encoder_input_grads(low, grad_latent, *ties):
        return call(
            encoder_input_grad_kernel,
            where_row,
            [low, grad_latent, *feat, *enc, prev_ok, next_ok],
            [((own, cols), BF16)] * 4 + [((8, LANES), F32)],
            taken,
            ties,
            cost(6 * rows * depth * depth, 10e6),
            PARAMS,
        )

    def put(mask, block, total, pieces, ties=(), params=None):
        return call(
            functools.partial(place_kernel, block=block),
            mask.reshape(1),
            pieces,
            [((total, pieces[0].shape[1]), F32)],
            ties=ties,
            price=cost(0, 8 * total * pieces[0].shape[1]),
            params=params,
        )[0]

    def gather_near(block):
        return jnp.concatenate([block] + [swap(block, "dp", k) for k in range(1, near)], 0)

    def stage(*groups):
        flat = lax.optimization_barrier(tuple(x for group in groups for x in group))
        out = []
        for group in groups:
            out.append(list(flat[: len(group)]))
            flat = flat[len(group) :]
        return out

    grad_other, table_other, mark = quantize_back(1 - side)
    dec_0, dec_2, dec_send = dec_grads
    dec_core = swap(dec_send, "mp", 1)
    dec_send = low_sum(dec_2, dec_core[1]).astype(BF16)
    dec_x = swap(dec_send, "mp", 2)
    table_got = swap(table_other, "mp", 1)
    grad_mine, table_mine, mark = quantize_back(side, mark, dec_send)

    if quad:
        packed_half, table = (cols // 2, packed), table_shape[2:]
        mark_shape = ((8, LANES), F32)
        dec_mine, dec_send, book_send, mark = call(
            halve_kernel,
            where_row,
            [dec_0, dec_core, dec_x, table_mine, table_got],
            [(packed_half, F32), (packed_half, BF16), (table_shape[1:], BF16), mark_shape],
        )
        book_x, dec_got = swap(book_send, "mp", 2), swap(dec_send, "dp", 1)
        enc_0, enc_2, enc_send, low, grad_latent, mark = encoder_weight_grads(mark)
        book_mine, book_send, dec_mine, dec_send, enc_send = call(
            near_kernel,
            where_row,
            [table_mine, table_got, book_x, dec_mine, dec_got, enc_send],
            [(table, F32), (table, BF16), (packed_half, F32), (packed_half, BF16)]
            + [((2, cols, packed), BF16)],
            ties=[mark],
        )
        enc_core = swap(enc_send, "mp", 1)
        book_got, dec_got = swap(book_send, "dp", 1), swap(dec_send, "dp", 2)
        book_mine, book_send, enc_mine, enc_near, enc_x, enc_both, dec_mine, dec_send, mark = call(
            spread_kernel,
            where_row,
            [book_mine, book_got, enc_0, enc_2, enc_core, dec_mine, dec_got],
            [(table, F32), (table, BF16), (packed_half, F32)] + [(packed_half, BF16)] * 3
            + [(packed_half, F32), (packed_half, BF16), mark_shape],
        )
        enc_got = [swap(enc_near, "dp", 1), swap(enc_x, "mp", 2), swap_both(enc_both, 1, 2)]
        book_got, dec_got = swap(book_send, "dp", 2), swap(dec_send, "dp", 4)
        *outs, mark = encoder_input_grads(low, grad_latent, mark)
        book_mine, book_send, enc_mine, enc_send, dec_send = call(
            sum_kernel,
            where_row,
            [book_mine, book_got, enc_mine, *enc_got, dec_mine, dec_got],
            [(table, F32), (table, BF16), (packed_half, F32)] + [(packed_half, BF16)] * 2,
            ties=[mark],
        )
        book_got, enc_got = swap(book_send, "dp", 4), swap(enc_send, "dp", 2)
        dec_got = swap(dec_send, "dp", 1)
        outs = [outs[0]] + [swap(outs[k], "mp", k) for k in (1, 2, 3)]
        grad_features = put(me * own, own, frames, outs)
        fresh, enc_mine, enc_send = call(
            functools.partial(refresh_kernel, share=num_codes / (frames * n_dp)),
            where_row,
            [book_mine, book_got, books_own, chosen, enc_mine, enc_got],
            [((codes, group_dim), BF16), (packed_half, F32), (packed_half, BF16)],
            ties=[grad_features],
        )
        fresh = [fresh, swap(fresh, "dp", 1), swap(fresh, "mp", 2), swap_both(fresh, 1, 2)]
        enc_got = swap(enc_send, "dp", 4)
        (enc_send,) = call(join_kernel, where_row, [enc_mine, enc_got], [(packed_half, BF16)])
        enc_got = swap(enc_send, "dp", 1)
        fresh = fresh + [swap(piece, "mp", 1) for piece in fresh]
        mask = (side * levels + level_side) * num_codes + first
        new_codebooks = put(mask, codes, groups * levels * num_codes, fresh, params=PARAMS)

        def unpack(mask, *parts):
            conv3, conv1, bias3, bias1 = call(
                functools.partial(unpack_kernel, block=cols // 2),
                mask.reshape(1),
                parts,
                [((3 * depth, cols), F32), ((depth, cols), F32)] + [((1, cols), F32)] * 2,
                [((cols, packed), F32)],
            )
            return (conv3.reshape(3, depth, cols), bias3[0], conv1, bias1[0])

        half = near_at * (cols // 2)
        return (
            grad_features,
            *unpack(half, enc_send, enc_got),
            *unpack(half, dec_send, dec_got),
            new_codebooks.reshape(codebooks.shape),
        )

    book_send = low_sum(table_mine[1], table_got[1]).astype(BF16)
    dec_mine, *dec_send = parts_of(low_sum(dec_0, dec_core[0], dec_x), near)
    dec_send = [piece.astype(BF16) for piece in dec_send]

    (mark,), (book_send,), dec_send = stage([mark], [book_send], dec_send)
    book_x = swap(book_send, "mp", 2)
    dec_got = [swap(piece, "dp", k + 1) for k, piece in enumerate(dec_send)]
    enc_0, enc_2, enc_send, low, grad_latent, mark = encoder_weight_grads(mark)

    def book_sum(k):
        return low_sum(table_mine[0, k], table_got[0, k], book_x[k])

    def pair_sum(held, sent, bit):
        return held + swap(sent, "dp", bit).astype(F32)

    dec_held = low_sum(dec_mine, *dec_got)
    enc_core = swap(enc_send, "mp", 1)
    book_send, (dec_send, _) = stage(
        [book_sum(k).astype(BF16) for k in range(1, near)], [dec_held.astype(BF16), mark]
    )
    book_got = [swap(piece, "dp", k + 1) for k, piece in enumerate(book_send)]
    dec_held = pair_sum(dec_held, dec_send, far_bits[0])
    enc_mine, *enc_near = parts_of(low_sum(enc_0, enc_core[0]), near)
    enc_near = [piece.astype(BF16) for piece in enc_near]
    enc_far = parts_of(low_sum(enc_2, enc_core[1]).astype(BF16), near)
    book_held = low_sum(book_sum(0), *book_got)

    (mark,), enc_near, enc_far, (book_send, dec_send) = stage(
        [mark], enc_near, enc_far, [book_held.astype(BF16), dec_held.astype(BF16)]
    )
    enc_got = [swap(piece, "dp", k + 1) for k, piece in enumerate(enc_near)] + [
        swap_both(piece, k, 2) for k, piece in enumerate(enc_far)
    ]
    book_held = pair_sum(book_held, book_send, far_bits[0])
    dec_held = pair_sum(dec_held, dec_send, far_bits[1])
    for bit in far_bits[2:]:
        dec_held = pair_sum(dec_held, dec_held.astype(BF16), bit)
    *outs, _ = encoder_input_grads(low, grad_latent, mark)

    enc_held = low_sum(enc_mine, *enc_got)
    (book_send, dec_send, enc_send), outs_send = stage(
        [book_held.astype(BF16), dec_held.astype(BF16), enc_held.astype(BF16)], outs[1:]
    )
    book_held = pair_sum(book_held, book_send, far_bits[1])
    enc_held = pair_sum(enc_held, enc_send, far_bits[0])
    outs = [outs[0]] + [swap(piece, "mp", k + 1) for k, piece in enumerate(outs_send)]
    dec_held = gather_near(dec_send)
    for bit in far_bits[2:]:
        book_held = pair_sum(book_held, book_held.astype(BF16), bit)

    share = num_codes / (frames * n_dp)
    book_held = book_held.T
    ratio = book_held[:, group_dim : group_dim + 1] * share
    refresh = jax.nn.sigmoid(SHARPNESS * (THRESHOLD - ratio))
    stepped = books_own - (STEP_SCALE * share) * book_held[:, :group_dim]
    fresh = ((1.0 - refresh) * stepped + refresh * chosen).astype(BF16)

    ((fresh, enc_send),) = stage([fresh, enc_held.astype(BF16)])
    enc_held = pair_sum(enc_held, enc_send, far_bits[1])
    for bit in far_bits[2:]:
        enc_held = pair_sum(enc_held, enc_held.astype(BF16), bit)
    fresh = [
        swap_both(fresh, k, bits) if k or bits else fresh for bits in (0, 2) for k in range(near)
    ]
    enc_held = gather_near(enc_held.astype(BF16))
    fresh = fresh + [swap(part, "mp", 1) for part in fresh]

    mask = (side * levels + level_side) * num_codes + first
    new_codebooks = put(mask, codes, groups * levels * num_codes, fresh)

    def unpack(held):
        biases = dot_tn(held[:, 4 * depth :], turn)
        return (
            dot_tn(held[:, : 3 * depth], turn).reshape(3, depth, cols),
            biases[0],
            dot_tn(held[:, 3 * depth : 4 * depth], turn),
            biases[1],
        )

    grad_features = put(me * own, own, frames, outs)

    return (
        grad_features,
        *unpack(enc_held),
        *unpack(dec_held),
        new_codebooks.reshape(codebooks.shape),
    )


def solution(mesh):
    return jax.shard_map(
        body,
        mesh=mesh,
        in_specs=(
            P("dp", "mp"),
            P("dp", None),
            P(None, None, "mp"),
            P("mp"),
            P(None, "mp"),
            P("mp"),
            P(),
            P(None, None, "mp"),
            P("mp"),
            P(None, "mp"),
            P(),
            P(),
            P("dp", "mp"),
        ),
        out_specs=(
            P("dp", "mp"),
            P(None, None, "mp"),
            P("mp"),
            P(None, "mp"),
            P("mp"),
            P(None, None, "mp"),
            P("mp"),
            P(None, "mp"),
            P("mp"),
            P(),
        ),
        check_vma=False,
    )
```

```python
import functools
import math

import jax
import jax.numpy as jnp
from jax import lax
from jax.experimental import pallas as pl
from jax.experimental.pallas import tpu as pltpu
from jax.sharding import PartitionSpec as P

SOFTMAX_WARMTH = 8.0
THRESHOLD = 0.7
SHARPNESS = 4.0
STEP_SCALE = 0.5
HALO = 16
LANES = 128
LOG2E = math.log2(math.e)
BF16 = jnp.bfloat16
F32 = jnp.float32
VMEM_LIMIT = 56 * 1024 * 1024


def dot_nn(left, right):
    return jnp.dot(left, right, preferred_element_type=F32)


def dot_nt(left, right):
    return lax.dot_general(left, right, (((1,), (1,)), ((), ())), preferred_element_type=F32)


def dot_tn(left, right):
    return lax.dot_general(left, right, (((0,), (0,)), ((), ())), preferred_element_type=F32)


def elu(values):
    return jnp.where(values > 0, values, jnp.exp(jnp.minimum(values, 0.0)) - 1.0)


def elu_slope(values):
    return jnp.exp(jnp.minimum(values, 0.0))


def swap(values, axis, bits):
    size = lax.axis_size(axis)
    return lax.ppermute(values, axis, [(i, i ^ bits) for i in range(size)])


def after(values, *others):
    return lax.optimization_barrier((values,) + others)[0]


def parts_of(total, count):
    size = total.shape[0] // count
    return [total[k * size : k * size + size] for k in range(count)]


def swap_both(values, dp_bits, mp_bits):
    mp = lax.axis_size("mp")
    count = lax.axis_size("dp") * mp
    pairs = [(i, i ^ (dp_bits * mp + mp_bits)) for i in range(count)]
    return lax.ppermute(values, ("dp", "mp"), pairs)


def low_sum(*terms):
    return functools.reduce(lambda x, y: x + y, [t.astype(F32) for t in terms])


def columns_of(me, k):
    return pl.ds(pl.multiple_of((me ^ k) * LANES, LANES), LANES)


def assemble(me, target, pieces):
    for k, piece in enumerate(pieces):
        target[:, columns_of(me, k)] = piece[...]


def assemble_halves(me, side, target, own, across, halves):
    target[:, columns_of(me, 0)] = own[...]
    target[:, columns_of(me, 1)] = across[...]
    for k in (2, 3):
        for j in range(2):
            piece = halves[2 * (k - 2) + j]
            rows = piece.shape[0]
            start = pl.multiple_of((side ^ j) * rows, 16)
            target[pl.ds(start, rows), columns_of(me, k)] = piece[...]


def frames_kernel(where_ref, values, *outs):
    own = outs[0].shape[0] - 2 * HALO
    for k, out in enumerate(outs):
        start = pl.multiple_of((where_ref[0] ^ k) * own, own)
        above = pl.multiple_of(jnp.maximum(start - HALO, 0), HALO)
        below = pl.multiple_of(jnp.minimum(start + own, values.shape[0] - HALO), HALO)
        out[0:HALO, :] = values[pl.ds(above, HALO), :]
        out[HALO : HALO + own, :] = values[pl.ds(start, own), :]
        out[HALO + own : 2 * HALO + own, :] = values[pl.ds(below, HALO), :]


def pack_kernel(where_ref, conv3, conv1, *refs, count):
    biases, weight = refs[:count], refs[count]
    first, second = conv3.shape[0], conv3.shape[0] + conv1.shape[0]
    weight[0:first, :] = conv3[...]
    weight[first:second, :] = conv1[...]
    row = lax.broadcasted_iota(jnp.int32, (32, LANES), 0)
    rows = jnp.zeros((32, LANES), F32)
    for i, bias in enumerate(biases):
        rows = jnp.where(row == i, bias[...].astype(F32), rows)
    weight[second : second + 32, :] = rows.astype(BF16)
    for half in refs[count + 1 :]:
        size = half.shape[0]
        half[...] = weight[pl.ds(pl.multiple_of(where_ref[1] * size, 16), size), :]


def taps_into(source, target, first_ok, last_ok, rows, depth):
    step = rows // 3
    for r in range(0, rows, step):
        here = slice(r, r + step)
        before = source[7 + r : 7 + r + step, :] * first_ok[here, :]
        later = source[9 + r : 9 + r + step, :] * last_ok[here, :]
        target[here, 0:depth] = before.astype(BF16)
        target[here, depth : 2 * depth] = source[8 + r : 8 + r + step, :].astype(BF16)
        target[here, 2 * depth : 3 * depth] = later.astype(BF16)


def encoder_kernel(
    me_ref, f0, f1, f2, f3, w0, w1, w2a, w2b, w3a, w3b, prev_ok, next_ok,
    slope_ref, mid_ref, latent_ref, feat, weight, act, act3,
):
    me = me_ref[0]
    rows, depth = slope_ref.shape
    assemble(me, feat, (f0, f1, f2, f3))
    assemble_halves(me, me_ref[1], weight, w0, w1, (w2a, w2b, w3a, w3b))
    step = rows // 3
    for r in range(0, rows, step):
        act[8 + r : 8 + r + step, :] = (
            elu(feat[r : r + step, :].astype(F32)).astype(BF16).astype(F32)
        )
    act[0:8, :] = jnp.zeros((8, depth), F32)
    act[8 + rows : 16 + rows, :] = jnp.zeros((8, depth), F32)
    taps_into(act, act3, prev_ok, next_ok, rows, depth)
    biases = weight[4 * depth : 4 * depth + 16, :].astype(F32)
    for r in range(0, rows, step):
        here = slice(r, r + step)
        hidden = dot_nn(act3[here, :], weight[0 : 3 * depth, :]) + biases[0:1, :]
        slope_ref[here, :] = elu_slope(hidden).astype(BF16)
        mid = elu(hidden).astype(BF16)
        mid_ref[here, :] = mid
        latent = (
            feat[here, :].astype(F32)
            + dot_nn(mid, weight[3 * depth : 4 * depth, :])
            + biases[1:2, :]
        )
        latent_ref[here, :] = latent.astype(BF16)


def quantize_kernel(latent_ref, books, norms, quant_ref, usage_ref, prob_ref, second_ref, *, own):
    groups, levels, _, depth = books.shape
    rows = latent_ref.shape[0]
    place = pl.program_id(0) * rows + lax.broadcasted_iota(jnp.int32, (rows, 1), 0)
    mine = jnp.where((place >= HALO) & (place < HALO + own), 1.0, 0.0).astype(F32)

    @pl.when(pl.program_id(0) == 0)
    def _():
        usage_ref[...] = jnp.zeros_like(usage_ref)

    current = [latent_ref[:, g * depth : (g + 1) * depth] for g in range(groups)]
    remain = [c.astype(F32) for c in current]
    summed = [None] * groups
    for level in range(levels):
        for g in range(groups):
            book = books[g, level]
            scores = dot_nt(current[g], book) * (2.0 * LOG2E / SOFTMAX_WARMTH) - norms[g, level]
            terms = jnp.exp2(scores - jnp.max(scores, axis=1, keepdims=True))
            prob = terms * (1.0 / jnp.sum(terms, axis=1, keepdims=True))
            low = prob.astype(BF16)
            prob_ref[g, level] = low
            usage_ref[g, level] += jnp.sum(prob * mine, axis=0, keepdims=True)
            picked = dot_nn(low, book)
            summed[g] = picked if summed[g] is None else summed[g] + picked
            if level + 1 < levels:
                remain[g] = remain[g] - picked
                current[g] = remain[g].astype(BF16)
                second_ref[level, :, g * depth : (g + 1) * depth] = current[g]
    for g in range(groups):
        quant_ref[:, g * depth : (g + 1) * depth] = summed[g].astype(BF16)


def weight_grads(where_ref, near, targets, grad, deep, grad1, deep1, own, depth):
    here = slice(HALO, HALO + own)
    lane = lax.broadcasted_iota(jnp.int32, (own, LANES), 1)
    ones3 = jnp.where(lane == 0, 1.0, 0.0).astype(BF16)
    ones1 = jnp.where(lane == 1, 1.0, 0.0).astype(BF16)
    size = LANES // near

    def ordered(values):
        return jnp.concatenate(
            [values[here, columns_of(where_ref[0], k)] for k in range(len(targets))], 1
        )

    def put(first, values):
        count = values.shape[1]
        for k, target in enumerate(targets):
            for j in range(near):
                start = pl.multiple_of((where_ref[1] ^ j) * size, size)
                row = k * LANES + j * size
                target[pl.ds(start, size), first : first + count] = values[
                    row : row + size, :
                ].astype(target.dtype)

    left, left1 = ordered(grad), ordered(grad1)
    for first in range(0, 3 * depth, depth):
        put(first, dot_tn(left, deep[here, first : first + depth]))
    put(3 * depth, dot_tn(left1, deep1[here, :]))
    put(4 * depth, dot_tn(left, ones3) + dot_tn(left1, ones1))


def input_grad(taps, weight, here, depth):
    return (
        dot_nt(taps[here, 2 * depth : 3 * depth], weight[0:depth, :])
        + dot_nt(taps[here, depth : 2 * depth], weight[depth : 2 * depth, :])
        + dot_nt(taps[here, 0:depth], weight[2 * depth : 3 * depth, :])
    )


def decoder_kernel(
    me_ref, quant, c0, c1, c2, c3, w0, w1, w2, w3, prev_ok, next_ok,
    grad_ref, g0, g2, sent, cot, weight, act, act3, low, mid, *, near,
):
    me = me_ref[0]
    rows, depth = quant.shape
    own = rows - 2 * HALO
    assemble(me, cot, (c0, c1, c2, c3))
    assemble(me, weight, (w0, w1, w2, w3))
    step = rows // 3
    for r in range(0, rows, step):
        act[8 + r : 8 + r + step, :] = (
            elu(quant[r : r + step, :].astype(F32)).astype(BF16).astype(F32)
        )
    act[0:8, :] = jnp.zeros((8, depth), F32)
    act[8 + rows : 16 + rows, :] = jnp.zeros((8, depth), F32)
    taps_into(act, act3, prev_ok, next_ok, rows, depth)
    bias = weight[4 * depth : 4 * depth + 16, :].astype(F32)[0:1, :]
    for r in range(0, rows, step):
        here = slice(r, r + step)
        hidden = dot_nn(act3[here, :], weight[0 : 3 * depth, :]) + bias
        mid[here, :] = elu(hidden).astype(BF16)
        grad = dot_nt(cot[here, :], weight[3 * depth : 4 * depth, :]) * elu_slope(hidden)
        grad = grad.astype(BF16)
        low[here, :] = grad
        act[8 + r : 8 + r + step, :] = grad.astype(F32)
    targets = (g0, sent.at[0], g2, sent.at[1])
    weight_grads(me_ref, near, targets, low, act3, cot, mid, own, depth)
    taps_into(act, act3, prev_ok, next_ok, rows, depth)
    for r in range(0, rows, step):
        here = slice(r, r + step)
        grad_ref[here, :] = (
            cot[here, :].astype(F32)
            + elu_slope(quant[here, :].astype(F32)) * input_grad(act3, weight, here, depth)
        ).astype(BF16)


def quantize_back_kernel(
    where_ref, grad_ref, prob_ref, first_ref, second_ref, books, usage,
    out_ref, table_ref, mark_ref, total, columns, *, own, levels,
):
    step = pl.program_id(0)
    rows = grad_ref.shape[0]
    place = step * rows + lax.broadcasted_iota(jnp.int32, (rows, 1), 0)
    mine = jnp.where((place >= HALO) & (place < HALO + own), 1.0, 0.0).astype(F32)
    mine_low = mine.astype(BF16)
    scale = 2.0 / SOFTMAX_WARMTH

    @pl.when(step == 0)
    def _():
        total[...] = jnp.zeros_like(total)
        columns[...] = jnp.zeros_like(columns)

    grad_remain = None
    for level in reversed(range(levels)):
        book = books[0, level]
        low = prob_ref[0, level]
        current = first_ref[...] if level == 0 else second_ref[level - 1]
        picked = grad_ref[...] if grad_remain is None else grad_ref[...] - grad_remain
        picked = picked.astype(BF16)
        grad_prob = dot_nt(picked, book)
        prob = low.astype(F32)
        inner = jnp.sum(prob * grad_prob, axis=1, keepdims=True)
        grad_scores = (prob * (grad_prob - inner)).astype(BF16)
        through = dot_nn(grad_scores, book) * scale
        grad_remain = through if grad_remain is None else grad_remain + through
        left = jnp.concatenate([picked * mine_low, current * (mine_low * scale)], 0)
        total[level] += dot_tn(left, jnp.concatenate([low, grad_scores], 0))
        columns[level] += jnp.sum(grad_scores.astype(F32) * mine, axis=0, keepdims=True)
    out_ref[...] = grad_remain.astype(BF16)

    @pl.when(step == pl.num_programs(0) - 1)
    def _():
        depth = books.shape[3]
        row = lax.broadcasted_iota(jnp.int32, (16, table_ref.shape[3]), 0)
        for j in range(levels):
            table = table_ref.at[j]
            level = where_ref[4] ^ j
            codes = table.shape[2]
            turned = books[0, level].astype(F32).T
            for k in range(table.shape[0]):
                here = slice(k * codes, k * codes + codes)
                part = where_ref[1] ^ k
                table[part, 0:depth, :] = (
                    total[level, :, here] - scale * columns[level, :, here] * turned[:, here]
                ).astype(BF16)
                table[part, depth : depth + 16, :] = jnp.where(
                    row == 0, usage[0, level, :, here], 0.0
                ).astype(BF16)
        mark_ref[...] = jnp.zeros_like(mark_ref)


def encoder_weight_grad_kernel(
    me_ref, grad_mine, grad_other, slope, mid, f0, f1, f2, f3,
    w0, w1, w2a, w2b, w3a, w3b, prev_ok, next_ok,
    g0, g2, sent, low, grad_latent, mark, feat, weight, act, act3, *, near,
):
    mark[...] = jnp.zeros_like(mark)
    me = me_ref[0]
    rows, depth = slope.shape
    own = rows - 2 * HALO
    half = grad_mine.shape[1]
    side = me_ref[2]
    grad_latent[:, pl.ds(pl.multiple_of(side * half, half), half)] = grad_mine[...]
    grad_latent[:, pl.ds(pl.multiple_of((1 - side) * half, half), half)] = grad_other[...]
    assemble(me, feat, (f0, f1, f2, f3))
    assemble_halves(me, me_ref[1], weight, w0, w1, (w2a, w2b, w3a, w3b))
    step = rows // 3
    for r in range(0, rows, step):
        act[8 + r : 8 + r + step, :] = (
            elu(feat[r : r + step, :].astype(F32)).astype(BF16).astype(F32)
        )
    act[0:8, :] = jnp.zeros((8, depth), F32)
    act[8 + rows : 16 + rows, :] = jnp.zeros((8, depth), F32)
    taps_into(act, act3, prev_ok, next_ok, rows, depth)
    for r in range(0, rows, step):
        here = slice(r, r + step)
        grad = dot_nt(grad_latent[here, :], weight[3 * depth : 4 * depth, :])
        low[here, :] = (grad * slope[here, :].astype(F32)).astype(BF16)
    targets = (g0, sent.at[0], g2, sent.at[1])
    weight_grads(me_ref, near, targets, low, act3, grad_latent, mid, own, depth)


def encoder_input_grad_kernel(
    me_ref, low, grad_latent, f0, f1, f2, f3, w0, w1, w2a, w2b, w3a, w3b, prev_ok, next_ok,
    o0, o1, o2, o3, mark, feat, weight, act, act3,
):
    mark[...] = jnp.zeros_like(mark)
    me = me_ref[0]
    rows, depth = low.shape
    own = rows - 2 * HALO
    assemble(me, feat, (f0, f1, f2, f3))
    assemble_halves(me, me_ref[1], weight, w0, w1, (w2a, w2b, w3a, w3b))
    act[8 : 8 + rows, :] = low[...].astype(F32)
    act[0:8, :] = jnp.zeros((8, depth), F32)
    act[8 + rows : 16 + rows, :] = jnp.zeros((8, depth), F32)
    taps_into(act, act3, prev_ok, next_ok, rows, depth)
    for r in range(HALO, HALO + own, own // 4):
        here = slice(r, r + own // 4)
        feat[here, :] = (
            grad_latent[here, :].astype(F32)
            + elu_slope(feat[here, :].astype(F32)) * input_grad(act3, weight, here, depth)
        ).astype(BF16)
    for k, out in enumerate((o0, o1, o2, o3)):
        out[...] = feat[HALO : HALO + own, columns_of(me, k)]


def place_kernel(mask_ref, *refs, block):
    out, first = refs[-1], 0
    for ref in refs[:-1]:
        for r in range(0, ref.shape[0], block):
            start = pl.multiple_of((first + r) ^ mask_ref[0], block)
            out[pl.ds(start, block), :] = ref[r : r + block, :].astype(F32)
        first += ref.shape[0]


def sum_of(*refs):
    return functools.reduce(lambda x, y: x + y, [ref[...].astype(F32) for ref in refs])


def halve_kernel(where_ref, d0, d1, dx, t0, t1, mine, sent, book_sent, mark):
    half = mine.shape[0]
    total = sum_of(d0, d1.at[0], dx)
    mine[...] = total[:half]
    sent[...] = total[half:].astype(BF16)
    book_sent[...] = sum_of(t0.at[1], t1.at[1]).astype(BF16)
    mark[...] = jnp.zeros_like(mark)


def near_kernel(
    where_ref, t0, t1, bx, d0, d1, core, book_mine, book_sent, dec_mine, dec_sent, passed
):
    passed[...] = core[...]
    for k, out in enumerate((book_mine, book_sent)):
        out[...] = sum_of(t0.at[0, k], t1.at[0, k], bx.at[k]).astype(out.dtype)
    total = sum_of(d0, d1)
    dec_mine[...] = total
    dec_sent[...] = total.astype(BF16)


def spread_kernel(
    where_ref, b0, b1, e0, e2, core, d0, d1,
    book_mine, book_sent, enc_mine, enc_near, enc_x, enc_both, dec_mine, dec_sent, mark,
):
    half = enc_mine.shape[0]
    total = sum_of(e0, core.at[0])
    enc_mine[...] = total[:half]
    enc_near[...] = total[half:].astype(BF16)
    total = sum_of(e2, core.at[1])
    enc_x[...] = total[:half].astype(BF16)
    enc_both[...] = total[half:].astype(BF16)
    for mine, sent, total in (
        (book_mine, book_sent, sum_of(b0, b1)),
        (dec_mine, dec_sent, sum_of(d0, d1)),
    ):
        mine[...] = total
        sent[...] = total.astype(BF16)
    mark[...] = jnp.zeros_like(mark)


def sum_kernel(where_ref, b0, b1, e0, e1, e2, e3, book_mine, book_sent, enc_mine, enc_sent):
    for mine, sent, total in (
        (book_mine, book_sent, sum_of(b0, b1)),
        (enc_mine, enc_sent, sum_of(e0, e1, e2, e3)),
    ):
        mine[...] = total
        sent[...] = total.astype(BF16)


def refresh_kernel(
    where_ref, b0, b1, books, chosen, e0, e1, d0, d1, fresh, enc_mine, enc_sent, dec_sent, *, share
):
    held = sum_of(b0, b1)
    depth = books.shape[0]
    ratio = held[depth : depth + 1, :] * share
    refresh = jax.nn.sigmoid(SHARPNESS * (THRESHOLD - ratio))
    stepped = books[...] - (STEP_SCALE * share) * held[:depth, :]
    fresh[...] = ((1.0 - refresh) * stepped + refresh * chosen[...]).T.astype(BF16)
    total = sum_of(e0, e1)
    enc_mine[...] = total
    enc_sent[...] = total.astype(BF16)
    dec_sent[...] = sum_of(d0, d1).astype(BF16)


def join_kernel(where_ref, e0, e1, enc):
    enc[...] = sum_of(e0, e1).astype(BF16)


def unpack_kernel(mask_ref, *refs, block):
    *parts, conv3, conv1, bias3, bias1, held = refs
    first = 0
    for part in parts:
        for r in range(0, part.shape[0], block):
            start = pl.multiple_of((first + r) ^ mask_ref[0], block)
            held[pl.ds(start, block), :] = part[r : r + block, :].astype(F32)
        first += part.shape[0]
    count3, count1 = conv3.shape[0], conv1.shape[0]
    conv3[...] = held[:, 0:count3].T
    conv1[...] = held[:, count3 : count3 + count1].T
    biases = held[:, count3 + count1 :].T
    bias3[...] = biases[0:1, :]
    bias1[...] = biases[1:2, :]


def whole(count, smem_first=False):
    specs = [pl.BlockSpec(memory_space=pltpu.VMEM)] * count
    if smem_first:
        specs[0] = pl.BlockSpec(memory_space=pltpu.SMEM)
    return specs


def cost(flops, moved):
    return pl.CostEstimate(flops=int(flops), bytes_accessed=int(moved), transcendentals=0)


def shaped(shape, dtype):
    return jax.ShapeDtypeStruct(shape, dtype)


PARAMS = pltpu.CompilerParams(vmem_limit_bytes=VMEM_LIMIT)
LIGHT = pltpu.CompilerParams(vmem_limit_bytes=14 * 1024 * 1024)


def tied(kernel, first, count):
    def without(*refs):
        kernel(*refs[:first], *refs[first + count :])

    return without


def call(kernel, row, inputs, outs, scratch=(), ties=(), price=None, params=None):
    return pl.pallas_call(
        tied(kernel, 1 + len(inputs), len(ties)),
        out_shape=[shaped(*out) for out in outs],
        in_specs=whole(1 + len(inputs), True) + [pl.BlockSpec(memory_space=pl.ANY)] * len(ties),
        out_specs=whole(len(outs)),
        scratch_shapes=[pltpu.VMEM(*buffer) for buffer in scratch],
        compiler_params=params or LIGHT,
        cost_estimate=price or cost(0, 2e6),
    )(row, *inputs, *ties)


def body(
    features,
    lengths,
    enc_conv3,
    enc_bias3,
    enc_conv1,
    enc_bias1,
    codebooks,
    dec_conv3,
    dec_bias3,
    dec_conv1,
    code_buffer,
    buffer_index,
    out_cotangent,
):
    frames, cols = features.shape
    groups, levels, num_codes, group_dim = codebooks.shape
    width = lax.axis_size("mp")
    n_dp = lax.axis_size("dp")
    me = lax.axis_index("mp")
    place = lax.axis_index("dp")
    own = frames // width
    rows = own + 2 * HALO
    depth = cols * width
    side, level_side = me % 2, me // 2
    near = 2 if n_dp % 2 == 0 else n_dp
    near_at = place % near
    far_bits = [near << i for i in range((n_dp // near).bit_length() - 1)]
    where_row = jnp.stack([me, near_at, side, place // near, level_side])
    quad = near == 2 and n_dp == 8

    def pack(conv3, conv1, biases, half, ties=(), params=None):
        total = conv3.shape[0] * conv3.shape[1] + conv1.shape[0] + 32
        return call(
            functools.partial(pack_kernel, count=len(biases)),
            where_row,
            [conv3.reshape(3 * depth, cols), conv1]
            + [bias.reshape(1, cols) for bias in biases],
            [((total, cols), BF16)] + [((total // 2, cols), BF16)] * half,
            ties=ties,
            params=params,
        )

    def frames_out(values, ties=(), params=None):
        outs = [((rows, cols), BF16)] * 4
        return call(frames_kernel, where_row, [values], outs, ties=ties, params=params)

    enc_own, enc_half = pack(enc_conv3, enc_conv1, [enc_bias3, enc_bias1], 1, params=PARAMS)
    enc_2a = swap(enc_half, "mp", 2)
    feat = list(frames_out(features, [enc_half], PARAMS))
    feat[2], feat[3] = swap(feat[2], "mp", 2), swap(feat[3], "mp", 3)
    feat[1] = swap(feat[1], "mp", 1)
    enc_1 = swap(enc_own, "mp", 1)
    enc_2b = swap(enc_2a, "dp", 1)
    enc_3a = swap(enc_2a, "mp", 1)
    enc_3b = swap(enc_2b, "mp", 1)
    enc = (enc_own, enc_1, enc_2a, enc_2b, enc_3a, enc_3b)

    clip_ends = jnp.cumsum(lengths[0])
    starts = clip_ends - lengths[0]

    def ok_at(shift):
        at = me * own - HALO + shift + jnp.arange(rows, dtype=jnp.int32)
        is_start = jnp.any(at[:, None] == starts[None, :], axis=1) | (at == frames)
        return jnp.where(is_start, 0.0, 1.0).astype(F32)[:, None]

    prev_ok, next_ok = ok_at(0), ok_at(1)
    books_f = codebooks.astype(F32)
    norms = jnp.sum(books_f * books_f, axis=3) * (LOG2E / SOFTMAX_WARMTH)
    norms = norms[:, :, None, :]

    codes = num_codes // near
    first = near_at * codes

    def own_codes(array):
        start = (side, level_side, first) + (jnp.int32(0),) * (array.ndim - 3)
        return lax.dynamic_slice(array, start, (1, 1, codes) + array.shape[3:])[0, 0]

    index = own_codes(buffer_index)
    one_hot = index[:, None] == jnp.arange(code_buffer.shape[0], dtype=jnp.int32)[None, :]
    buffer_half = lax.dynamic_slice_in_dim(code_buffer, side * group_dim, group_dim, 1)
    chosen = dot_nn(one_hot.astype(BF16), buffer_half)
    books_own = own_codes(codebooks).astype(F32)
    if quad:
        chosen, books_own = chosen.T, books_own.T

    at = jnp.arange(cols, dtype=jnp.int32)
    turn = ((at[:, None] ^ (near_at * (cols // near))) == at[None, :]).astype(BF16)
    cot = list(frames_out(out_cotangent, [chosen, books_own, norms, prev_ok, next_ok]))
    (dec_own,) = pack(dec_conv3, dec_conv1, [dec_bias3], 0, [cot[0], feat[1], enc_1])
    dec_1 = swap(dec_own, "mp", 1)
    dec_2 = swap(after(dec_own, feat[2], feat[3]), "mp", 2)

    taken = [((rows, depth), BF16), ((4 * depth + 32, depth), BF16)]
    taken += [((rows + 16, depth), F32), ((rows, 3 * depth), BF16)]
    slope_enc, act_mid, latent = call(
        encoder_kernel,
        where_row,
        [*feat, *enc, prev_ok, next_ok],
        [((rows, depth), BF16)] * 3,
        taken,
        [dec_own],
        cost(8 * rows * depth * depth, 12e6),
        PARAMS,
    )

    dec_3 = swap(after(dec_2, latent), "mp", 1)
    dec = (dec_own, dec_1, dec_2, dec_3)
    cot[2], cot[3], _ = lax.optimization_barrier((cot[2], cot[3], dec_2))
    cot = [cot[0]] + [swap(cot[k], "mp", k) for k in (1, 2, 3)]

    step = rows // 3
    quant, usage, prob, second = pl.pallas_call(
        functools.partial(quantize_kernel, own=own),
        grid=(3,),
        out_shape=(
            shaped((rows, depth), BF16),
            shaped((groups, levels, 1, num_codes), F32),
            shaped((groups, levels, rows, num_codes), BF16),
            shaped((levels - 1, rows, depth), BF16),
        ),
        in_specs=[
            pl.BlockSpec((step, depth), lambda i: (i, 0)),
            pl.BlockSpec(codebooks.shape, lambda i: (0, 0, 0, 0)),
            pl.BlockSpec(norms.shape, lambda i: (0, 0, 0, 0)),
        ],
        out_specs=(
            pl.BlockSpec((step, depth), lambda i: (i, 0)),
            pl.BlockSpec((groups, levels, 1, num_codes), lambda i: (0, 0, 0, 0)),
            pl.BlockSpec((groups, levels, step, num_codes), lambda i: (0, 0, i, 0)),
            pl.BlockSpec((levels - 1, step, depth), lambda i: (0, i, 0)),
        ),
        compiler_params=PARAMS,
        cost_estimate=cost(16 * rows * num_codes * group_dim, 30e6),
    )(latent, codebooks, norms)

    packed = 4 * depth + LANES
    grads_shape = (
        shaped((cols, packed), BF16),
        shaped((cols, packed), BF16),
        shaped((2, cols, packed), BF16),
    )
    grad_quant, *dec_grads = pl.pallas_call(
        functools.partial(decoder_kernel, near=near),
        out_shape=(shaped((rows, depth), BF16),) + grads_shape,
        in_specs=whole(12, True),
        out_specs=tuple(whole(4)),
        scratch_shapes=[
            pltpu.VMEM((rows, depth), BF16),
            pltpu.VMEM((4 * depth + 32, depth), BF16),
            pltpu.VMEM((rows + 16, depth), F32),
            pltpu.VMEM((rows, 3 * depth), BF16),
            pltpu.VMEM((rows, depth), BF16),
            pltpu.VMEM((rows, depth), BF16),
        ],
        compiler_params=PARAMS,
        cost_estimate=cost(24 * rows * depth * depth, 20e6),
    )(where_row, quant, *cot, *dec, prev_ok, next_ok)

    table_shape = (levels, near, group_dim + 16, num_codes // near)

    def quantize_back(flip, *ties):
        return pl.pallas_call(
            tied(functools.partial(quantize_back_kernel, own=own, levels=levels), 7, len(ties)),
            grid_spec=pltpu.PrefetchScalarGridSpec(
                num_scalar_prefetch=1,
                grid=(2,),
                in_specs=[
                    pl.BlockSpec((rows // 2, group_dim), lambda i, g: (i, g[2] ^ flip)),
                    pl.BlockSpec((1, levels, rows // 2, num_codes), lambda i, g: (g[2] ^ flip, 0, i, 0)),
                    pl.BlockSpec((rows // 2, group_dim), lambda i, g: (i, g[2] ^ flip)),
                    pl.BlockSpec((levels - 1, rows // 2, group_dim), lambda i, g: (0, i, g[2] ^ flip)),
                    pl.BlockSpec((1, levels, num_codes, group_dim), lambda i, g: (g[2] ^ flip, 0, 0, 0)),
                    pl.BlockSpec((1, levels, 1, num_codes), lambda i, g: (g[2] ^ flip, 0, 0, 0)),
                ]
                + [pl.BlockSpec(memory_space=pl.ANY)] * len(ties),
                out_specs=(
                    pl.BlockSpec((rows // 2, group_dim), lambda i, g: (i, 0)),
                    pl.BlockSpec(table_shape, lambda i, g: (0, 0, 0, 0)),
                    pl.BlockSpec((8, LANES), lambda i, g: (0, 0)),
                ),
                scratch_shapes=[
                    pltpu.VMEM((levels, group_dim, num_codes), F32),
                    pltpu.VMEM((levels, 1, num_codes), F32),
                ],
            ),
            out_shape=(
                shaped((rows, group_dim), BF16),
                shaped(table_shape, BF16),
                shaped((8, LANES), F32),
            ),
            compiler_params=PARAMS,
            cost_estimate=cost(16 * rows * num_codes * group_dim, 15e6),
        )(
            where_row, grad_quant, prob, latent, second, codebooks, usage, *ties,
        )

    def encoder_weight_grads(*ties):
        return call(
            functools.partial(encoder_weight_grad_kernel, near=near),
            where_row,
            [grad_mine, grad_other, slope_enc, act_mid, *feat, *enc, prev_ok, next_ok],
            [(out.shape, out.dtype) for out in grads_shape]
            + [((rows, depth), BF16)] * 2 + [((8, LANES), F32)],
            taken,
            ties,
            cost(12 * rows * depth * depth, 20e6),
            PARAMS,
        )

    def encoder_input_grads(low, grad_latent, *ties):
        return call(
            encoder_input_grad_kernel,
            where_row,
            [low, grad_latent, *feat, *enc, prev_ok, next_ok],
            [((own, cols), BF16)] * 4 + [((8, LANES), F32)],
            taken,
            ties,
            cost(6 * rows * depth * depth, 10e6),
            PARAMS,
        )

    def put(mask, block, total, pieces, ties=(), params=None):
        return call(
            functools.partial(place_kernel, block=block),
            mask.reshape(1),
            pieces,
            [((total, pieces[0].shape[1]), F32)],
            ties=ties,
            price=cost(0, 8 * total * pieces[0].shape[1]),
            params=params,
        )[0]

    def gather_near(block):
        return jnp.concatenate([block] + [swap(block, "dp", k) for k in range(1, near)], 0)

    def stage(*groups):
        flat = lax.optimization_barrier(tuple(x for group in groups for x in group))
        out = []
        for group in groups:
            out.append(list(flat[: len(group)]))
            flat = flat[len(group) :]
        return out

    grad_other, table_other, mark = quantize_back(1)
    dec_0, dec_2, dec_send = dec_grads
    dec_core = swap(dec_send, "mp", 1)
    dec_send = low_sum(dec_2, dec_core[1]).astype(BF16)
    dec_x = swap(dec_send, "mp", 2)
    table_got = swap(table_other, "mp", 1)
    grad_mine, table_mine, mark = quantize_back(0, mark, dec_send)

    if quad:
        packed_half, table = (cols // 2, packed), table_shape[2:]
        mark_shape = ((8, LANES), F32)
        dec_mine, dec_send, book_send, mark = call(
            halve_kernel,
            where_row,
            [dec_0, dec_core, dec_x, table_mine, table_got],
            [(packed_half, F32), (packed_half, BF16), (table_shape[1:], BF16), mark_shape],
        )
        book_x, dec_got = swap(book_send, "mp", 2), swap(dec_send, "dp", 1)
        enc_0, enc_2, enc_send, low, grad_latent, mark = encoder_weight_grads(mark)
        book_mine, book_send, dec_mine, dec_send, enc_send = call(
            near_kernel,
            where_row,
            [table_mine, table_got, book_x, dec_mine, dec_got, enc_send],
            [(table, F32), (table, BF16), (packed_half, F32), (packed_half, BF16)]
            + [((2, cols, packed), BF16)],
            ties=[mark],
        )
        enc_core = swap(enc_send, "mp", 1)
        book_got, dec_got = swap(book_send, "dp", 1), swap(dec_send, "dp", 2)
        book_mine, book_send, enc_mine, enc_near, enc_x, enc_both, dec_mine, dec_send, mark = call(
            spread_kernel,
            where_row,
            [book_mine, book_got, enc_0, enc_2, enc_core, dec_mine, dec_got],
            [(table, F32), (table, BF16), (packed_half, F32)] + [(packed_half, BF16)] * 3
            + [(packed_half, F32), (packed_half, BF16), mark_shape],
        )
        enc_got = [swap(enc_near, "dp", 1), swap(enc_x, "mp", 2), swap_both(enc_both, 1, 2)]
        book_got, dec_got = swap(book_send, "dp", 2), swap(dec_send, "dp", 4)
        *outs, mark = encoder_input_grads(low, grad_latent, mark)
        book_mine, book_send, enc_mine, enc_send = call(
            sum_kernel,
            where_row,
            [book_mine, book_got, enc_mine, *enc_got],
            [(table, F32), (table, BF16), (packed_half, F32), (packed_half, BF16)],
            ties=[mark],
        )
        book_got, enc_got = swap(book_send, "dp", 4), swap(enc_send, "dp", 2)
        outs = [outs[0]] + [swap(outs[k], "mp", k) for k in (1, 2, 3)]
        fresh, enc_mine, enc_send, dec_send = call(
            functools.partial(refresh_kernel, share=num_codes / (frames * n_dp)),
            where_row,
            [book_mine, book_got, books_own, chosen, enc_mine, enc_got, dec_mine, dec_got],
            [((codes, group_dim), BF16), (packed_half, F32)] + [(packed_half, BF16)] * 2,
        )
        dec_got = swap(dec_send, "dp", 1)
        grad_features = put(me * own, own, frames, outs, [enc_send])
        fresh = [fresh, swap(fresh, "dp", 1), swap(fresh, "mp", 2), swap_both(fresh, 1, 2)]
        enc_got = swap(enc_send, "dp", 4)
        (enc_send,) = call(
            join_kernel,
            where_row,
            [enc_mine, enc_got],
            [(packed_half, BF16)],
            ties=[grad_features],
        )
        enc_got = swap(enc_send, "dp", 1)
        fresh = fresh + [swap(piece, "mp", 1) for piece in fresh]
        mask = (side * levels + level_side) * num_codes + first
        new_codebooks = put(mask, codes, groups * levels * num_codes, fresh, params=PARAMS)

        def unpack(mask, *parts):
            conv3, conv1, bias3, bias1 = call(
                functools.partial(unpack_kernel, block=cols // 2),
                mask.reshape(1),
                parts,
                [((3 * depth, cols), F32), ((depth, cols), F32)] + [((1, cols), F32)] * 2,
                [((cols, packed), F32)],
            )
            return (conv3.reshape(3, depth, cols), bias3[0], conv1, bias1[0])

        half = near_at * (cols // 2)
        return (
            grad_features,
            *unpack(half, enc_send, enc_got),
            *unpack(half, dec_send, dec_got),
            new_codebooks.reshape(codebooks.shape),
        )

    book_send = low_sum(table_mine[1], table_got[1]).astype(BF16)
    dec_mine, *dec_send = parts_of(low_sum(dec_0, dec_core[0], dec_x), near)
    dec_send = [piece.astype(BF16) for piece in dec_send]

    (mark,), (book_send,), dec_send = stage([mark], [book_send], dec_send)
    book_x = swap(book_send, "mp", 2)
    dec_got = [swap(piece, "dp", k + 1) for k, piece in enumerate(dec_send)]
    enc_0, enc_2, enc_send, low, grad_latent, mark = encoder_weight_grads(mark)

    def book_sum(k):
        return low_sum(table_mine[0, k], table_got[0, k], book_x[k])

    def pair_sum(held, sent, bit):
        return held + swap(sent, "dp", bit).astype(F32)

    dec_held = low_sum(dec_mine, *dec_got)
    enc_core = swap(enc_send, "mp", 1)
    book_send, (dec_send, _) = stage(
        [book_sum(k).astype(BF16) for k in range(1, near)], [dec_held.astype(BF16), mark]
    )
    book_got = [swap(piece, "dp", k + 1) for k, piece in enumerate(book_send)]
    dec_held = pair_sum(dec_held, dec_send, far_bits[0])
    enc_mine, *enc_near = parts_of(low_sum(enc_0, enc_core[0]), near)
    enc_near = [piece.astype(BF16) for piece in enc_near]
    enc_far = parts_of(low_sum(enc_2, enc_core[1]).astype(BF16), near)
    book_held = low_sum(book_sum(0), *book_got)

    (mark,), enc_near, enc_far, (book_send, dec_send) = stage(
        [mark], enc_near, enc_far, [book_held.astype(BF16), dec_held.astype(BF16)]
    )
    enc_got = [swap(piece, "dp", k + 1) for k, piece in enumerate(enc_near)] + [
        swap_both(piece, k, 2) for k, piece in enumerate(enc_far)
    ]
    book_held = pair_sum(book_held, book_send, far_bits[0])
    dec_held = pair_sum(dec_held, dec_send, far_bits[1])
    for bit in far_bits[2:]:
        dec_held = pair_sum(dec_held, dec_held.astype(BF16), bit)
    *outs, _ = encoder_input_grads(low, grad_latent, mark)

    enc_held = low_sum(enc_mine, *enc_got)
    (book_send, dec_send, enc_send), outs_send = stage(
        [book_held.astype(BF16), dec_held.astype(BF16), enc_held.astype(BF16)], outs[1:]
    )
    book_held = pair_sum(book_held, book_send, far_bits[1])
    enc_held = pair_sum(enc_held, enc_send, far_bits[0])
    outs = [outs[0]] + [swap(piece, "mp", k + 1) for k, piece in enumerate(outs_send)]
    dec_held = gather_near(dec_send)
    for bit in far_bits[2:]:
        book_held = pair_sum(book_held, book_held.astype(BF16), bit)

    share = num_codes / (frames * n_dp)
    book_held = book_held.T
    ratio = book_held[:, group_dim : group_dim + 1] * share
    refresh = jax.nn.sigmoid(SHARPNESS * (THRESHOLD - ratio))
    stepped = books_own - (STEP_SCALE * share) * book_held[:, :group_dim]
    fresh = ((1.0 - refresh) * stepped + refresh * chosen).astype(BF16)

    ((fresh, enc_send),) = stage([fresh, enc_held.astype(BF16)])
    enc_held = pair_sum(enc_held, enc_send, far_bits[1])
    for bit in far_bits[2:]:
        enc_held = pair_sum(enc_held, enc_held.astype(BF16), bit)
    fresh = [
        swap_both(fresh, k, bits) if k or bits else fresh for bits in (0, 2) for k in range(near)
    ]
    enc_held = gather_near(enc_held.astype(BF16))
    fresh = fresh + [swap(part, "mp", 1) for part in fresh]

    mask = (side * levels + level_side) * num_codes + first
    new_codebooks = put(mask, codes, groups * levels * num_codes, fresh)

    def unpack(held):
        biases = dot_tn(held[:, 4 * depth :], turn)
        return (
            dot_tn(held[:, : 3 * depth], turn).reshape(3, depth, cols),
            biases[0],
            dot_tn(held[:, 3 * depth : 4 * depth], turn),
            biases[1],
        )

    grad_features = put(me * own, own, frames, outs)

    return (
        grad_features,
        *unpack(enc_held),
        *unpack(dec_held),
        new_codebooks.reshape(codebooks.shape),
    )


def solution(mesh):
    return jax.shard_map(
        body,
        mesh=mesh,
        in_specs=(
            P("dp", "mp"),
            P("dp", None),
            P(None, None, "mp"),
            P("mp"),
            P(None, "mp"),
            P("mp"),
            P(),
            P(None, None, "mp"),
            P("mp"),
            P(None, "mp"),
            P(),
            P(),
            P("dp", "mp"),
        ),
        out_specs=(
            P("dp", "mp"),
            P(None, None, "mp"),
            P("mp"),
            P(None, "mp"),
            P("mp"),
            P(None, None, "mp"),
            P("mp"),
            P(None, "mp"),
            P("mp"),
            P(),
        ),
        check_vma=False,
    )
```

```python
import functools
import math

import jax
import jax.numpy as jnp
from jax import lax
from jax.experimental import pallas as pl
from jax.experimental.pallas import tpu as pltpu
from jax.sharding import PartitionSpec as P

SOFTMAX_WARMTH = 8.0
THRESHOLD = 0.7
SHARPNESS = 4.0
STEP_SCALE = 0.5
HALO = 16
LANES = 128
LOG2E = math.log2(math.e)
BF16 = jnp.bfloat16
F32 = jnp.float32
VMEM_LIMIT = 44 * 1024 * 1024


def dot_nn(left, right):
    return jnp.dot(left, right, preferred_element_type=F32)


def dot_nt(left, right):
    return lax.dot_general(left, right, (((1,), (1,)), ((), ())), preferred_element_type=F32)


def dot_tn(left, right):
    return lax.dot_general(left, right, (((0,), (0,)), ((), ())), preferred_element_type=F32)


def elu(values):
    return jnp.where(values > 0, values, jnp.exp(jnp.minimum(values, 0.0)) - 1.0)


def elu_slope(values):
    return jnp.exp(jnp.minimum(values, 0.0))


def swap(values, axis, bits):
    size = lax.axis_size(axis)
    return lax.ppermute(values, axis, [(i, i ^ bits) for i in range(size)])


def after(values, *others):
    return lax.optimization_barrier((values,) + others)[0]


def parts_of(total, count):
    size = total.shape[0] // count
    return [total[k * size : k * size + size] for k in range(count)]


def swap_both(values, dp_bits, mp_bits):
    mp = lax.axis_size("mp")
    count = lax.axis_size("dp") * mp
    pairs = [(i, i ^ (dp_bits * mp + mp_bits)) for i in range(count)]
    return lax.ppermute(values, ("dp", "mp"), pairs)


def low_sum(*terms):
    return functools.reduce(lambda x, y: x + y, [t.astype(F32) for t in terms])


def columns_of(me, k):
    return pl.ds(pl.multiple_of((me ^ k) * LANES, LANES), LANES)


def assemble(me, target, pieces):
    for k, piece in enumerate(pieces):
        target[:, columns_of(me, k)] = piece[...]


def assemble_halves(me, side, target, own, across, halves):
    target[:, columns_of(me, 0)] = own[...]
    target[:, columns_of(me, 1)] = across[...]
    for k in (2, 3):
        for j in range(2):
            piece = halves[2 * (k - 2) + j]
            rows = piece.shape[0]
            start = pl.multiple_of((side ^ j) * rows, 16)
            target[pl.ds(start, rows), columns_of(me, k)] = piece[...]


def frames_kernel(values, *outs):
    own, me = outs[0].shape[0] - 2 * HALO, lax.axis_index("mp")
    for k, out in enumerate(outs):
        start = pl.multiple_of((me ^ k) * own, own)
        above = pl.multiple_of(jnp.maximum(start - HALO, 0), HALO)
        below = pl.multiple_of(jnp.minimum(start + own, values.shape[0] - HALO), HALO)
        out[0:HALO, :] = values[pl.ds(above, HALO), :]
        out[HALO : HALO + own, :] = values[pl.ds(start, own), :]
        out[HALO + own : 2 * HALO + own, :] = values[pl.ds(below, HALO), :]


def pack_kernel(conv3, conv1, *refs, count, near):
    biases, weight = refs[:count], refs[count]
    first, second = conv3.shape[0], conv3.shape[0] + conv1.shape[0]
    weight[0:first, :] = conv3[...]
    weight[first:second, :] = conv1[...]
    row = lax.broadcasted_iota(jnp.int32, (32, LANES), 0)
    rows = jnp.zeros((32, LANES), F32)
    for i, bias in enumerate(biases):
        rows = jnp.where(row == i, bias[...].astype(F32), rows)
    weight[second : second + 32, :] = rows.astype(BF16)
    for half in refs[count + 1 :]:
        size = half.shape[0]
        side = lax.axis_index("dp") % near
        half[...] = weight[pl.ds(pl.multiple_of(side * size, 16), size), :]


def taps_into(source, target, first_ok, last_ok, rows, depth):
    step = rows // 3
    for r in range(0, rows, step):
        here = slice(r, r + step)
        before = source[7 + r : 7 + r + step, :] * first_ok[here, :]
        later = source[9 + r : 9 + r + step, :] * last_ok[here, :]
        target[here, 0:depth] = before.astype(BF16)
        target[here, depth : 2 * depth] = source[8 + r : 8 + r + step, :].astype(BF16)
        target[here, 2 * depth : 3 * depth] = later.astype(BF16)


def encoder_kernel(
    me_ref, f0, f1, f2, f3, w0, w1, w2a, w2b, w3a, w3b, prev_ok, next_ok,
    slope_ref, mid_ref, latent_ref, feat, weight, act, act3,
):
    me = me_ref[0]
    rows, depth = slope_ref.shape
    assemble(me, feat, (f0, f1, f2, f3))
    assemble_halves(me, me_ref[1], weight, w0, w1, (w2a, w2b, w3a, w3b))
    step = rows // 3
    for r in range(0, rows, step):
        act[8 + r : 8 + r + step, :] = (
            elu(feat[r : r + step, :].astype(F32)).astype(BF16).astype(F32)
        )
    act[0:8, :] = jnp.zeros((8, depth), F32)
    act[8 + rows : 16 + rows, :] = jnp.zeros((8, depth), F32)
    taps_into(act, act3, prev_ok, next_ok, rows, depth)
    biases = weight[4 * depth : 4 * depth + 16, :].astype(F32)
    for r in range(0, rows, step):
        here = slice(r, r + step)
        hidden = dot_nn(act3[here, :], weight[0 : 3 * depth, :]) + biases[0:1, :]
        slope_ref[here, :] = elu_slope(hidden).astype(BF16)
        mid = elu(hidden).astype(BF16)
        mid_ref[here, :] = mid
        latent = (
            feat[here, :].astype(F32)
            + dot_nn(mid, weight[3 * depth : 4 * depth, :])
            + biases[1:2, :]
        )
        latent_ref[here, :] = latent.astype(BF16)


def quantize_kernel(latent_ref, books, norms, quant_ref, usage_ref, prob_ref, second_ref, *, own):
    groups, levels, _, depth = books.shape
    rows = latent_ref.shape[0]
    place = pl.program_id(0) * rows + lax.broadcasted_iota(jnp.int32, (rows, 1), 0)
    mine = jnp.where((place >= HALO) & (place < HALO + own), 1.0, 0.0).astype(F32)

    @pl.when(pl.program_id(0) == 0)
    def _():
        usage_ref[...] = jnp.zeros_like(usage_ref)

    current = [latent_ref[:, g * depth : (g + 1) * depth] for g in range(groups)]
    remain = [c.astype(F32) for c in current]
    summed = [None] * groups
    for level in range(levels):
        for g in range(groups):
            book = books[g, level]
            scores = dot_nt(current[g], book) * (2.0 * LOG2E / SOFTMAX_WARMTH) - norms[g, level]
            terms = jnp.exp2(scores - jnp.max(scores, axis=1, keepdims=True))
            prob = terms * (1.0 / jnp.sum(terms, axis=1, keepdims=True))
            low = prob.astype(BF16)
            prob_ref[g, level] = low
            usage_ref[g, level] += jnp.sum(prob * mine, axis=0, keepdims=True)
            picked = dot_nn(low, book)
            summed[g] = picked if summed[g] is None else summed[g] + picked
            if level + 1 < levels:
                remain[g] = remain[g] - picked
                current[g] = remain[g].astype(BF16)
                second_ref[level, :, g * depth : (g + 1) * depth] = current[g]
    for g in range(groups):
        quant_ref[:, g * depth : (g + 1) * depth] = summed[g].astype(BF16)


def weight_grads(where_ref, near, targets, grad, deep, grad1, deep1, own, depth):
    here = slice(HALO, HALO + own)
    lane = lax.broadcasted_iota(jnp.int32, (own, LANES), 1)
    ones3 = jnp.where(lane == 0, 1.0, 0.0).astype(BF16)
    ones1 = jnp.where(lane == 1, 1.0, 0.0).astype(BF16)
    size = LANES // near

    def ordered(values):
        return jnp.concatenate(
            [values[here, columns_of(where_ref[0], k)] for k in range(len(targets))], 1
        )

    def put(first, values):
        count = values.shape[1]
        for k, target in enumerate(targets):
            for j in range(near):
                start = pl.multiple_of((where_ref[1] ^ j) * size, size)
                row = k * LANES + j * size
                target[pl.ds(start, size), first : first + count] = values[
                    row : row + size, :
                ].astype(target.dtype)

    left, left1 = ordered(grad), ordered(grad1)
    for first in range(0, 3 * depth, depth):
        put(first, dot_tn(left, deep[here, first : first + depth]))
    put(3 * depth, dot_tn(left1, deep1[here, :]))
    put(4 * depth, dot_tn(left, ones3) + dot_tn(left1, ones1))


def input_grad(taps, weight, here, depth):
    return (
        dot_nt(taps[here, 2 * depth : 3 * depth], weight[0:depth, :])
        + dot_nt(taps[here, depth : 2 * depth], weight[depth : 2 * depth, :])
        + dot_nt(taps[here, 0:depth], weight[2 * depth : 3 * depth, :])
    )


def decoder_kernel(
    me_ref, quant, c0, c1, c2, c3, w0, w1, w2, w3, prev_ok, next_ok,
    grad_ref, g0, g2, sent, cot, weight, act, act3, low, mid, *, near,
):
    me = me_ref[0]
    rows, depth = quant.shape
    own = rows - 2 * HALO
    assemble(me, cot, (c0, c1, c2, c3))
    assemble(me, weight, (w0, w1, w2, w3))
    step = rows // 3
    for r in range(0, rows, step):
        act[8 + r : 8 + r + step, :] = (
            elu(quant[r : r + step, :].astype(F32)).astype(BF16).astype(F32)
        )
    act[0:8, :] = jnp.zeros((8, depth), F32)
    act[8 + rows : 16 + rows, :] = jnp.zeros((8, depth), F32)
    taps_into(act, act3, prev_ok, next_ok, rows, depth)
    bias = weight[4 * depth : 4 * depth + 16, :].astype(F32)[0:1, :]
    for r in range(0, rows, step):
        here = slice(r, r + step)
        hidden = dot_nn(act3[here, :], weight[0 : 3 * depth, :]) + bias
        mid[here, :] = elu(hidden).astype(BF16)
        grad = dot_nt(cot[here, :], weight[3 * depth : 4 * depth, :]) * elu_slope(hidden)
        grad = grad.astype(BF16)
        low[here, :] = grad
        act[8 + r : 8 + r + step, :] = grad.astype(F32)
    targets = (g0, sent.at[0], g2, sent.at[1])
    weight_grads(me_ref, near, targets, low, act3, cot, mid, own, depth)
    taps_into(act, act3, prev_ok, next_ok, rows, depth)
    for r in range(0, rows, step):
        here = slice(r, r + step)
        grad_ref[here, :] = (
            cot[here, :].astype(F32)
            + elu_slope(quant[here, :].astype(F32)) * input_grad(act3, weight, here, depth)
        ).astype(BF16)


def quantize_back_kernel(
    where_ref, grad_ref, prob_ref, first_ref, second_ref, books, usage,
    out_ref, table_ref, mark_ref, total, columns, *, own, levels,
):
    step = pl.program_id(0)
    rows = grad_ref.shape[0]
    place = step * rows + lax.broadcasted_iota(jnp.int32, (rows, 1), 0)
    mine = jnp.where((place >= HALO) & (place < HALO + own), 1.0, 0.0).astype(F32)
    mine_low = mine.astype(BF16)
    scale = 2.0 / SOFTMAX_WARMTH

    @pl.when(step == 0)
    def _():
        total[...] = jnp.zeros_like(total)
        columns[...] = jnp.zeros_like(columns)

    grad_remain = None
    for level in reversed(range(levels)):
        book = books[0, level]
        low = prob_ref[0, level]
        current = first_ref[...] if level == 0 else second_ref[level - 1]
        picked = grad_ref[...] if grad_remain is None else grad_ref[...] - grad_remain
        picked = picked.astype(BF16)
        grad_prob = dot_nt(picked, book)
        prob = low.astype(F32)
        inner = jnp.sum(prob * grad_prob, axis=1, keepdims=True)
        grad_scores = (prob * (grad_prob - inner)).astype(BF16)
        through = dot_nn(grad_scores, book) * scale
        grad_remain = through if grad_remain is None else grad_remain + through
        left = jnp.concatenate([picked * mine_low, current * (mine_low * scale)], 0)
        total[level] += dot_tn(left, jnp.concatenate([low, grad_scores], 0))
        columns[level] += jnp.sum(grad_scores.astype(F32) * mine, axis=0, keepdims=True)
    out_ref[...] = grad_remain.astype(BF16)

    @pl.when(step == pl.num_programs(0) - 1)
    def _():
        depth = books.shape[3]
        row = lax.broadcasted_iota(jnp.int32, (16, table_ref.shape[3]), 0)
        for j in range(levels):
            table = table_ref.at[j]
            level = where_ref[4] ^ j
            codes = table.shape[2]
            turned = books[0, level].astype(F32).T
            for k in range(table.shape[0]):
                here = slice(k * codes, k * codes + codes)
                part = where_ref[1] ^ k
                table[part, 0:depth, :] = (
                    total[level, :, here] - scale * columns[level, :, here] * turned[:, here]
                ).astype(BF16)
                table[part, depth : depth + 16, :] = jnp.where(
                    row == 0, usage[0, level, :, here], 0.0
                ).astype(BF16)
        mark_ref[...] = jnp.zeros_like(mark_ref)


def encoder_weight_grad_kernel(
    me_ref, grad_mine, grad_other, slope, mid, f0, f1, f2, f3,
    w0, w1, w2a, w2b, w3a, w3b, prev_ok, next_ok,
    g0, g2, sent, low, grad_latent, mark, feat, weight, act, act3, *, near,
):
    mark[...] = jnp.zeros_like(mark)
    me = me_ref[0]
    rows, depth = slope.shape
    own = rows - 2 * HALO
    half = grad_mine.shape[1]
    side = me_ref[2]
    grad_latent[:, pl.ds(pl.multiple_of(side * half, half), half)] = grad_mine[...]
    grad_latent[:, pl.ds(pl.multiple_of((1 - side) * half, half), half)] = grad_other[...]
    assemble(me, feat, (f0, f1, f2, f3))
    assemble_halves(me, me_ref[1], weight, w0, w1, (w2a, w2b, w3a, w3b))
    step = rows // 3
    for r in range(0, rows, step):
        act[8 + r : 8 + r + step, :] = (
            elu(feat[r : r + step, :].astype(F32)).astype(BF16).astype(F32)
        )
    act[0:8, :] = jnp.zeros((8, depth), F32)
    act[8 + rows : 16 + rows, :] = jnp.zeros((8, depth), F32)
    taps_into(act, act3, prev_ok, next_ok, rows, depth)
    for r in range(0, rows, step):
        here = slice(r, r + step)
        grad = dot_nt(grad_latent[here, :], weight[3 * depth : 4 * depth, :])
        low[here, :] = (grad * slope[here, :].astype(F32)).astype(BF16)
    targets = (g0, sent.at[0], g2, sent.at[1])
    weight_grads(me_ref, near, targets, low, act3, grad_latent, mid, own, depth)


def encoder_input_grad_kernel(
    me_ref, low, grad_latent, f0, f1, f2, f3, w0, w1, w2a, w2b, w3a, w3b, prev_ok, next_ok,
    o0, o1, o2, o3, mark, feat, weight, act, act3,
):
    mark[...] = jnp.zeros_like(mark)
    me = me_ref[0]
    rows, depth = low.shape
    own = rows - 2 * HALO
    assemble(me, feat, (f0, f1, f2, f3))
    assemble_halves(me, me_ref[1], weight, w0, w1, (w2a, w2b, w3a, w3b))
    act[8 : 8 + rows, :] = low[...].astype(F32)
    act[0:8, :] = jnp.zeros((8, depth), F32)
    act[8 + rows : 16 + rows, :] = jnp.zeros((8, depth), F32)
    taps_into(act, act3, prev_ok, next_ok, rows, depth)
    for r in range(HALO, HALO + own, own // 4):
        here = slice(r, r + own // 4)
        feat[here, :] = (
            grad_latent[here, :].astype(F32)
            + elu_slope(feat[here, :].astype(F32)) * input_grad(act3, weight, here, depth)
        ).astype(BF16)
    for k, out in enumerate((o0, o1, o2, o3)):
        out[...] = feat[HALO : HALO + own, columns_of(me, k)]


def place_kernel(mask_ref, *refs, block):
    out, first = refs[-1], 0
    for ref in refs[:-1]:
        for r in range(0, ref.shape[0], block):
            start = pl.multiple_of((first + r) ^ mask_ref[0], block)
            out[pl.ds(start, block), :] = ref[r : r + block, :].astype(F32)
        first += ref.shape[0]


def sum_of(*refs):
    return functools.reduce(lambda x, y: x + y, [ref[...].astype(F32) for ref in refs])


def halve_kernel(where_ref, d0, d1, dx, t0, t1, mine, sent, book_sent, mark):
    half = mine.shape[0]
    total = sum_of(d0, d1.at[0], dx)
    mine[...] = total[:half]
    sent[...] = total[half:].astype(BF16)
    book_sent[...] = sum_of(t0.at[1], t1.at[1]).astype(BF16)
    mark[...] = jnp.zeros_like(mark)


def near_kernel(
    where_ref, t0, t1, bx, d0, d1, core, book_mine, book_sent, dec_mine, dec_sent, passed
):
    passed[...] = core[...]
    for k, out in enumerate((book_mine, book_sent)):
        out[...] = sum_of(t0.at[0, k], t1.at[0, k], bx.at[k]).astype(out.dtype)
    total = sum_of(d0, d1)
    dec_mine[...] = total
    dec_sent[...] = total.astype(BF16)


def spread_kernel(
    where_ref, b0, b1, e0, e2, core, d0, d1,
    book_mine, book_sent, enc_mine, enc_near, enc_x, enc_both, dec_mine, dec_sent, mark,
):
    half = enc_mine.shape[0]
    total = sum_of(e0, core.at[0])
    enc_mine[...] = total[:half]
    enc_near[...] = total[half:].astype(BF16)
    total = sum_of(e2, core.at[1])
    enc_x[...] = total[:half].astype(BF16)
    enc_both[...] = total[half:].astype(BF16)
    for mine, sent, total in (
        (book_mine, book_sent, sum_of(b0, b1)),
        (dec_mine, dec_sent, sum_of(d0, d1)),
    ):
        mine[...] = total
        sent[...] = total.astype(BF16)
    mark[...] = jnp.zeros_like(mark)


def sum_kernel(where_ref, b0, b1, e0, e1, e2, e3, book_mine, book_sent, enc_mine, enc_sent):
    for mine, sent, total in (
        (book_mine, book_sent, sum_of(b0, b1)),
        (enc_mine, enc_sent, sum_of(e0, e1, e2, e3)),
    ):
        mine[...] = total
        sent[...] = total.astype(BF16)


def refresh_kernel(
    where_ref, b0, b1, books, chosen, e0, e1, d0, d1, fresh, enc_mine, enc_sent, dec_sent, *, share
):
    held = sum_of(b0, b1)
    depth = books.shape[0]
    ratio = held[depth : depth + 1, :] * share
    refresh = jax.nn.sigmoid(SHARPNESS * (THRESHOLD - ratio))
    stepped = books[...] - (STEP_SCALE * share) * held[:depth, :]
    fresh[...] = ((1.0 - refresh) * stepped + refresh * chosen[...]).T.astype(BF16)
    total = sum_of(e0, e1)
    enc_mine[...] = total
    enc_sent[...] = total.astype(BF16)
    dec_sent[...] = sum_of(d0, d1).astype(BF16)


def join_kernel(where_ref, e0, e1, enc):
    enc[...] = sum_of(e0, e1).astype(BF16)


def unpack_kernel(mask_ref, *refs, block):
    *parts, conv3, conv1, bias3, bias1, held = refs
    first = 0
    for part in parts:
        for r in range(0, part.shape[0], block):
            start = pl.multiple_of((first + r) ^ mask_ref[0], block)
            held[pl.ds(start, block), :] = part[r : r + block, :].astype(F32)
        first += part.shape[0]
    count3, count1 = conv3.shape[0], conv1.shape[0]
    conv3[...] = held[:, 0:count3].T
    conv1[...] = held[:, count3 : count3 + count1].T
    biases = held[:, count3 + count1 :].T
    bias3[...] = biases[0:1, :]
    bias1[...] = biases[1:2, :]


def whole(count, smem_first=False):
    specs = [pl.BlockSpec(memory_space=pltpu.VMEM)] * count
    if smem_first:
        specs[0] = pl.BlockSpec(memory_space=pltpu.SMEM)
    return specs


def cost(flops, moved):
    return pl.CostEstimate(flops=int(flops), bytes_accessed=int(moved), transcendentals=0)


def shaped(shape, dtype):
    return jax.ShapeDtypeStruct(shape, dtype)


PARAMS = pltpu.CompilerParams(vmem_limit_bytes=VMEM_LIMIT)
LIGHT = pltpu.CompilerParams(vmem_limit_bytes=14 * 1024 * 1024)


def tied(kernel, first, count):
    def without(*refs):
        kernel(*refs[:first], *refs[first + count :])

    return without


def call(kernel, row, inputs, outs, scratch=(), ties=(), price=None, params=None):
    inputs = list(inputs) if row is None else [row, *inputs]
    return pl.pallas_call(
        tied(kernel, len(inputs), len(ties)),
        out_shape=[shaped(*out) for out in outs],
        in_specs=whole(len(inputs), row is not None)
        + [pl.BlockSpec(memory_space=pl.ANY)] * len(ties),
        out_specs=whole(len(outs)),
        scratch_shapes=[pltpu.VMEM(*buffer) for buffer in scratch],
        compiler_params=params or LIGHT,
        cost_estimate=price or cost(0, 2e6),
    )(*inputs, *ties)


def body(
    features,
    lengths,
    enc_conv3,
    enc_bias3,
    enc_conv1,
    enc_bias1,
    codebooks,
    dec_conv3,
    dec_bias3,
    dec_conv1,
    code_buffer,
    buffer_index,
    out_cotangent,
):
    frames, cols = features.shape
    groups, levels, num_codes, group_dim = codebooks.shape
    width = lax.axis_size("mp")
    n_dp = lax.axis_size("dp")
    me = lax.axis_index("mp")
    place = lax.axis_index("dp")
    own = frames // width
    rows = own + 2 * HALO
    depth = cols * width
    side, level_side = me % 2, me // 2
    near = 2 if n_dp % 2 == 0 else n_dp
    near_at = place % near
    far_bits = [near << i for i in range((n_dp // near).bit_length() - 1)]
    where_row = jnp.stack([me, near_at, side, place // near, level_side])
    quad = near == 2 and n_dp == 8

    def pack(conv3, conv1, biases, half, ties=(), params=None):
        total = conv3.shape[0] * conv3.shape[1] + conv1.shape[0] + 32
        return call(
            functools.partial(pack_kernel, count=len(biases), near=near),
            None,
            [conv3.reshape(3 * depth, cols), conv1]
            + [bias.reshape(1, cols) for bias in biases],
            [((total, cols), BF16)] + [((total // 2, cols), BF16)] * half,
            ties=ties,
            params=params,
        )

    def frames_out(values, ties=(), params=None):
        outs = [((rows, cols), BF16)] * 4
        return call(frames_kernel, None, [values], outs, ties=ties, params=params)

    enc_own, enc_half = pack(enc_conv3, enc_conv1, [enc_bias3, enc_bias1], 1, params=PARAMS)
    enc_2a = swap(enc_half, "mp", 2)
    feat = list(frames_out(features, [enc_half], PARAMS))
    feat[2], feat[3] = swap(feat[2], "mp", 2), swap(feat[3], "mp", 3)
    feat[1] = swap(feat[1], "mp", 1)
    enc_1 = swap(enc_own, "mp", 1)
    enc_2b = swap(enc_2a, "dp", 1)
    enc_3a = swap(enc_2a, "mp", 1)
    enc_3b = swap(enc_2b, "mp", 1)
    enc = (enc_own, enc_1, enc_2a, enc_2b, enc_3a, enc_3b)

    clip_ends = jnp.cumsum(lengths[0])
    starts = clip_ends - lengths[0]

    def ok_at(shift):
        at = me * own - HALO + shift + jnp.arange(rows, dtype=jnp.int32)
        is_start = jnp.any(at[:, None] == starts[None, :], axis=1) | (at == frames)
        return jnp.where(is_start, 0.0, 1.0).astype(F32)[:, None]

    prev_ok, next_ok = ok_at(0), ok_at(1)
    books_f = codebooks.astype(F32)
    norms = jnp.sum(books_f * books_f, axis=3) * (LOG2E / SOFTMAX_WARMTH)
    norms = norms[:, :, None, :]

    codes = num_codes // near
    first = near_at * codes

    def own_codes(array):
        start = (side, level_side, first) + (jnp.int32(0),) * (array.ndim - 3)
        return lax.dynamic_slice(array, start, (1, 1, codes) + array.shape[3:])[0, 0]

    index = own_codes(buffer_index)
    one_hot = index[:, None] == jnp.arange(code_buffer.shape[0], dtype=jnp.int32)[None, :]
    buffer_half = lax.dynamic_slice_in_dim(code_buffer, side * group_dim, group_dim, 1)
    chosen = dot_nn(one_hot.astype(BF16), buffer_half)
    books_own = own_codes(codebooks).astype(F32)
    if quad:
        chosen, books_own = chosen.T, books_own.T

    at = jnp.arange(cols, dtype=jnp.int32)
    turn = ((at[:, None] ^ (near_at * (cols // near))) == at[None, :]).astype(BF16)
    cot = list(frames_out(
        out_cotangent, [chosen, books_own, norms, prev_ok, next_ok, where_row]
    ))
    (dec_own,) = pack(dec_conv3, dec_conv1, [dec_bias3], 0, [cot[0], feat[1], enc_1])
    dec_1 = swap(dec_own, "mp", 1)
    dec_2 = swap(after(dec_own, feat[2], feat[3]), "mp", 2)

    taken = [((rows, depth), BF16), ((4 * depth + 32, depth), BF16)]
    taken += [((rows + 16, depth), F32), ((rows, 3 * depth), BF16)]
    slope_enc, act_mid, latent = call(
        encoder_kernel,
        where_row,
        [*feat, *enc, prev_ok, next_ok],
        [((rows, depth), BF16)] * 3,
        taken,
        [dec_own],
        cost(8 * rows * depth * depth, 12e6),
        PARAMS,
    )

    dec_3 = swap(after(dec_2, latent), "mp", 1)
    dec = (dec_own, dec_1, dec_2, dec_3)
    cot[2], cot[3], _ = lax.optimization_barrier((cot[2], cot[3], dec_2))
    cot = [cot[0]] + [swap(cot[k], "mp", k) for k in (1, 2, 3)]

    step = rows // 3
    quant, usage, prob, second = pl.pallas_call(
        functools.partial(quantize_kernel, own=own),
        grid=(3,),
        out_shape=(
            shaped((rows, depth), BF16),
            shaped((groups, levels, 1, num_codes), F32),
            shaped((groups, levels, rows, num_codes), BF16),
            shaped((levels - 1, rows, depth), BF16),
        ),
        in_specs=[
            pl.BlockSpec((step, depth), lambda i: (i, 0)),
            pl.BlockSpec(codebooks.shape, lambda i: (0, 0, 0, 0)),
            pl.BlockSpec(norms.shape, lambda i: (0, 0, 0, 0)),
        ],
        out_specs=(
            pl.BlockSpec((step, depth), lambda i: (i, 0)),
            pl.BlockSpec((groups, levels, 1, num_codes), lambda i: (0, 0, 0, 0)),
            pl.BlockSpec((groups, levels, step, num_codes), lambda i: (0, 0, i, 0)),
            pl.BlockSpec((levels - 1, step, depth), lambda i: (0, i, 0)),
        ),
        compiler_params=PARAMS,
        cost_estimate=cost(16 * rows * num_codes * group_dim, 30e6),
    )(latent, codebooks, norms)

    packed = 4 * depth + LANES
    grads_shape = (
        shaped((cols, packed), BF16),
        shaped((cols, packed), BF16),
        shaped((2, cols, packed), BF16),
    )
    grad_quant, *dec_grads = pl.pallas_call(
        functools.partial(decoder_kernel, near=near),
        out_shape=(shaped((rows, depth), BF16),) + grads_shape,
        in_specs=whole(12, True),
        out_specs=tuple(whole(4)),
        scratch_shapes=[
            pltpu.VMEM((rows, depth), BF16),
            pltpu.VMEM((4 * depth + 32, depth), BF16),
            pltpu.VMEM((rows + 16, depth), F32),
            pltpu.VMEM((rows, 3 * depth), BF16),
            pltpu.VMEM((rows, depth), BF16),
            pltpu.VMEM((rows, depth), BF16),
        ],
        compiler_params=PARAMS,
        cost_estimate=cost(24 * rows * depth * depth, 20e6),
    )(where_row, quant, *cot, *dec, prev_ok, next_ok)

    table_shape = (levels, near, group_dim + 16, num_codes // near)

    def quantize_back(flip, *ties):
        return pl.pallas_call(
            tied(functools.partial(quantize_back_kernel, own=own, levels=levels), 7, len(ties)),
            grid_spec=pltpu.PrefetchScalarGridSpec(
                num_scalar_prefetch=1,
                grid=(1,),
                in_specs=[
                    pl.BlockSpec((rows, group_dim), lambda i, g: (i, g[2] ^ flip)),
                    pl.BlockSpec((1, levels, rows, num_codes), lambda i, g: (g[2] ^ flip, 0, i, 0)),
                    pl.BlockSpec((rows, group_dim), lambda i, g: (i, g[2] ^ flip)),
                    pl.BlockSpec((levels - 1, rows, group_dim), lambda i, g: (0, i, g[2] ^ flip)),
                    pl.BlockSpec((1, levels, num_codes, group_dim), lambda i, g: (g[2] ^ flip, 0, 0, 0)),
                    pl.BlockSpec((1, levels, 1, num_codes), lambda i, g: (g[2] ^ flip, 0, 0, 0)),
                ]
                + [pl.BlockSpec(memory_space=pl.ANY)] * len(ties),
                out_specs=(
                    pl.BlockSpec((rows, group_dim), lambda i, g: (i, 0)),
                    pl.BlockSpec(table_shape, lambda i, g: (0, 0, 0, 0)),
                    pl.BlockSpec((8, LANES), lambda i, g: (0, 0)),
                ),
                scratch_shapes=[
                    pltpu.VMEM((levels, group_dim, num_codes), F32),
                    pltpu.VMEM((levels, 1, num_codes), F32),
                ],
            ),
            out_shape=(
                shaped((rows, group_dim), BF16),
                shaped(table_shape, BF16),
                shaped((8, LANES), F32),
            ),
            compiler_params=PARAMS,
            cost_estimate=cost(16 * rows * num_codes * group_dim, 15e6),
        )(
            where_row, grad_quant, prob, latent, second, codebooks, usage, *ties,
        )

    def encoder_weight_grads(*ties):
        return call(
            functools.partial(encoder_weight_grad_kernel, near=near),
            where_row,
            [grad_mine, grad_other, slope_enc, act_mid, *feat, *enc, prev_ok, next_ok],
            [(out.shape, out.dtype) for out in grads_shape]
            + [((rows, depth), BF16)] * 2 + [((8, LANES), F32)],
            taken,
            ties,
            cost(12 * rows * depth * depth, 20e6),
            PARAMS,
        )

    def encoder_input_grads(low, grad_latent, *ties):
        return call(
            encoder_input_grad_kernel,
            where_row,
            [low, grad_latent, *feat, *enc, prev_ok, next_ok],
            [((own, cols), BF16)] * 4 + [((8, LANES), F32)],
            taken,
            ties,
            cost(6 * rows * depth * depth, 10e6),
            PARAMS,
        )

    def put(mask, block, total, pieces, ties=(), params=None):
        return call(
            functools.partial(place_kernel, block=block),
            mask.reshape(1),
            pieces,
            [((total, pieces[0].shape[1]), F32)],
            ties=ties,
            price=cost(0, 8 * total * pieces[0].shape[1]),
            params=params,
        )[0]

    def gather_near(block):
        return jnp.concatenate([block] + [swap(block, "dp", k) for k in range(1, near)], 0)

    def stage(*groups):
        flat = lax.optimization_barrier(tuple(x for group in groups for x in group))
        out = []
        for group in groups:
            out.append(list(flat[: len(group)]))
            flat = flat[len(group) :]
        return out

    grad_other, table_other, mark = quantize_back(1)
    dec_0, dec_2, dec_send = dec_grads
    dec_core = swap(dec_send, "mp", 1)
    dec_send = low_sum(dec_2, dec_core[1]).astype(BF16)
    dec_x = swap(dec_send, "mp", 2)
    table_got = swap(table_other, "mp", 1)
    grad_mine, table_mine, mark = quantize_back(0, mark, dec_send)

    if quad:
        packed_half, table = (cols // 2, packed), table_shape[2:]
        mark_shape = ((8, LANES), F32)
        dec_mine, dec_send, book_send, mark = call(
            halve_kernel,
            where_row,
            [dec_0, dec_core, dec_x, table_mine, table_got],
            [(packed_half, F32), (packed_half, BF16), (table_shape[1:], BF16), mark_shape],
        )
        book_x, dec_got = swap(book_send, "mp", 2), swap(dec_send, "dp", 1)
        enc_0, enc_2, enc_send, low, grad_latent, mark = encoder_weight_grads(mark)
        book_mine, book_send, dec_mine, dec_send, enc_send = call(
            near_kernel,
            where_row,
            [table_mine, table_got, book_x, dec_mine, dec_got, enc_send],
            [(table, F32), (table, BF16), (packed_half, F32), (packed_half, BF16)]
            + [((2, cols, packed), BF16)],
            ties=[mark],
        )
        enc_core = swap(enc_send, "mp", 1)
        book_got, dec_got = swap(book_send, "dp", 1), swap(dec_send, "dp", 2)
        book_mine, book_send, enc_mine, enc_near, enc_x, enc_both, dec_mine, dec_send, mark = call(
            spread_kernel,
            where_row,
            [book_mine, book_got, enc_0, enc_2, enc_core, dec_mine, dec_got],
            [(table, F32), (table, BF16), (packed_half, F32)] + [(packed_half, BF16)] * 3
            + [(packed_half, F32), (packed_half, BF16), mark_shape],
        )
        enc_got = [swap(enc_near, "dp", 1), swap(enc_x, "mp", 2), swap_both(enc_both, 1, 2)]
        book_got, dec_got = swap(book_send, "dp", 2), swap(dec_send, "dp", 4)
        *outs, mark = encoder_input_grads(low, grad_latent, mark)
        book_mine, book_send, enc_mine, enc_send = call(
            sum_kernel,
            where_row,
            [book_mine, book_got, enc_mine, *enc_got],
            [(table, F32), (table, BF16), (packed_half, F32), (packed_half, BF16)],
            ties=[mark],
        )
        book_got, enc_got = swap(book_send, "dp", 4), swap(enc_send, "dp", 2)
        outs = [outs[0]] + [swap(outs[k], "mp", k) for k in (1, 2, 3)]
        fresh, enc_mine, enc_send, dec_send = call(
            functools.partial(refresh_kernel, share=num_codes / (frames * n_dp)),
            where_row,
            [book_mine, book_got, books_own, chosen, enc_mine, enc_got, dec_mine, dec_got],
            [((codes, group_dim), BF16), (packed_half, F32)] + [(packed_half, BF16)] * 2,
        )
        dec_got = swap(dec_send, "dp", 1)
        grad_features = put(me * own, own, frames, outs, [enc_send])
        fresh = [fresh, swap(fresh, "dp", 1), swap(fresh, "mp", 2), swap_both(fresh, 1, 2)]
        enc_got = swap(enc_send, "dp", 4)
        (enc_send,) = call(
            join_kernel,
            where_row,
            [enc_mine, enc_got],
            [(packed_half, BF16)],
            ties=[grad_features],
        )
        enc_got = swap(enc_send, "dp", 1)
        fresh = fresh + [swap(piece, "mp", 1) for piece in fresh]
        mask = (side * levels + level_side) * num_codes + first
        new_codebooks = put(mask, codes, groups * levels * num_codes, fresh, params=PARAMS)

        def unpack(mask, *parts):
            conv3, conv1, bias3, bias1 = call(
                functools.partial(unpack_kernel, block=cols // 2),
                mask.reshape(1),
                parts,
                [((3 * depth, cols), F32), ((depth, cols), F32)] + [((1, cols), F32)] * 2,
                [((cols, packed), F32)],
            )
            return (conv3.reshape(3, depth, cols), bias3[0], conv1, bias1[0])

        half = near_at * (cols // 2)
        return (
            grad_features,
            *unpack(half, enc_send, enc_got),
            *unpack(half, dec_send, dec_got),
            new_codebooks.reshape(codebooks.shape),
        )

    book_send = low_sum(table_mine[1], table_got[1]).astype(BF16)
    dec_mine, *dec_send = parts_of(low_sum(dec_0, dec_core[0], dec_x), near)
    dec_send = [piece.astype(BF16) for piece in dec_send]

    (mark,), (book_send,), dec_send = stage([mark], [book_send], dec_send)
    book_x = swap(book_send, "mp", 2)
    dec_got = [swap(piece, "dp", k + 1) for k, piece in enumerate(dec_send)]
    enc_0, enc_2, enc_send, low, grad_latent, mark = encoder_weight_grads(mark)

    def book_sum(k):
        return low_sum(table_mine[0, k], table_got[0, k], book_x[k])

    def pair_sum(held, sent, bit):
        return held + swap(sent, "dp", bit).astype(F32)

    dec_held = low_sum(dec_mine, *dec_got)
    enc_core = swap(enc_send, "mp", 1)
    book_send, (dec_send, _) = stage(
        [book_sum(k).astype(BF16) for k in range(1, near)], [dec_held.astype(BF16), mark]
    )
    book_got = [swap(piece, "dp", k + 1) for k, piece in enumerate(book_send)]
    dec_held = pair_sum(dec_held, dec_send, far_bits[0])
    enc_mine, *enc_near = parts_of(low_sum(enc_0, enc_core[0]), near)
    enc_near = [piece.astype(BF16) for piece in enc_near]
    enc_far = parts_of(low_sum(enc_2, enc_core[1]).astype(BF16), near)
    book_held = low_sum(book_sum(0), *book_got)

    (mark,), enc_near, enc_far, (book_send, dec_send) = stage(
        [mark], enc_near, enc_far, [book_held.astype(BF16), dec_held.astype(BF16)]
    )
    enc_got = [swap(piece, "dp", k + 1) for k, piece in enumerate(enc_near)] + [
        swap_both(piece, k, 2) for k, piece in enumerate(enc_far)
    ]
    book_held = pair_sum(book_held, book_send, far_bits[0])
    dec_held = pair_sum(dec_held, dec_send, far_bits[1])
    for bit in far_bits[2:]:
        dec_held = pair_sum(dec_held, dec_held.astype(BF16), bit)
    *outs, _ = encoder_input_grads(low, grad_latent, mark)

    enc_held = low_sum(enc_mine, *enc_got)
    (book_send, dec_send, enc_send), outs_send = stage(
        [book_held.astype(BF16), dec_held.astype(BF16), enc_held.astype(BF16)], outs[1:]
    )
    book_held = pair_sum(book_held, book_send, far_bits[1])
    enc_held = pair_sum(enc_held, enc_send, far_bits[0])
    outs = [outs[0]] + [swap(piece, "mp", k + 1) for k, piece in enumerate(outs_send)]
    dec_held = gather_near(dec_send)
    for bit in far_bits[2:]:
        book_held = pair_sum(book_held, book_held.astype(BF16), bit)

    share = num_codes / (frames * n_dp)
    book_held = book_held.T
    ratio = book_held[:, group_dim : group_dim + 1] * share
    refresh = jax.nn.sigmoid(SHARPNESS * (THRESHOLD - ratio))
    stepped = books_own - (STEP_SCALE * share) * book_held[:, :group_dim]
    fresh = ((1.0 - refresh) * stepped + refresh * chosen).astype(BF16)

    ((fresh, enc_send),) = stage([fresh, enc_held.astype(BF16)])
    enc_held = pair_sum(enc_held, enc_send, far_bits[1])
    for bit in far_bits[2:]:
        enc_held = pair_sum(enc_held, enc_held.astype(BF16), bit)
    fresh = [
        swap_both(fresh, k, bits) if k or bits else fresh for bits in (0, 2) for k in range(near)
    ]
    enc_held = gather_near(enc_held.astype(BF16))
    fresh = fresh + [swap(part, "mp", 1) for part in fresh]

    mask = (side * levels + level_side) * num_codes + first
    new_codebooks = put(mask, codes, groups * levels * num_codes, fresh)

    def unpack(held):
        biases = dot_tn(held[:, 4 * depth :], turn)
        return (
            dot_tn(held[:, : 3 * depth], turn).reshape(3, depth, cols),
            biases[0],
            dot_tn(held[:, 3 * depth : 4 * depth], turn),
            biases[1],
        )

    grad_features = put(me * own, own, frames, outs)

    return (
        grad_features,
        *unpack(enc_held),
        *unpack(dec_held),
        new_codebooks.reshape(codebooks.shape),
    )


def solution(mesh):
    return jax.shard_map(
        body,
        mesh=mesh,
        in_specs=(
            P("dp", "mp"),
            P("dp", None),
            P(None, None, "mp"),
            P("mp"),
            P(None, "mp"),
            P("mp"),
            P(),
            P(None, None, "mp"),
            P("mp"),
            P(None, "mp"),
            P(),
            P(),
            P("dp", "mp"),
        ),
        out_specs=(
            P("dp", "mp"),
            P(None, None, "mp"),
            P("mp"),
            P(None, "mp"),
            P("mp"),
            P(None, None, "mp"),
            P("mp"),
            P(None, "mp"),
            P("mp"),
            P(),
        ),
        check_vma=False,
    )
```

```python
import functools
import math

import jax
import jax.numpy as jnp
from jax import lax
from jax.experimental import pallas as pl
from jax.experimental.pallas import tpu as pltpu
from jax.sharding import PartitionSpec as P

SOFTMAX_WARMTH = 8.0
THRESHOLD = 0.7
SHARPNESS = 4.0
STEP_SCALE = 0.5
HALO = 16
LANES = 128
LOG2E = math.log2(math.e)
BF16 = jnp.bfloat16
F32 = jnp.float32
VMEM_LIMIT = 42 * 1024 * 1024


def dot_nn(left, right):
    return jnp.dot(left, right, preferred_element_type=F32)


def dot_nt(left, right):
    return lax.dot_general(left, right, (((1,), (1,)), ((), ())), preferred_element_type=F32)


def dot_tn(left, right):
    return lax.dot_general(left, right, (((0,), (0,)), ((), ())), preferred_element_type=F32)


def elu(values):
    return jnp.where(values > 0, values, jnp.exp(jnp.minimum(values, 0.0)) - 1.0)


def elu_slope(values):
    return jnp.exp(jnp.minimum(values, 0.0))


def swap(values, axis, bits):
    size = lax.axis_size(axis)
    return lax.ppermute(values, axis, [(i, i ^ bits) for i in range(size)])


def after(values, *others):
    return lax.optimization_barrier((values,) + others)[0]


def parts_of(total, count):
    size = total.shape[0] // count
    return [total[k * size : k * size + size] for k in range(count)]


def swap_both(values, dp_bits, mp_bits):
    mp = lax.axis_size("mp")
    count = lax.axis_size("dp") * mp
    pairs = [(i, i ^ (dp_bits * mp + mp_bits)) for i in range(count)]
    return lax.ppermute(values, ("dp", "mp"), pairs)


def low_sum(*terms):
    return functools.reduce(lambda x, y: x + y, [t.astype(F32) for t in terms])


def columns_of(me, k):
    return pl.ds(pl.multiple_of((me ^ k) * LANES, LANES), LANES)


def assemble(me, target, pieces):
    for k, piece in enumerate(pieces):
        target[:, columns_of(me, k)] = piece[...]


def assemble_halves(me, side, target, own, across, halves):
    target[:, columns_of(me, 0)] = own[...]
    target[:, columns_of(me, 1)] = across[...]
    for k in (2, 3):
        for j in range(2):
            piece = halves[2 * (k - 2) + j]
            rows = piece.shape[0]
            start = pl.multiple_of((side ^ j) * rows, 16)
            target[pl.ds(start, rows), columns_of(me, k)] = piece[...]


def frames_kernel(values, *outs):
    own, me = outs[0].shape[0] - 2 * HALO, lax.axis_index("mp")
    for k, out in enumerate(outs):
        start = pl.multiple_of((me ^ k) * own, own)
        above = pl.multiple_of(jnp.maximum(start - HALO, 0), HALO)
        below = pl.multiple_of(jnp.minimum(start + own, values.shape[0] - HALO), HALO)
        out[0:HALO, :] = values[pl.ds(above, HALO), :]
        out[HALO : HALO + own, :] = values[pl.ds(start, own), :]
        out[HALO + own : 2 * HALO + own, :] = values[pl.ds(below, HALO), :]


def pack_kernel(conv3, conv1, *refs, count, near):
    biases, weight = refs[:count], refs[count]
    first, second = conv3.shape[0], conv3.shape[0] + conv1.shape[0]
    weight[0:first, :] = conv3[...]
    weight[first:second, :] = conv1[...]
    row = lax.broadcasted_iota(jnp.int32, (32, LANES), 0)
    rows = jnp.zeros((32, LANES), F32)
    for i, bias in enumerate(biases):
        rows = jnp.where(row == i, bias[...].astype(F32), rows)
    weight[second : second + 32, :] = rows.astype(BF16)
    for half in refs[count + 1 :]:
        size = half.shape[0]
        side = lax.axis_index("dp") % near
        half[...] = weight[pl.ds(pl.multiple_of(side * size, 16), size), :]


def taps_into(source, target, first_ok, last_ok, rows, depth):
    step = rows // 3
    for r in range(0, rows, step):
        here = slice(r, r + step)
        before = source[7 + r : 7 + r + step, :] * first_ok[here, :]
        later = source[9 + r : 9 + r + step, :] * last_ok[here, :]
        target[here, 0:depth] = before.astype(BF16)
        target[here, depth : 2 * depth] = source[8 + r : 8 + r + step, :].astype(BF16)
        target[here, 2 * depth : 3 * depth] = later.astype(BF16)


def encoder_kernel(
    me_ref, f0, f1, f2, f3, w0, w1, w2a, w2b, w3a, w3b, prev_ok, next_ok,
    slope_ref, mid_ref, latent_ref, feat, weight, act, act3,
):
    me = me_ref[0]
    rows, depth = slope_ref.shape
    assemble(me, feat, (f0, f1, f2, f3))
    assemble_halves(me, me_ref[1], weight, w0, w1, (w2a, w2b, w3a, w3b))
    step = rows // 3
    for r in range(0, rows, step):
        act[8 + r : 8 + r + step, :] = (
            elu(feat[r : r + step, :].astype(F32)).astype(BF16).astype(F32)
        )
    act[0:8, :] = jnp.zeros((8, depth), F32)
    act[8 + rows : 16 + rows, :] = jnp.zeros((8, depth), F32)
    taps_into(act, act3, prev_ok, next_ok, rows, depth)
    biases = weight[4 * depth : 4 * depth + 16, :].astype(F32)
    for r in range(0, rows, step):
        here = slice(r, r + step)
        hidden = dot_nn(act3[here, :], weight[0 : 3 * depth, :]) + biases[0:1, :]
        slope_ref[here, :] = elu_slope(hidden).astype(BF16)
        mid = elu(hidden).astype(BF16)
        mid_ref[here, :] = mid
        latent = (
            feat[here, :].astype(F32)
            + dot_nn(mid, weight[3 * depth : 4 * depth, :])
            + biases[1:2, :]
        )
        latent_ref[here, :] = latent.astype(BF16)


def quantize_kernel(latent_ref, books, norms, quant_ref, usage_ref, prob_ref, second_ref, *, own):
    groups, levels, _, depth = books.shape
    rows = latent_ref.shape[0]
    place = pl.program_id(0) * rows + lax.broadcasted_iota(jnp.int32, (rows, 1), 0)
    mine = jnp.where((place >= HALO) & (place < HALO + own), 1.0, 0.0).astype(F32)

    @pl.when(pl.program_id(0) == 0)
    def _():
        usage_ref[...] = jnp.zeros_like(usage_ref)

    current = [latent_ref[:, g * depth : (g + 1) * depth] for g in range(groups)]
    remain = [c.astype(F32) for c in current]
    summed = [None] * groups
    for level in range(levels):
        for g in range(groups):
            book = books[g, level]
            scores = dot_nt(current[g], book) * (2.0 * LOG2E / SOFTMAX_WARMTH) - norms[g, level]
            terms = jnp.exp2(scores - jnp.max(scores, axis=1, keepdims=True))
            prob = terms * (1.0 / jnp.sum(terms, axis=1, keepdims=True))
            low = prob.astype(BF16)
            prob_ref[g, level] = low
            usage_ref[g, level] += jnp.sum(prob * mine, axis=0, keepdims=True)
            picked = dot_nn(low, book)
            summed[g] = picked if summed[g] is None else summed[g] + picked
            if level + 1 < levels:
                remain[g] = remain[g] - picked
                current[g] = remain[g].astype(BF16)
                second_ref[level, :, g * depth : (g + 1) * depth] = current[g]
    for g in range(groups):
        quant_ref[:, g * depth : (g + 1) * depth] = summed[g].astype(BF16)


def weight_grads(where_ref, near, targets, grad, deep, grad1, deep1, own, depth):
    here = slice(HALO, HALO + own)
    lane = lax.broadcasted_iota(jnp.int32, (own, LANES), 1)
    ones3 = jnp.where(lane == 0, 1.0, 0.0).astype(BF16)
    ones1 = jnp.where(lane == 1, 1.0, 0.0).astype(BF16)
    size = LANES // near

    def ordered(values):
        return jnp.concatenate(
            [values[here, columns_of(where_ref[0], k)] for k in range(len(targets))], 1
        )

    def put(first, values):
        count = values.shape[1]
        for k, target in enumerate(targets):
            for j in range(near):
                start = pl.multiple_of((where_ref[1] ^ j) * size, size)
                row = k * LANES + j * size
                target[pl.ds(start, size), first : first + count] = values[
                    row : row + size, :
                ].astype(target.dtype)

    left, left1 = ordered(grad), ordered(grad1)
    for first in range(0, 3 * depth, depth):
        put(first, dot_tn(left, deep[here, first : first + depth]))
    put(3 * depth, dot_tn(left1, deep1[here, :]))
    put(4 * depth, dot_tn(left, ones3) + dot_tn(left1, ones1))


def input_grad(taps, weight, here, depth):
    return (
        dot_nt(taps[here, 2 * depth : 3 * depth], weight[0:depth, :])
        + dot_nt(taps[here, depth : 2 * depth], weight[depth : 2 * depth, :])
        + dot_nt(taps[here, 0:depth], weight[2 * depth : 3 * depth, :])
    )


def decoder_kernel(
    me_ref, quant, c0, c1, c2, c3, w0, w1, w2, w3, prev_ok, next_ok,
    grad_ref, g0, g2, sent, cot, weight, act, act3, low, mid, *, near,
):
    me = me_ref[0]
    rows, depth = quant.shape
    own = rows - 2 * HALO
    assemble(me, cot, (c0, c1, c2, c3))
    assemble(me, weight, (w0, w1, w2, w3))
    step = rows // 3
    for r in range(0, rows, step):
        act[8 + r : 8 + r + step, :] = (
            elu(quant[r : r + step, :].astype(F32)).astype(BF16).astype(F32)
        )
    act[0:8, :] = jnp.zeros((8, depth), F32)
    act[8 + rows : 16 + rows, :] = jnp.zeros((8, depth), F32)
    taps_into(act, act3, prev_ok, next_ok, rows, depth)
    bias = weight[4 * depth : 4 * depth + 16, :].astype(F32)[0:1, :]
    for r in range(0, rows, step):
        here = slice(r, r + step)
        hidden = dot_nn(act3[here, :], weight[0 : 3 * depth, :]) + bias
        mid[here, :] = elu(hidden).astype(BF16)
        grad = dot_nt(cot[here, :], weight[3 * depth : 4 * depth, :]) * elu_slope(hidden)
        grad = grad.astype(BF16)
        low[here, :] = grad
        act[8 + r : 8 + r + step, :] = grad.astype(F32)
    targets = (g0, sent.at[0], g2, sent.at[1])
    weight_grads(me_ref, near, targets, low, act3, cot, mid, own, depth)
    taps_into(act, act3, prev_ok, next_ok, rows, depth)
    for r in range(0, rows, step):
        here = slice(r, r + step)
        grad_ref[here, :] = (
            cot[here, :].astype(F32)
            + elu_slope(quant[here, :].astype(F32)) * input_grad(act3, weight, here, depth)
        ).astype(BF16)


def quantize_back_kernel(
    where_ref, grad_ref, prob_ref, first_ref, second_ref, books, usage,
    out_ref, table_ref, mark_ref, total, columns, *, own, levels,
):
    step = pl.program_id(0)
    rows = grad_ref.shape[0]
    place = step * rows + lax.broadcasted_iota(jnp.int32, (rows, 1), 0)
    mine = jnp.where((place >= HALO) & (place < HALO + own), 1.0, 0.0).astype(F32)
    mine_low = mine.astype(BF16)
    scale = 2.0 / SOFTMAX_WARMTH

    @pl.when(step == 0)
    def _():
        total[...] = jnp.zeros_like(total)
        columns[...] = jnp.zeros_like(columns)

    grad_remain = None
    for level in reversed(range(levels)):
        book = books[0, level]
        low = prob_ref[0, level]
        current = first_ref[...] if level == 0 else second_ref[level - 1]
        picked = grad_ref[...] if grad_remain is None else grad_ref[...] - grad_remain
        picked = picked.astype(BF16)
        grad_prob = dot_nt(picked, book)
        prob = low.astype(F32)
        inner = jnp.sum(prob * grad_prob, axis=1, keepdims=True)
        grad_scores = (prob * (grad_prob - inner)).astype(BF16)
        through = dot_nn(grad_scores, book) * scale
        grad_remain = through if grad_remain is None else grad_remain + through
        left = jnp.concatenate([picked * mine_low, current * (mine_low * scale)], 0)
        total[level] += dot_tn(left, jnp.concatenate([low, grad_scores], 0))
        columns[level] += jnp.sum(grad_scores.astype(F32) * mine, axis=0, keepdims=True)
    out_ref[...] = grad_remain.astype(BF16)

    @pl.when(step == pl.num_programs(0) - 1)
    def _():
        depth = books.shape[3]
        row = lax.broadcasted_iota(jnp.int32, (16, table_ref.shape[3]), 0)
        for j in range(levels):
            table = table_ref.at[j]
            level = where_ref[4] ^ j
            codes = table.shape[2]
            turned = books[0, level].astype(F32).T
            for k in range(table.shape[0]):
                here = slice(k * codes, k * codes + codes)
                part = where_ref[1] ^ k
                table[part, 0:depth, :] = (
                    total[level, :, here] - scale * columns[level, :, here] * turned[:, here]
                ).astype(BF16)
                table[part, depth : depth + 16, :] = jnp.where(
                    row == 0, usage[0, level, :, here], 0.0
                ).astype(BF16)
        mark_ref[...] = jnp.zeros_like(mark_ref)


def encoder_weight_grad_kernel(
    me_ref, grad_mine, grad_other, slope, mid, f0, f1, f2, f3,
    w0, w1, w2a, w2b, w3a, w3b, prev_ok, next_ok,
    g0, g2, sent, low, grad_latent, mark, feat, weight, act, act3, *, near,
):
    mark[...] = jnp.zeros_like(mark)
    me = me_ref[0]
    rows, depth = slope.shape
    own = rows - 2 * HALO
    half = grad_mine.shape[1]
    side = me_ref[2]
    grad_latent[:, pl.ds(pl.multiple_of(side * half, half), half)] = grad_mine[...]
    grad_latent[:, pl.ds(pl.multiple_of((1 - side) * half, half), half)] = grad_other[...]
    assemble(me, feat, (f0, f1, f2, f3))
    assemble_halves(me, me_ref[1], weight, w0, w1, (w2a, w2b, w3a, w3b))
    step = rows // 3
    for r in range(0, rows, step):
        act[8 + r : 8 + r + step, :] = (
            elu(feat[r : r + step, :].astype(F32)).astype(BF16).astype(F32)
        )
    act[0:8, :] = jnp.zeros((8, depth), F32)
    act[8 + rows : 16 + rows, :] = jnp.zeros((8, depth), F32)
    taps_into(act, act3, prev_ok, next_ok, rows, depth)
    for r in range(0, rows, step):
        here = slice(r, r + step)
        grad = dot_nt(grad_latent[here, :], weight[3 * depth : 4 * depth, :])
        low[here, :] = (grad * slope[here, :].astype(F32)).astype(BF16)
    targets = (g0, sent.at[0], g2, sent.at[1])
    weight_grads(me_ref, near, targets, low, act3, grad_latent, mid, own, depth)


def encoder_input_grad_kernel(
    me_ref, low, grad_latent, f0, f1, f2, f3, w0, w1, w2a, w2b, w3a, w3b, prev_ok, next_ok,
    o0, o1, o2, o3, mark, feat, weight, act, act3,
):
    mark[...] = jnp.zeros_like(mark)
    me = me_ref[0]
    rows, depth = low.shape
    own = rows - 2 * HALO
    assemble(me, feat, (f0, f1, f2, f3))
    assemble_halves(me, me_ref[1], weight, w0, w1, (w2a, w2b, w3a, w3b))
    act[8 : 8 + rows, :] = low[...].astype(F32)
    act[0:8, :] = jnp.zeros((8, depth), F32)
    act[8 + rows : 16 + rows, :] = jnp.zeros((8, depth), F32)
    taps_into(act, act3, prev_ok, next_ok, rows, depth)
    for r in range(HALO, HALO + own, own // 4):
        here = slice(r, r + own // 4)
        feat[here, :] = (
            grad_latent[here, :].astype(F32)
            + elu_slope(feat[here, :].astype(F32)) * input_grad(act3, weight, here, depth)
        ).astype(BF16)
    for k, out in enumerate((o0, o1, o2, o3)):
        out[...] = feat[HALO : HALO + own, columns_of(me, k)]


def place_kernel(mask_ref, *refs, block):
    out, first = refs[-1], 0
    for ref in refs[:-1]:
        for r in range(0, ref.shape[0], block):
            start = pl.multiple_of((first + r) ^ mask_ref[0], block)
            out[pl.ds(start, block), :] = ref[r : r + block, :].astype(F32)
        first += ref.shape[0]


def sum_of(*refs):
    return functools.reduce(lambda x, y: x + y, [ref[...].astype(F32) for ref in refs])


def halve_kernel(where_ref, d0, d1, dx, t0, t1, mine, sent, book_sent, mark):
    half = mine.shape[0]
    total = sum_of(d0, d1.at[0], dx)
    mine[...] = total[:half]
    sent[...] = total[half:].astype(BF16)
    book_sent[...] = sum_of(t0.at[1], t1.at[1]).astype(BF16)
    mark[...] = jnp.zeros_like(mark)


def near_kernel(
    where_ref, t0, t1, bx, d0, d1, core, book_mine, book_sent, dec_mine, dec_sent, passed
):
    passed[...] = core[...]
    for k, out in enumerate((book_mine, book_sent)):
        out[...] = sum_of(t0.at[0, k], t1.at[0, k], bx.at[k]).astype(out.dtype)
    total = sum_of(d0, d1)
    dec_mine[...] = total
    dec_sent[...] = total.astype(BF16)


def spread_kernel(
    where_ref, b0, b1, e0, e2, core, d0, d1,
    book_mine, book_sent, enc_mine, enc_near, enc_x, enc_both, dec_mine, dec_sent, mark,
):
    half = enc_mine.shape[0]
    total = sum_of(e0, core.at[0])
    enc_mine[...] = total[:half]
    enc_near[...] = total[half:].astype(BF16)
    total = sum_of(e2, core.at[1])
    enc_x[...] = total[:half].astype(BF16)
    enc_both[...] = total[half:].astype(BF16)
    for mine, sent, total in (
        (book_mine, book_sent, sum_of(b0, b1)),
        (dec_mine, dec_sent, sum_of(d0, d1)),
    ):
        mine[...] = total
        sent[...] = total.astype(BF16)
    mark[...] = jnp.zeros_like(mark)


def sum_kernel(where_ref, b0, b1, e0, e1, e2, e3, book_mine, book_sent, enc_mine, enc_sent):
    for mine, sent, total in (
        (book_mine, book_sent, sum_of(b0, b1)),
        (enc_mine, enc_sent, sum_of(e0, e1, e2, e3)),
    ):
        mine[...] = total
        sent[...] = total.astype(BF16)


def refresh_kernel(
    where_ref, b0, b1, books, chosen, e0, e1, d0, d1, fresh, enc_mine, enc_sent, dec_sent, *, share
):
    held = sum_of(b0, b1)
    depth = books.shape[0]
    ratio = held[depth : depth + 1, :] * share
    refresh = jax.nn.sigmoid(SHARPNESS * (THRESHOLD - ratio))
    stepped = books[...] - (STEP_SCALE * share) * held[:depth, :]
    fresh[...] = ((1.0 - refresh) * stepped + refresh * chosen[...]).T.astype(BF16)
    total = sum_of(e0, e1)
    enc_mine[...] = total
    enc_sent[...] = total.astype(BF16)
    dec_sent[...] = sum_of(d0, d1).astype(BF16)


def join_kernel(where_ref, e0, e1, enc):
    enc[...] = sum_of(e0, e1).astype(BF16)


def unpack_kernel(mask_ref, *refs, block):
    *parts, conv3, conv1, bias3, bias1, held = refs
    first = 0
    for part in parts:
        for r in range(0, part.shape[0], block):
            start = pl.multiple_of((first + r) ^ mask_ref[0], block)
            held[pl.ds(start, block), :] = part[r : r + block, :].astype(F32)
        first += part.shape[0]
    count3, count1 = conv3.shape[0], conv1.shape[0]
    conv3[...] = held[:, 0:count3].T
    conv1[...] = held[:, count3 : count3 + count1].T
    biases = held[:, count3 + count1 :].T
    bias3[...] = biases[0:1, :]
    bias1[...] = biases[1:2, :]


def whole(count, smem_first=False):
    specs = [pl.BlockSpec(memory_space=pltpu.VMEM)] * count
    if smem_first:
        specs[0] = pl.BlockSpec(memory_space=pltpu.SMEM)
    return specs


def cost(flops, moved):
    return pl.CostEstimate(flops=int(flops), bytes_accessed=int(moved), transcendentals=0)


def shaped(shape, dtype):
    return jax.ShapeDtypeStruct(shape, dtype)


PARAMS = pltpu.CompilerParams(vmem_limit_bytes=VMEM_LIMIT)
LARGE = pltpu.CompilerParams(vmem_limit_bytes=58 * 1024 * 1024)
LIGHT = pltpu.CompilerParams(vmem_limit_bytes=14 * 1024 * 1024)


def tied(kernel, first, count):
    def without(*refs):
        kernel(*refs[:first], *refs[first + count :])

    return without


def call(kernel, row, inputs, outs, scratch=(), ties=(), price=None, params=None):
    inputs = list(inputs) if row is None else [row, *inputs]
    return pl.pallas_call(
        tied(kernel, len(inputs), len(ties)),
        out_shape=[shaped(*out) for out in outs],
        in_specs=whole(len(inputs), row is not None)
        + [pl.BlockSpec(memory_space=pl.ANY)] * len(ties),
        out_specs=whole(len(outs)),
        scratch_shapes=[pltpu.VMEM(*buffer) for buffer in scratch],
        compiler_params=params or LIGHT,
        cost_estimate=price or cost(0, 2e6),
    )(*inputs, *ties)


def body(
    features,
    lengths,
    enc_conv3,
    enc_bias3,
    enc_conv1,
    enc_bias1,
    codebooks,
    dec_conv3,
    dec_bias3,
    dec_conv1,
    code_buffer,
    buffer_index,
    out_cotangent,
):
    frames, cols = features.shape
    groups, levels, num_codes, group_dim = codebooks.shape
    width = lax.axis_size("mp")
    n_dp = lax.axis_size("dp")
    me = lax.axis_index("mp")
    place = lax.axis_index("dp")
    own = frames // width
    rows = own + 2 * HALO
    depth = cols * width
    side, level_side = me % 2, me // 2
    near = 2 if n_dp % 2 == 0 else n_dp
    near_at = place % near
    far_bits = [near << i for i in range((n_dp // near).bit_length() - 1)]
    where_row = jnp.stack([me, near_at, side, place // near, level_side])
    quad = near == 2 and n_dp == 8

    def pack(conv3, conv1, biases, half, ties=(), params=None):
        total = conv3.shape[0] * conv3.shape[1] + conv1.shape[0] + 32
        return call(
            functools.partial(pack_kernel, count=len(biases), near=near),
            None,
            [conv3.reshape(3 * depth, cols), conv1]
            + [bias.reshape(1, cols) for bias in biases],
            [((total, cols), BF16)] + [((total // 2, cols), BF16)] * half,
            ties=ties,
            params=params,
        )

    def frames_out(values, ties=(), params=None):
        outs = [((rows, cols), BF16)] * 4
        return call(frames_kernel, None, [values], outs, ties=ties, params=params)

    enc_own, enc_half = pack(enc_conv3, enc_conv1, [enc_bias3, enc_bias1], 1, params=LARGE)
    enc_2a = swap(enc_half, "mp", 2)
    feat = list(frames_out(features, [enc_half], PARAMS))
    feat[2], feat[3] = swap(feat[2], "mp", 2), swap(feat[3], "mp", 3)
    feat[1] = swap(feat[1], "mp", 1)
    enc_1 = swap(enc_own, "mp", 1)
    enc_2b = swap(enc_2a, "dp", 1)
    enc_3a = swap(enc_2a, "mp", 1)
    enc_3b = swap(enc_2b, "mp", 1)
    enc = (enc_own, enc_1, enc_2a, enc_2b, enc_3a, enc_3b)

    clip_ends = jnp.cumsum(lengths[0])
    starts = clip_ends - lengths[0]

    def ok_at(shift):
        at = me * own - HALO + shift + jnp.arange(rows, dtype=jnp.int32)
        is_start = jnp.any(at[:, None] == starts[None, :], axis=1) | (at == frames)
        return jnp.where(is_start, 0.0, 1.0).astype(F32)[:, None]

    prev_ok, next_ok = ok_at(0), ok_at(1)
    books_f = codebooks.astype(F32)
    norms = jnp.sum(books_f * books_f, axis=3) * (LOG2E / SOFTMAX_WARMTH)
    norms = norms[:, :, None, :]

    codes = num_codes // near
    first = near_at * codes

    def own_codes(array):
        start = (side, level_side, first) + (jnp.int32(0),) * (array.ndim - 3)
        return lax.dynamic_slice(array, start, (1, 1, codes) + array.shape[3:])[0, 0]

    index = own_codes(buffer_index)
    one_hot = index[:, None] == jnp.arange(code_buffer.shape[0], dtype=jnp.int32)[None, :]
    buffer_half = lax.dynamic_slice_in_dim(code_buffer, side * group_dim, group_dim, 1)
    chosen = dot_nn(one_hot.astype(BF16), buffer_half)
    books_own = own_codes(codebooks).astype(F32)
    if quad:
        chosen, books_own = chosen.T, books_own.T

    at = jnp.arange(cols, dtype=jnp.int32)
    turn = ((at[:, None] ^ (near_at * (cols // near))) == at[None, :]).astype(BF16)
    cot = list(frames_out(
        out_cotangent, [chosen, books_own, norms, prev_ok, next_ok, where_row]
    ))
    (dec_own,) = pack(dec_conv3, dec_conv1, [dec_bias3], 0, [cot[0], feat[1], enc_1])
    dec_1 = swap(dec_own, "mp", 1)
    dec_2 = swap(after(dec_own, feat[2], feat[3]), "mp", 2)

    taken = [((rows, depth), BF16), ((4 * depth + 32, depth), BF16)]
    taken += [((rows + 16, depth), F32), ((rows, 3 * depth), BF16)]
    slope_enc, act_mid, latent = call(
        encoder_kernel,
        where_row,
        [*feat, *enc, prev_ok, next_ok],
        [((rows, depth), BF16)] * 3,
        taken,
        [dec_own],
        cost(8 * rows * depth * depth, 12e6),
        PARAMS,
    )

    dec_3 = swap(after(dec_2, latent), "mp", 1)
    dec = (dec_own, dec_1, dec_2, dec_3)
    cot[2], cot[3], _ = lax.optimization_barrier((cot[2], cot[3], dec_2))
    cot = [cot[0]] + [swap(cot[k], "mp", k) for k in (1, 2, 3)]

    step = rows // 3
    quant, usage, prob, second = pl.pallas_call(
        functools.partial(quantize_kernel, own=own),
        grid=(3,),
        out_shape=(
            shaped((rows, depth), BF16),
            shaped((groups, levels, 1, num_codes), F32),
            shaped((groups, levels, rows, num_codes), BF16),
            shaped((levels - 1, rows, depth), BF16),
        ),
        in_specs=[
            pl.BlockSpec((step, depth), lambda i: (i, 0)),
            pl.BlockSpec(codebooks.shape, lambda i: (0, 0, 0, 0)),
            pl.BlockSpec(norms.shape, lambda i: (0, 0, 0, 0)),
        ],
        out_specs=(
            pl.BlockSpec((step, depth), lambda i: (i, 0)),
            pl.BlockSpec((groups, levels, 1, num_codes), lambda i: (0, 0, 0, 0)),
            pl.BlockSpec((groups, levels, step, num_codes), lambda i: (0, 0, i, 0)),
            pl.BlockSpec((levels - 1, step, depth), lambda i: (0, i, 0)),
        ),
        compiler_params=PARAMS,
        cost_estimate=cost(16 * rows * num_codes * group_dim, 30e6),
    )(latent, codebooks, norms)

    packed = 4 * depth + LANES
    grads_shape = (
        shaped((cols, packed), BF16),
        shaped((cols, packed), BF16),
        shaped((2, cols, packed), BF16),
    )
    grad_quant, *dec_grads = pl.pallas_call(
        functools.partial(decoder_kernel, near=near),
        out_shape=(shaped((rows, depth), BF16),) + grads_shape,
        in_specs=whole(12, True),
        out_specs=tuple(whole(4)),
        scratch_shapes=[
            pltpu.VMEM((rows, depth), BF16),
            pltpu.VMEM((4 * depth + 32, depth), BF16),
            pltpu.VMEM((rows + 16, depth), F32),
            pltpu.VMEM((rows, 3 * depth), BF16),
            pltpu.VMEM((rows, depth), BF16),
            pltpu.VMEM((rows, depth), BF16),
        ],
        compiler_params=PARAMS,
        cost_estimate=cost(24 * rows * depth * depth, 20e6),
    )(where_row, quant, *cot, *dec, prev_ok, next_ok)

    table_shape = (levels, near, group_dim + 16, num_codes // near)

    def quantize_back(flip, *ties):
        return pl.pallas_call(
            tied(functools.partial(quantize_back_kernel, own=own, levels=levels), 7, len(ties)),
            grid_spec=pltpu.PrefetchScalarGridSpec(
                num_scalar_prefetch=1,
                grid=(1,),
                in_specs=[
                    pl.BlockSpec((rows, group_dim), lambda i, g: (i, g[2] ^ flip)),
                    pl.BlockSpec((1, levels, rows, num_codes), lambda i, g: (g[2] ^ flip, 0, i, 0)),
                    pl.BlockSpec((rows, group_dim), lambda i, g: (i, g[2] ^ flip)),
                    pl.BlockSpec((levels - 1, rows, group_dim), lambda i, g: (0, i, g[2] ^ flip)),
                    pl.BlockSpec((1, levels, num_codes, group_dim), lambda i, g: (g[2] ^ flip, 0, 0, 0)),
                    pl.BlockSpec((1, levels, 1, num_codes), lambda i, g: (g[2] ^ flip, 0, 0, 0)),
                ]
                + [pl.BlockSpec(memory_space=pl.ANY)] * len(ties),
                out_specs=(
                    pl.BlockSpec((rows, group_dim), lambda i, g: (i, 0)),
                    pl.BlockSpec(table_shape, lambda i, g: (0, 0, 0, 0)),
                    pl.BlockSpec((8, LANES), lambda i, g: (0, 0)),
                ),
                scratch_shapes=[
                    pltpu.VMEM((levels, group_dim, num_codes), F32),
                    pltpu.VMEM((levels, 1, num_codes), F32),
                ],
            ),
            out_shape=(
                shaped((rows, group_dim), BF16),
                shaped(table_shape, BF16),
                shaped((8, LANES), F32),
            ),
            compiler_params=PARAMS,
            cost_estimate=cost(16 * rows * num_codes * group_dim, 15e6),
        )(
            where_row, grad_quant, prob, latent, second, codebooks, usage, *ties,
        )

    def encoder_weight_grads(*ties):
        return call(
            functools.partial(encoder_weight_grad_kernel, near=near),
            where_row,
            [grad_mine, grad_other, slope_enc, act_mid, *feat, *enc, prev_ok, next_ok],
            [(out.shape, out.dtype) for out in grads_shape]
            + [((rows, depth), BF16)] * 2 + [((8, LANES), F32)],
            taken,
            ties,
            cost(12 * rows * depth * depth, 20e6),
            PARAMS,
        )

    def encoder_input_grads(low, grad_latent, *ties):
        return call(
            encoder_input_grad_kernel,
            where_row,
            [low, grad_latent, *feat, *enc, prev_ok, next_ok],
            [((own, cols), BF16)] * 4 + [((8, LANES), F32)],
            taken,
            ties,
            cost(6 * rows * depth * depth, 10e6),
            PARAMS,
        )

    def put(mask, block, total, pieces, ties=(), params=None):
        return call(
            functools.partial(place_kernel, block=block),
            mask.reshape(1),
            pieces,
            [((total, pieces[0].shape[1]), F32)],
            ties=ties,
            price=cost(0, 8 * total * pieces[0].shape[1]),
            params=params,
        )[0]

    def gather_near(block):
        return jnp.concatenate([block] + [swap(block, "dp", k) for k in range(1, near)], 0)

    def stage(*groups):
        flat = lax.optimization_barrier(tuple(x for group in groups for x in group))
        out = []
        for group in groups:
            out.append(list(flat[: len(group)]))
            flat = flat[len(group) :]
        return out

    grad_other, table_other, mark = quantize_back(1)
    dec_0, dec_2, dec_send = dec_grads
    dec_core = swap(dec_send, "mp", 1)
    dec_send = low_sum(dec_2, dec_core[1]).astype(BF16)
    dec_x = swap(dec_send, "mp", 2)
    table_got = swap(table_other, "mp", 1)
    grad_mine, table_mine, mark = quantize_back(0, mark, dec_send)

    if quad:
        packed_half, table = (cols // 2, packed), table_shape[2:]
        mark_shape = ((8, LANES), F32)
        dec_mine, dec_send, book_send, mark = call(
            halve_kernel,
            where_row,
            [dec_0, dec_core, dec_x, table_mine, table_got],
            [(packed_half, F32), (packed_half, BF16), (table_shape[1:], BF16), mark_shape],
        )
        book_x, dec_got = swap(book_send, "mp", 2), swap(dec_send, "dp", 1)
        enc_0, enc_2, enc_send, low, grad_latent, mark = encoder_weight_grads(mark)
        book_mine, book_send, dec_mine, dec_send, enc_send = call(
            near_kernel,
            where_row,
            [table_mine, table_got, book_x, dec_mine, dec_got, enc_send],
            [(table, F32), (table, BF16), (packed_half, F32), (packed_half, BF16)]
            + [((2, cols, packed), BF16)],
            ties=[mark],
        )
        enc_core = swap(enc_send, "mp", 1)
        book_got, dec_got = swap(book_send, "dp", 1), swap(dec_send, "dp", 2)
        book_mine, book_send, enc_mine, enc_near, enc_x, enc_both, dec_mine, dec_send, mark = call(
            spread_kernel,
            where_row,
            [book_mine, book_got, enc_0, enc_2, enc_core, dec_mine, dec_got],
            [(table, F32), (table, BF16), (packed_half, F32)] + [(packed_half, BF16)] * 3
            + [(packed_half, F32), (packed_half, BF16), mark_shape],
        )
        enc_got = [swap(enc_near, "dp", 1), swap(enc_x, "mp", 2), swap_both(enc_both, 1, 2)]
        book_got, dec_got = swap(book_send, "dp", 2), swap(dec_send, "dp", 4)
        *outs, mark = encoder_input_grads(low, grad_latent, mark)
        book_mine, book_send, enc_mine, enc_send = call(
            sum_kernel,
            where_row,
            [book_mine, book_got, enc_mine, *enc_got],
            [(table, F32), (table, BF16), (packed_half, F32), (packed_half, BF16)],
            ties=[mark],
        )
        book_got, enc_got = swap(book_send, "dp", 4), swap(enc_send, "dp", 2)
        outs = [outs[0]] + [swap(outs[k], "mp", k) for k in (1, 2, 3)]
        fresh, enc_mine, enc_send, dec_send = call(
            functools.partial(refresh_kernel, share=num_codes / (frames * n_dp)),
            where_row,
            [book_mine, book_got, books_own, chosen, enc_mine, enc_got, dec_mine, dec_got],
            [((codes, group_dim), BF16), (packed_half, F32)] + [(packed_half, BF16)] * 2,
        )
        dec_got = swap(dec_send, "dp", 1)
        grad_features = put(me * own, own, frames, outs, [enc_send])
        fresh = [fresh, swap(fresh, "dp", 1), swap(fresh, "mp", 2), swap_both(fresh, 1, 2)]
        enc_got = swap(enc_send, "dp", 4)
        (enc_send,) = call(
            join_kernel,
            where_row,
            [enc_mine, enc_got],
            [(packed_half, BF16)],
            ties=[grad_features],
        )
        enc_got = swap(enc_send, "dp", 1)
        fresh = fresh + [swap(piece, "mp", 1) for piece in fresh]
        mask = (side * levels + level_side) * num_codes + first
        new_codebooks = put(mask, codes, groups * levels * num_codes, fresh, params=PARAMS)

        def unpack(mask, *parts):
            conv3, conv1, bias3, bias1 = call(
                functools.partial(unpack_kernel, block=cols // 2),
                mask.reshape(1),
                parts,
                [((3 * depth, cols), F32), ((depth, cols), F32)] + [((1, cols), F32)] * 2,
                [((cols, packed), F32)],
            )
            return (conv3.reshape(3, depth, cols), bias3[0], conv1, bias1[0])

        half = near_at * (cols // 2)
        return (
            grad_features,
            *unpack(half, enc_send, enc_got),
            *unpack(half, dec_send, dec_got),
            new_codebooks.reshape(codebooks.shape),
        )

    book_send = low_sum(table_mine[1], table_got[1]).astype(BF16)
    dec_mine, *dec_send = parts_of(low_sum(dec_0, dec_core[0], dec_x), near)
    dec_send = [piece.astype(BF16) for piece in dec_send]

    (mark,), (book_send,), dec_send = stage([mark], [book_send], dec_send)
    book_x = swap(book_send, "mp", 2)
    dec_got = [swap(piece, "dp", k + 1) for k, piece in enumerate(dec_send)]
    enc_0, enc_2, enc_send, low, grad_latent, mark = encoder_weight_grads(mark)

    def book_sum(k):
        return low_sum(table_mine[0, k], table_got[0, k], book_x[k])

    def pair_sum(held, sent, bit):
        return held + swap(sent, "dp", bit).astype(F32)

    dec_held = low_sum(dec_mine, *dec_got)
    enc_core = swap(enc_send, "mp", 1)
    book_send, (dec_send, _) = stage(
        [book_sum(k).astype(BF16) for k in range(1, near)], [dec_held.astype(BF16), mark]
    )
    book_got = [swap(piece, "dp", k + 1) for k, piece in enumerate(book_send)]
    dec_held = pair_sum(dec_held, dec_send, far_bits[0])
    enc_mine, *enc_near = parts_of(low_sum(enc_0, enc_core[0]), near)
    enc_near = [piece.astype(BF16) for piece in enc_near]
    enc_far = parts_of(low_sum(enc_2, enc_core[1]).astype(BF16), near)
    book_held = low_sum(book_sum(0), *book_got)

    (mark,), enc_near, enc_far, (book_send, dec_send) = stage(
        [mark], enc_near, enc_far, [book_held.astype(BF16), dec_held.astype(BF16)]
    )
    enc_got = [swap(piece, "dp", k + 1) for k, piece in enumerate(enc_near)] + [
        swap_both(piece, k, 2) for k, piece in enumerate(enc_far)
    ]
    book_held = pair_sum(book_held, book_send, far_bits[0])
    dec_held = pair_sum(dec_held, dec_send, far_bits[1])
    for bit in far_bits[2:]:
        dec_held = pair_sum(dec_held, dec_held.astype(BF16), bit)
    *outs, _ = encoder_input_grads(low, grad_latent, mark)

    enc_held = low_sum(enc_mine, *enc_got)
    (book_send, dec_send, enc_send), outs_send = stage(
        [book_held.astype(BF16), dec_held.astype(BF16), enc_held.astype(BF16)], outs[1:]
    )
    book_held = pair_sum(book_held, book_send, far_bits[1])
    enc_held = pair_sum(enc_held, enc_send, far_bits[0])
    outs = [outs[0]] + [swap(piece, "mp", k + 1) for k, piece in enumerate(outs_send)]
    dec_held = gather_near(dec_send)
    for bit in far_bits[2:]:
        book_held = pair_sum(book_held, book_held.astype(BF16), bit)

    share = num_codes / (frames * n_dp)
    book_held = book_held.T
    ratio = book_held[:, group_dim : group_dim + 1] * share
    refresh = jax.nn.sigmoid(SHARPNESS * (THRESHOLD - ratio))
    stepped = books_own - (STEP_SCALE * share) * book_held[:, :group_dim]
    fresh = ((1.0 - refresh) * stepped + refresh * chosen).astype(BF16)

    ((fresh, enc_send),) = stage([fresh, enc_held.astype(BF16)])
    enc_held = pair_sum(enc_held, enc_send, far_bits[1])
    for bit in far_bits[2:]:
        enc_held = pair_sum(enc_held, enc_held.astype(BF16), bit)
    fresh = [
        swap_both(fresh, k, bits) if k or bits else fresh for bits in (0, 2) for k in range(near)
    ]
    enc_held = gather_near(enc_held.astype(BF16))
    fresh = fresh + [swap(part, "mp", 1) for part in fresh]

    mask = (side * levels + level_side) * num_codes + first
    new_codebooks = put(mask, codes, groups * levels * num_codes, fresh)

    def unpack(held):
        biases = dot_tn(held[:, 4 * depth :], turn)
        return (
            dot_tn(held[:, : 3 * depth], turn).reshape(3, depth, cols),
            biases[0],
            dot_tn(held[:, 3 * depth : 4 * depth], turn),
            biases[1],
        )

    grad_features = put(me * own, own, frames, outs)

    return (
        grad_features,
        *unpack(enc_held),
        *unpack(dec_held),
        new_codebooks.reshape(codebooks.shape),
    )


def solution(mesh):
    return jax.shard_map(
        body,
        mesh=mesh,
        in_specs=(
            P("dp", "mp"),
            P("dp", None),
            P(None, None, "mp"),
            P("mp"),
            P(None, "mp"),
            P("mp"),
            P(),
            P(None, None, "mp"),
            P("mp"),
            P(None, "mp"),
            P(),
            P(),
            P("dp", "mp"),
        ),
        out_specs=(
            P("dp", "mp"),
            P(None, None, "mp"),
            P("mp"),
            P(None, "mp"),
            P("mp"),
            P(None, None, "mp"),
            P("mp"),
            P(None, "mp"),
            P("mp"),
            P(),
        ),
        check_vma=False,
    )
```
